32 devices in a mesh: seq: 2 (over y), ctx: 16 (over z, x, core).
Axes of the slice: x: 2, y: 2, z: 4, core: 2. Of those that a mesh axis runs over, the one named last changes fastest.
Arguments:
- hidden_in: bfloat16 [2, 2048, 768], P('seq', 'ctx'), may hold values from -6 to 6
- w_qkv: bfloat16 [768, 2304], P(('seq', 'ctx')), may hold values from -0.21875 to 0.21875
- q_bias: bfloat16 [768], P(('seq', 'ctx')), may hold values from -3 to 3
- v_bias: bfloat16 [768], P(('seq', 'ctx')), may hold values from -3 to 3
- w_out: bfloat16 [768, 768], P(('seq', 'ctx')), may hold values from -0.875 to 0.875
- out_bias: bfloat16 [768], P(('seq', 'ctx')), may hold values from -2 to 2
- w_up: bfloat16 [768, 3072], P(('seq', 'ctx')), may hold values from -0.21875 to 0.21875
- up_bias: bfloat16 [3072], P(('seq', 'ctx')), may hold values from -2 to 2
- w_down: bfloat16 [3072, 768], P(('seq', 'ctx')), may hold values from -0.15625 to 0.15625
- down_bias: bfloat16 [768], P(('seq', 'ctx')), may hold values from -2 to 2
- ln1_gain: bfloat16 [768], P(('seq', 'ctx')), may hold values from 0.5 to 1.5
- ln1_bias: bfloat16 [768], P(('seq', 'ctx')), may hold values from -2 to 2
- ln2_gain: bfloat16 [768], P(('seq', 'ctx')), may hold values from 0.5 to 1.5
- ln2_bias: bfloat16 [768], P(('seq', 'ctx')), may hold values from -2 to 2
- segment_ids: int32 [2, 2048], P('seq', 'ctx'), may hold values from 0 to 4, as said below
- padding_mask: int32 [2, 2048], P('seq', 'ctx'), may hold values from 0 to 1, as said below
- teacher: bfloat16 [2, 2048, 768], P('seq', 'ctx'), may hold values from -6 to 6
- cotangent: bfloat16 [2, 2048, 768], P('seq', 'ctx'), may hold values from -6 to 6
Outputs:
- layer_out: bfloat16 [2, 2048, 768], P('seq', 'ctx')
- loss: float32 [], replicated
- input_grad: float32 [2, 2048, 768], P('seq', 'ctx')
- grad_w_qkv: float32 [768, 2304], P(('seq', 'ctx'))
- grad_q_bias: float32 [768], P(('seq', 'ctx'))
- grad_v_bias: float32 [768], P(('seq', 'ctx'))
- grad_w_out: float32 [768, 768], P(('seq', 'ctx'))
- grad_out_bias: float32 [768], P(('seq', 'ctx'))
- grad_w_up: float32 [768, 3072], P(('seq', 'ctx'))
- grad_up_bias: float32 [3072], P(('seq', 'ctx'))
- grad_w_down: float32 [3072, 768], P(('seq', 'ctx'))
- grad_down_bias: float32 [768], P(('seq', 'ctx'))
- grad_ln1_gain: float32 [768], P(('seq', 'ctx'))
- grad_ln1_bias: float32 [768], P(('seq', 'ctx'))
- grad_ln2_gain: float32 [768], P(('seq', 'ctx'))
- grad_ln2_bias: float32 [768], P(('seq', 'ctx'))
The draws below stay inside these ranges and needn't reach their ends.
Inputs may be any that keep to these rules, and one draw needn't show every extreme that they name: `segment_ids`: in each sequence the ids never fall and each of the 5 documents holds one token or more; document 2 begins within the first 128 tokens and ends within the last 128 tokens. `padding_mask`: in each sequence the tokens with 1 come first, the padding after them.
All inputs are finite; a program needn't handle non-finite values.
Results may differ from the reference program's by a relative error of at most 0.014.
Values may be sent and summed in bfloat16 or wider, within the bound.
No kernel may reach another device: no remote copies, remote signals or barrier semaphores. Data moves between devices by JAX's collectives and lax.ppermute only.
A program may use at most 192 MiB of HBM per device.

```python
import math
import jax
import jax.numpy as jnp
from jax import lax

D = 768
HEADS = 12
HEAD_DIM = 64
FF = 3072
TOK_DEV = 128
SEQ_LEN = 2048
SEQS = 2
TOKENS = 4096


def draw_padding_mask(key, part):
    padded = jax.random.randint(key, (SEQS, 1), 0, SEQ_LEN // 2 + 1)
    places = jnp.arange(SEQ_LEN, dtype=jnp.int32)[None, :]
    return (places < SEQ_LEN - padded).astype(jnp.int32)


def draw_segment_ids(key, part):
    key_head, key_first, key_tail, key_last = jax.random.split(jax.random.fold_in(key, 7), 4)
    head_len = jax.random.randint(key_head, (SEQS, 1), 2, TOK_DEV)
    first_cut = 1 + jax.random.randint(key_first, (SEQS, 1), 0, 1 << 20) % (head_len - 1)
    tail_len = jax.random.randint(key_tail, (SEQS, 1), 2, TOK_DEV)
    long_end = SEQ_LEN - tail_len
    last_cut = long_end + 1 + jax.random.randint(key_last, (SEQS, 1), 0, 1 << 20) % (tail_len - 1)
    places = jnp.arange(SEQ_LEN, dtype=jnp.int32)[None, :]
    ids = (places >= first_cut).astype(jnp.int32) + (places >= head_len).astype(jnp.int32)
    ids = ids + (places >= long_end).astype(jnp.int32) + (places >= last_cut).astype(jnp.int32)
    return ids.astype(jnp.int32)


def strengthened(array, stream_key, source, target, blocks, factor):
    def block_of(axis_at):
        return (jnp.arange(array.shape[axis_at]) // (array.shape[axis_at] // blocks)).reshape((-1,) + (1,) * (array.ndim - 1 - axis_at))

    one_side = jax.random.permutation(stream_key, blocks)[block_of(target)]
    other_side = (block_of(target) + blocks // 2) % blocks
    return jnp.where((block_of(source) == one_side) | (block_of(source) == other_side), factor * array, array)


def shard_levels(rng, dims, cuts, smallest, top_value):
    gain, own = 1.0, jax.random.fold_in(rng, 6)
    for dim, blocks in cuts:
        heights = jnp.exp(jax.random.uniform(jax.random.fold_in(own, dim), (blocks,), jnp.float32, smallest / len(cuts), top_value / len(cuts)))
        gain = gain * jnp.repeat(heights, dims[dim] // blocks).reshape([-1 if axis == dim else 1 for axis in range(len(dims))])
    return gain


def scatter_about(rng, extent, scale, reach, cuts=(), held_as=jnp.bfloat16):
    level = shard_levels(rng, extent, cuts, -0.22, 0.18) if cuts else 1.0
    array = jax.random.normal(rng, extent, jnp.float32) * scale * level
    return jnp.minimum(jnp.maximum(array, -reach), reach).astype(held_as)


def gaussian_with(stream_key, shape, spread, reach, pieces, heavy, kind=jnp.bfloat16):
    drawn = spread * jax.random.normal(stream_key, shape, jnp.float32)
    if pieces:
        drawn = drawn * shard_levels(stream_key, shape, pieces, -0.22, 0.18)
    return jnp.clip(strengthened(drawn, jax.random.fold_in(stream_key, 3), *heavy), -reach, reach).astype(kind)


def setup_inputs(seed: int = 0) -> dict:
    splits = jax.random.split(jax.random.key(seed), 19)
    return {
        "hidden_in": scatter_about(splits[0], (SEQS, SEQ_LEN, D), 1.0, 6.0, ((0, 2), (1, 16))),
        "w_qkv": scatter_about(splits[1], (D, 3 * D), D ** -0.5, 0.21875, ((0, 32),)),
        "q_bias": scatter_about(splits[2], (D,), 0.5, 3.0, ((0, 32),)),
        "v_bias": scatter_about(splits[3], (D,), 0.5, 3.0, ((0, 32),)),
        "w_out": scatter_about(splits[4], (D, D), (D // 16) ** -0.5, 0.875, ((0, 32),)),
        "out_bias": scatter_about(splits[5], (D,), 0.3, 2.0, ((0, 32),)),
        "w_up": scatter_about(splits[6], (D, FF), D ** -0.5, 0.21875, ((0, 32),)),
        "up_bias": scatter_about(splits[7], (FF,), 0.3, 2.0, ((0, 32),)),
        "w_down": scatter_about(splits[8], (FF, D), (FF // 2) ** -0.5, 0.15625, ((0, 32),)),
        "down_bias": scatter_about(splits[9], (D,), 0.3, 2.0, ((0, 32),)),
        "ln1_gain": jnp.clip(1.0 + 0.1 * jax.random.normal(splits[10], (D,), jnp.float32), 0.5, 1.5).astype(jnp.bfloat16),
        "ln1_bias": scatter_about(splits[11], (D,), 0.3, 2.0, ((0, 32),)),
        "ln2_gain": jnp.clip(1.0 + 0.1 * jax.random.normal(splits[12], (D,), jnp.float32), 0.5, 1.5).astype(jnp.bfloat16),
        "ln2_bias": scatter_about(splits[13], (D,), 0.3, 2.0, ((0, 32),)),
        "segment_ids": draw_segment_ids(jax.random.fold_in(splits[18], 71), 0),
        "padding_mask": draw_padding_mask(jax.random.fold_in(splits[18], 71), 0),
        "teacher": scatter_about(splits[16], (SEQS, SEQ_LEN, D), 1.0, 6.0, ((0, 2), (1, 16))),
        "cotangent": gaussian_with(splits[17], (SEQS, SEQ_LEN, D), 1.0, 6.0, ((0, 2), (1, 16)), (1, 2, 16, 2.0)),
    }


@jax.custom_vjp
def low(v):
    return lax.optimization_barrier(v.astype(jnp.bfloat16)).astype(jnp.float32)

@jax.custom_vjp
def low_back(v):
    return v

def low_keep(v):
    return (low(v), None)

def low_pass(kept, grad):
    return (grad,)

def back_keep(v):
    return (v, None)

def back_low(kept, grad):
    return (low(grad),)
low.defvjp(low_keep, low_pass)
low_back.defvjp(back_keep, back_low)

def layer_norm(values, gain_vec, shift_vec):
    mean_value = lax.optimization_barrier(jnp.mean(values, -1, keepdims=True))
    centered = values - mean_value
    variance = lax.optimization_barrier(jnp.mean(centered * centered, -1, keepdims=True))
    return centered * lax.rsqrt(variance + 1e-05) * gain_vec + shift_vec

def matmul(left, right):
    return jnp.dot(left, right, precision=lax.Precision.HIGHEST, preferred_element_type=jnp.float32)

def attend_sequence(queries, keys_seq, values_seq, seg_row):
    block_rows = math.gcd(SEQ_LEN, 512)
    key_heads = keys_seq.reshape(SEQ_LEN, HEADS, HEAD_DIM)
    value_heads = values_seq.reshape(SEQ_LEN, HEADS, HEAD_DIM)
    key_pos = jnp.arange(SEQ_LEN, dtype=jnp.int32)

    def one_block(inputs):
        query_block, first_row = inputs
        query_pos = first_row + jnp.arange(block_rows, dtype=jnp.int32)
        query_seg = lax.dynamic_slice_in_dim(seg_row, first_row, block_rows, 0)
        scores = jnp.einsum('qhd,khd->hqk', query_block.reshape(block_rows, HEADS, HEAD_DIM), key_heads, precision=lax.Precision.HIGHEST) * 0.125
        scores = low_back(scores)
        allowed = (query_pos[:, None] >= key_pos[None, :]) & (query_seg[:, None] == seg_row[None, :])
        exp_scores = jnp.where(allowed[None], jnp.exp(scores), 0.0)
        totals = lax.optimization_barrier(jnp.sum(exp_scores, -1))
        unnormed = low_back(jnp.einsum('hqk,khd->qhd', low(exp_scores), value_heads, precision=lax.Precision.HIGHEST))
        return (unnormed / totals.T[:, :, None]).reshape(block_rows, D)
    starts = jnp.arange(SEQ_LEN // block_rows, dtype=jnp.int32) * block_rows
    blocks = lax.map(jax.checkpoint(one_block), (queries.reshape(SEQ_LEN // block_rows, block_rows, D), starts))
    return blocks.reshape(SEQ_LEN, D)

def one_sequence(members):
    return attend_sequence(members[0], members[1], members[2], members[3])

def forward(rows_in, params, segment_ids, valid_rows, teacher_rows, cot_rows, valid_count):
    w_qkv, q_bias, v_bias, w_out, out_bias, w_up, up_bias, w_down, down_bias, ln1_gain, ln1_bias, ln2_gain, ln2_bias = params
    normed_one = low(layer_norm(rows_in, ln1_gain, ln1_bias))
    joined_rows = matmul(normed_one, w_qkv)
    queries = low(low_back(joined_rows[:, :D] + q_bias))
    keys_low = low(low_back(joined_rows[:, D:2 * D]))
    values_low = low(low_back(joined_rows[:, 2 * D:] + v_bias))
    attended = lax.map(one_sequence, (queries.reshape(SEQS, SEQ_LEN, D), keys_low.reshape(SEQS, SEQ_LEN, D), values_low.reshape(SEQS, SEQ_LEN, D), segment_ids))
    context = low(low_back(attended.reshape(TOKENS, D)))
    branch = low_back(matmul(context, w_out) + out_bias)
    residual = rows_in + branch
    normed_two = low(layer_norm(residual, ln2_gain, ln2_bias))
    hidden_pre = low_back(matmul(normed_two, w_up) + up_bias)
    activated = low(jax.nn.gelu(hidden_pre, approximate=True))
    mlp_out = low_back(matmul(activated, w_down) + down_bias)
    final_rows = residual + mlp_out
    deviation = final_rows - teacher_rows
    loss_value = jnp.sum(valid_rows * deviation * deviation) / (valid_count * D)
    objective_value = jnp.sum(valid_rows * cot_rows * final_rows) + loss_value
    return (objective_value, (final_rows, loss_value))

def reference(hidden_in, w_qkv, q_bias, v_bias, w_out, out_bias, w_up, up_bias, w_down, down_bias, ln1_gain, ln1_bias, ln2_gain, ln2_bias, segment_ids, padding_mask, teacher, cotangent):
    valid_rows = padding_mask.reshape(TOKENS, 1).astype(jnp.float32)
    valid_count = jnp.sum(valid_rows)
    params = tuple((member.astype(jnp.float32) for member in (w_qkv, q_bias, v_bias, w_out, out_bias, w_up, up_bias, w_down, down_bias, ln1_gain, ln1_bias, ln2_gain, ln2_bias)))
    teacher_rows = teacher.reshape(TOKENS, D).astype(jnp.float32)
    cot_rows = cotangent.reshape(TOKENS, D).astype(jnp.float32)

    def objective(rows_in, *weights):
        return forward(rows_in, weights, segment_ids, valid_rows, teacher_rows, cot_rows, valid_count)
    objective_value, pullback, extras = jax.vjp(objective, hidden_in.reshape(TOKENS, D).astype(jnp.float32), *params, has_aux=True)
    gradients = pullback(jnp.ones_like(objective_value))
    final_rows, loss_value = extras
    return (final_rows.astype(jnp.bfloat16).reshape(SEQS, SEQ_LEN, D), loss_value, gradients[0].reshape(SEQS, SEQ_LEN, D), gradients[1], gradients[2], gradients[3], gradients[4], gradients[5], gradients[6], gradients[7], gradients[8], gradients[9], gradients[10], gradients[11], gradients[12], gradients[13])
```

```python
import functools

import jax
import jax.numpy as jnp
from jax import lax
from jax.experimental import pallas as pl
from jax.experimental.pallas import tpu as pltpu
from jax.sharding import Mesh
from jax.sharding import PartitionSpec as P

HEADS = 12
HEAD_DIM = 64
ZS = 4
BF = jnp.bfloat16
F32 = jnp.float32
NEG = -1e30
LANES = 128


def shift(value, axis, step):
    size = lax.axis_size(axis)
    return lax.ppermute(value, axis, [(a, (a + step) % size) for a in range(size)])


def pair(mine, theirs, core, dim):
    low = jnp.where(core == 0, mine, theirs)
    high = jnp.where(core == 0, theirs, mine)
    return jnp.concatenate([low, high], dim)


def gather(value, axis, dim):
    size = lax.axis_size(axis)
    place = lax.axis_index(axis)
    pieces = [value] + [shift(value, axis, d) for d in range(1, size)]
    if size == 2:
        return pair(pieces[0], pieces[1], place, dim)
    shape = list(value.shape)
    shape[dim] *= size
    out = jnp.zeros(shape, value.dtype)
    for d in range(size):
        spot = lax.rem(place + size - d, size) * value.shape[dim]
        out = lax.dynamic_update_slice_in_dim(out, pieces[d], spot, dim)
    return out


def scatter_sum(value, axis, dim, last=BF):
    size = lax.axis_size(axis)
    place = lax.axis_index(axis)
    part = value.shape[dim] // size

    def cut(d):
        spot = lax.rem(place + d, size) * part
        return lax.dynamic_slice_in_dim(value, spot, part, dim)

    total = cut(0).astype(F32)
    for d in range(1, size):
        total = total + shift(cut(d), axis, d).astype(F32)
    return total.astype(last)


def dot(a, b):
    return jnp.dot(a, b, preferred_element_type=F32)


def dot_nt(a, b):
    return lax.dot_general(a, b, (((1,), (1,)), ((), ())), preferred_element_type=F32)


def dot_tn(a, b):
    return lax.dot_general(a, b, (((0,), (0,)), ((), ())), preferred_element_type=F32)


def lane_half(rows):
    return lax.broadcasted_iota(jnp.int32, (rows, LANES), 1) >= HEAD_DIM


def attend_kernel(pos, q_ref, k_ref, v_ref, segq_ref, segk_ref, ctx_ref, tot_ref, acc):
    block = pl.program_id(0)
    own = pos[0]
    rows = q_ref.shape[0]
    pairs = q_ref.shape[1] // LANES

    @pl.when(block == 0)
    def _():
        acc[...] = jnp.zeros_like(acc)

    @pl.when(block <= own)
    def _():
        row = own * rows + lax.broadcasted_iota(jnp.int32, (rows, rows), 0)
        col = block * rows + lax.broadcasted_iota(jnp.int32, (rows, rows), 1)
        ok = (col <= row) & (segq_ref[...] == segk_ref[0])
        bias = jnp.where(ok, 0.0, NEG)
        upper = lane_half(rows)
        for p in range(pairs):
            cols = slice(p * LANES, (p + 1) * LANES)
            q2, k2, v2 = q_ref[:, cols], k_ref[:, cols], v_ref[:, cols]
            for a in range(2):
                mine = upper if a else jnp.logical_not(upper)
                qa = jnp.where(mine, q2, jnp.zeros_like(q2))
                va = jnp.where(mine, v2, jnp.ones_like(v2))
                expo = jnp.exp(dot_nt(qa, k2) + bias)
                acc[2 * p + a] += dot(expo.astype(BF), va)

    @pl.when(block == pl.num_programs(0) - 1)
    def _():
        upper = lane_half(rows)
        for p in range(pairs):
            cols = slice(p * LANES, (p + 1) * LANES)
            u0, u1 = acc[2 * p], acc[2 * p + 1]
            unnormed = jnp.where(upper, u1, u0)
            totals = jnp.where(upper, pltpu.roll(u1, HEAD_DIM, 1), pltpu.roll(u0, HEAD_DIM, 1))
            tot_ref[:, cols] = totals
            ctx_ref[:, cols] = unnormed / totals


def attend(pos, q, k, v, segq, segk):
    rows, width = q.shape
    blocks = k.shape[0] // rows
    whole = lambda b, pos: (0, 0)
    seen = lambda b, pos: (jnp.minimum(b, pos[0]), 0)
    return pl.pallas_call(
        attend_kernel,
        grid_spec=pltpu.PrefetchScalarGridSpec(
            num_scalar_prefetch=1,
            grid=(blocks,),
            in_specs=[
                pl.BlockSpec((rows, width), whole),
                pl.BlockSpec((rows, width), seen),
                pl.BlockSpec((rows, width), seen),
                pl.BlockSpec((rows, 1), whole),
                pl.BlockSpec((1, 1, rows), lambda b, pos: (jnp.minimum(b, pos[0]), 0, 0)),
            ],
            out_specs=[pl.BlockSpec((rows, width), whole), pl.BlockSpec((rows, width), whole)],
            scratch_shapes=[pltpu.VMEM((width // HEAD_DIM, rows, LANES), F32)],
        ),
        out_shape=[jax.ShapeDtypeStruct((rows, width), F32)] * 2,
        compiler_params=pltpu.CompilerParams(vmem_limit_bytes=40 * 1024 * 1024),
        cost_estimate=pl.CostEstimate(flops=4 * rows * rows * blocks * width, bytes_accessed=8 << 20, transcendentals=rows * rows * blocks * width // HEAD_DIM),
        name="attend",
    )(pos, q, k, v, segq, segk.reshape(blocks, 1, rows))


def attend_back_kernel(pos, q_ref, gctx_ref, ctx_ref, tot_ref, k_ref, v_ref, segq_ref, segk_ref, dq_ref, dk_ref, dv_ref, gu_ref, ge_ref, acc):
    block = pl.program_id(0)
    own = pos[0]
    rows = q_ref.shape[0]
    pairs = q_ref.shape[1] // LANES
    upper = lane_half(rows)

    @pl.when(block == 0)
    def _():
        acc[...] = jnp.zeros_like(acc)
        lane = lax.broadcasted_iota(jnp.int32, (rows, LANES), 1)
        for p in range(pairs):
            cols = slice(p * LANES, (p + 1) * LANES)
            grad = gctx_ref[:, cols].astype(F32)
            tot = tot_ref[:, cols]
            gu = (grad / tot).astype(BF)
            gu_ref[:, cols] = gu
            weighed = grad * ctx_ref[:, cols] / tot
            for a in range(2):
                mine = upper if a else jnp.logical_not(upper)
                gtot = -jnp.sum(jnp.where(mine, weighed, 0.0), -1, keepdims=True)
                high = gtot.astype(BF)
                low = (gtot - high.astype(F32)).astype(BF)
                first = 0 if a else HEAD_DIM
                zero = jnp.zeros_like(gu)
                extra = jnp.where(lane == first, high, jnp.where(lane == first + 1, low, zero))
                ge_ref[2 * p + a] = jnp.where(mine, gu, extra)

    @pl.when(block <= own)
    def _():
        row = own * rows + lax.broadcasted_iota(jnp.int32, (rows, rows), 1)
        col = block * rows + lax.broadcasted_iota(jnp.int32, (rows, rows), 0)
        ok = (col <= row) & (segq_ref[0] == segk_ref[...])
        bias = jnp.where(ok, 0.0, NEG)
        for p in range(pairs):
            cols = slice(p * LANES, (p + 1) * LANES)
            q2, k2, v2, g2 = q_ref[:, cols], k_ref[:, cols], v_ref[:, cols], gu_ref[:, cols]
            dks, dvs, dqs = [], [], []
            for a in range(2):
                mine = upper if a else jnp.logical_not(upper)
                ka = jnp.where(mine, k2, jnp.zeros_like(k2))
                va = jnp.where(mine, v2, jnp.ones_like(v2))
                expo = jnp.exp(dot_nt(ka, q2) + bias)
                gprob = dot_nt(va, ge_ref[2 * p + a])
                gscore = (expo * gprob).astype(BF)
                dvs.append(dot(expo.astype(BF), g2))
                dks.append(dot(gscore, q2))
                dqs.append(dot_tn(gscore, k2))
            dk_ref[:, cols] = jnp.where(upper, dks[1], dks[0]).astype(BF)
            dv_ref[:, cols] = jnp.where(upper, dvs[1], dvs[0]).astype(BF)
            acc[:, cols] += jnp.where(upper, dqs[1], dqs[0])

    @pl.when(block > own)
    def _():
        dk_ref[...] = jnp.zeros_like(dk_ref)
        dv_ref[...] = jnp.zeros_like(dv_ref)

    @pl.when(block == pl.num_programs(0) - 1)
    def _():
        dq_ref[...] = (0.125 * acc[...]).astype(BF)


def attend_back(pos, q, gctx, ctx, tot, k, v, segq, segk):
    rows, width = q.shape
    blocks = k.shape[0] // rows
    whole = lambda b, pos: (0, 0)
    seen = lambda b, pos: (jnp.minimum(b, pos[0]), 0)
    each = lambda b, pos: (b, 0)
    heads = width // HEAD_DIM
    return pl.pallas_call(
        attend_back_kernel,
        grid_spec=pltpu.PrefetchScalarGridSpec(
            num_scalar_prefetch=1,
            grid=(blocks,),
            in_specs=[
                pl.BlockSpec((rows, width), whole),
                pl.BlockSpec((rows, width), whole),
                pl.BlockSpec((rows, width), whole),
                pl.BlockSpec((rows, width), whole),
                pl.BlockSpec((rows, width), seen),
                pl.BlockSpec((rows, width), seen),
                pl.BlockSpec((1, 1, rows), lambda b, pos: (0, 0, 0)),
                pl.BlockSpec((rows, 1), seen),
            ],
            out_specs=[
                pl.BlockSpec((rows, width), whole),
                pl.BlockSpec((rows, width), each),
                pl.BlockSpec((rows, width), each),
            ],
            scratch_shapes=[
                pltpu.VMEM((rows, width), BF),
                pltpu.VMEM((heads, rows, LANES), BF),
                pltpu.VMEM((rows, width), F32),
            ],
        ),
        out_shape=[
            jax.ShapeDtypeStruct((rows, width), BF),
            jax.ShapeDtypeStruct(k.shape, BF),
            jax.ShapeDtypeStruct(v.shape, BF),
        ],
        compiler_params=pltpu.CompilerParams(vmem_limit_bytes=40 * 1024 * 1024),
        cost_estimate=pl.CostEstimate(flops=10 * rows * rows * blocks * width, bytes_accessed=12 << 20, transcendentals=rows * rows * blocks * heads),
        name="attend_back",
    )(pos, q, gctx, ctx, tot, k, v, segq.reshape(1, 1, rows), segk.reshape(-1, 1))


def norm_parts(values):
    mean = jnp.mean(values, -1, keepdims=True)
    centered = values - mean
    rstd = lax.rsqrt(jnp.mean(centered * centered, -1, keepdims=True) + 1e-05)
    return centered * rstd, rstd


def norm_back(normed, rstd, grad, gain):
    q = grad * gain
    return rstd * (q - jnp.mean(q, -1, keepdims=True) - normed * jnp.mean(q * normed, -1, keepdims=True))


GC = 0.7978845608028654


def per_device(hidden_in, w_qkv, q_bias, v_bias, w_out, out_bias, w_up, up_bias, w_down, down_bias, ln1_gain, ln1_bias, ln2_gain, ln2_bias, segment_ids, padding_mask, teacher, cotangent):
    sy, sz, sx = (lax.axis_size(a) for a in ("y", "z", "x"))
    iy, iz, ix, core = (lax.axis_index(a) for a in ("y", "z", "x", "core"))
    chips = sy * sz * sx
    chip = (iy * sz + iz) * sx + ix
    own = iz * sx + ix
    rows, width = hidden_in.shape[1:]
    wr = w_qkv.shape[0]
    half = width // 2
    ffd = w_down.shape[0]
    fh = ffd * chips
    upc = ffd // wr
    segc = LANES - 16

    def of_core(value, which, dim):
        return lax.dynamic_index_in_dim(value, which, dim, keepdims=False)

    valid_own = padding_mask[0].astype(F32)
    count_own = jnp.sum(valid_own).astype(BF)
    seg_cols = jnp.zeros((wr * segc,), BF).at[:rows].set(segment_ids[0].astype(BF)).reshape(wr, segc)
    vec_block = jnp.concatenate(
        [jnp.stack([q_bias, v_bias, out_bias, down_bias, ln1_gain, ln1_bias, ln2_gain, ln2_bias], 1),
         up_bias.reshape(wr, upc), jnp.full((wr, 1), count_own), jnp.zeros((wr, 7 - upc), BF), seg_cols], 1)
    qkv_halves = w_qkv.reshape(wr, 3, 2, half)
    up_halves = w_up.reshape(wr, chips, 2, ffd)
    out_halves = w_out.reshape(wr, 2, half)

    def first_chunk(which):
        return jnp.concatenate([of_core(qkv_halves, which, 2).reshape(wr, 3 * half), vec_block], 1)

    def second_chunk(which):
        return jnp.concatenate([of_core(out_halves, which, 1), of_core(up_halves, which, 2).reshape(wr, fh)], 1)

    def spread(value, order):
        value = value[None, None, None]
        for axis in order:
            value = gather(value, axis, "yzx".index(axis))
        return value

    one = pair(first_chunk(core), shift(first_chunk(1 - core), "core", 1), core, 0)
    one = spread(one, "zxy").reshape(width, -1)
    hidden = hidden_in[None, None]
    for axis, dim in (("z", 0), ("x", 1), ("core", 2)):
        hidden = gather(hidden, axis, dim)
    hidden = hidden.reshape(-1, width)
    two = pair(second_chunk(core), shift(second_chunk(1 - core), "core", 1), core, 0)
    two = spread(two, "zxy").reshape(width, -1)
    w_down_h = spread(w_down, "zyx").reshape(fh, width)
    side = jnp.concatenate([teacher[0], cotangent[0]], 1)
    side = pair(side, shift(side, "core", 1), core, 0)
    valid = pair(valid_own, shift(valid_own, "core", 1), core, 0)[:, None]

    vec = one[:, 3 * half:]
    vec_rows = vec[:, :8].T.astype(F32)
    qb, vb, ob, db, g1, b1, g2, b2 = (vec_rows[i][None] for i in range(8))
    ub = of_core(vec[:, 8:8 + upc].reshape(chips, 2, ffd), core, 1).reshape(1, fh).astype(F32)
    count = jnp.sum(vec[:, 12].reshape(-1, wr)[:, 0].astype(F32))
    seg_all = of_core(vec[:, 16:].reshape(sy, sz * sx * 2, wr * segc), iy, 0)[:, :rows].reshape(-1).astype(jnp.int32)
    two_rows = 2 * rows
    seg_own = lax.dynamic_slice_in_dim(seg_all, own * two_rows, two_rows, 0)

    def half_of(row):
        return lax.dynamic_slice_in_dim(row, core * half, half, 1)

    hidden_f = hidden.astype(F32)
    n1, r1 = norm_parts(hidden_f)
    n1_low = (n1 * g1 + b1).astype(BF)
    n1_own = lax.dynamic_slice_in_dim(n1_low, own * two_rows, two_rows, 0)
    wq, wk, wv = (one[:, i * half:(i + 1) * half] for i in range(3))
    q = (0.125 * (dot(n1_own, wq) + half_of(qb)).astype(BF).astype(F32)).astype(BF)
    k = dot(n1_low, wk).astype(BF)
    v = (dot(n1_low, wv) + half_of(vb)).astype(BF)
    pos = own.astype(jnp.int32).reshape(1)
    ctx, tot = attend(pos, q, k, v, seg_own[:, None], seg_all)
    ctx_low = ctx.astype(BF)
    ctx_all = pair(ctx_low, shift(ctx_low, "core", 1), core, 1)
    wo_h = two[:, :half]
    wo = pair(wo_h, shift(wo_h, "core", 1), core, 1)
    w_up_h = two[:, half:]
    hidden_own = lax.dynamic_slice_in_dim(hidden, own * two_rows, two_rows, 0).astype(F32)
    residual = hidden_own + dot(ctx_all, wo) + ob
    n2, r2 = norm_parts(residual)
    n2_low = (n2 * g2 + b2).astype(BF)
    pre = dot(n2_low, w_up_h) + ub
    tanh = jnp.tanh(GC * (pre + 0.044715 * pre * pre * pre))
    act = (0.5 * pre * (1.0 + tanh)).astype(BF)
    slope = 0.5 * (1.0 + tanh) + 0.5 * pre * (1.0 - tanh * tanh) * GC * (1.0 + 0.134145 * pre * pre)
    mlp = dot(act, w_down_h)
    final = residual + mlp + shift(mlp, "core", 1) + db
    deviation = final - side[:, :width].astype(F32)
    error = jnp.sum(valid * deviation * deviation)
    layer_out = lax.dynamic_slice_in_dim(final, core * rows, rows, 0).astype(BF)

    grad_final = valid * (side[:, width:].astype(F32) + deviation * (2.0 / (count * width)))
    grad_mlp = grad_final.astype(BF)
    grad_pre = (dot_nt(grad_mlp, w_down_h) * slope).astype(BF)
    gn2 = dot_nt(grad_pre, w_up_h)
    gn2 = gn2 + shift(gn2, "core", 1)
    gw_down = dot_tn(act, grad_mlp).astype(BF)
    gw_down = gw_down.reshape(sy, sz, sx, ffd, width)
    for axis in ("x", "y"):
        gw_down = scatter_sum(gw_down, axis, "yzx".index(axis))
    gw_down = scatter_sum(gw_down, "z", 1, F32).reshape(ffd, width)
    grad_res = grad_final + norm_back(n2, r2, gn2, g2)
    grad_branch = grad_res.astype(BF)
    gw_up = dot_tn(n2_low, grad_pre).astype(BF)
    gw_out = dot_tn(ctx_all, lax.dynamic_slice_in_dim(grad_branch, core * half, half, 1)).astype(BF)
    second = jnp.concatenate([gw_out, gw_up], 1).reshape(sy, sz, sx, 2 * wr, half + fh)
    second = scatter_sum(scatter_sum(second, "y", 0), "x", 2)
    second = scatter_sum(second, "z", 1, F32).reshape(2, wr, half + fh)
    gctx = dot_nt(grad_branch, lax.dynamic_slice_in_dim(wo, core * half, half, 0)).astype(BF)
    dq, dk, dv = attend_back(pos, q, gctx, ctx, tot, k, v, seg_own, seg_all)
    gn1 = dot_nt(dk, wk) + dot_nt(dv, wv)
    gn1_own = lax.dynamic_slice_in_dim(gn1, own * two_rows, two_rows, 0) + dot_nt(dq, wq)
    gn1 = lax.dynamic_update_slice_in_dim(gn1, gn1_own, own * two_rows, 0)
    g_ln1 = jnp.sum(gn1 * n1, 0)
    b_ln1 = jnp.sum(gn1, 0)
    back = gn1.astype(BF).reshape(sz, sx, 2, rows, width)
    back = scatter_sum(scatter_sum(back, "core", 2), "x", 1)
    back = scatter_sum(back, "z", 0, F32).reshape(rows, width)
    gw_qkv = jnp.concatenate([dot_tn(n1_own, dq), dot_tn(n1_low, dk), dot_tn(n1_low, dv)], 1).astype(BF)

    once = jnp.where(core == 0, 1.0, 0.0)
    zeros = jnp.zeros((width,), F32)

    def own_heads(sums):
        return lax.dynamic_update_slice_in_dim(zeros, sums, core * half, 0)

    columns = jnp.stack([
        own_heads(jnp.sum(dq.astype(F32), 0)), own_heads(jnp.sum(dv.astype(F32), 0)),
        once * jnp.sum(grad_branch.astype(F32), 0), once * jnp.sum(grad_mlp.astype(F32), 0),
        g_ln1, b_ln1, once * jnp.sum(gn2 * n2, 0), once * jnp.sum(gn2, 0)], 1)
    up_sums = jnp.sum(grad_pre.astype(F32), 0).reshape(chips, 1, ffd)
    up_sums = lax.dynamic_update_slice_in_dim(jnp.zeros((chips, 2, ffd), F32), up_sums, core, 1).reshape(width, upc)
    slots = -(-chips // wr)
    slot = lax.broadcasted_iota(jnp.int32, (wr, slots), 0) + wr * lax.broadcasted_iota(jnp.int32, (wr, slots), 1)
    high = (error * once).astype(BF).astype(F32)
    low = error * once - high
    marks = jnp.concatenate([jnp.where(slot == chip, high, 0.0), jnp.where(slot == chip, low, 0.0)], 1)
    marks = jnp.tile(marks, (2 * chips, 1))
    columns = jnp.concatenate([columns, up_sums, jnp.zeros((width, 8 - upc), F32), marks, jnp.zeros((width, LANES - 16 - 2 * slots), F32)], 1)
    third = jnp.concatenate([gw_qkv, columns.astype(BF)], 1).reshape(sy, sz, sx, 2 * wr, -1)
    third = scatter_sum(scatter_sum(third, "y", 0), "x", 2)
    third = scatter_sum(third, "z", 1, F32).reshape(2, wr, -1)

    def swap(value):
        kept = of_core(value, core, 0)
        return kept, shift(of_core(value, 1 - core, 0), "core", 1)

    kept, came = swap(second)
    low_part, high_part = jnp.where(core == 0, kept, came), jnp.where(core == 0, came, kept)
    grad_w_out = jnp.concatenate([low_part[:, :half], high_part[:, :half]], 1)
    grad_w_up = jnp.stack([low_part[:, half:].reshape(wr, chips, ffd), high_part[:, half:].reshape(wr, chips, ffd)], 2).reshape(wr, -1)
    kept, came = swap(third)
    sums = kept[:, 3 * half:] + came[:, 3 * half:]
    low_part, high_part = jnp.where(core == 0, kept, came), jnp.where(core == 0, came, kept)
    grad_w_qkv = jnp.stack([low_part[:, :3 * half].reshape(wr, 3, half), high_part[:, :3 * half].reshape(wr, 3, half)], 2).reshape(wr, -1)
    loss = jnp.sum(sums[:, 16:16 + 2 * slots]) / (count * width)

    start = own * two_rows + core * rows
    n1_dev = lax.dynamic_slice_in_dim(n1, start, rows, 0)
    r1_dev = lax.dynamic_slice_in_dim(r1, start, rows, 0)
    input_grad = lax.dynamic_slice_in_dim(grad_res, core * rows, rows, 0) + norm_back(n1_dev, r1_dev, back, g1)
    return (
        layer_out[None], loss, input_grad[None], grad_w_qkv, sums[:, 0], sums[:, 1], grad_w_out, sums[:, 2],
        grad_w_up, sums[:, 8:8 + upc].reshape(-1), gw_down, sums[:, 3], sums[:, 4], sums[:, 5], sums[:, 6], sums[:, 7],
    )


def solution(mesh):
    seq, ctx = mesh.shape["seq"], mesh.shape["ctx"]
    grid = Mesh(mesh.devices.reshape(seq, ZS, ctx // (2 * ZS), 2), ("y", "z", "x", "core"))
    every = ("y", "z", "x", "core")
    matrix, vector = P(every, None), P(every)
    tokens = P("y", ("z", "x", "core"), None)
    marks = P("y", ("z", "x", "core"))
    return jax.shard_map(
        per_device,
        mesh=grid,
        in_specs=(tokens, matrix, vector, vector, matrix, vector, matrix, vector, matrix, vector, vector, vector, vector, vector, marks, marks, tokens, tokens),
        out_specs=(tokens, P(), tokens, matrix, vector, vector, matrix, vector, matrix, vector, matrix, vector, vector, vector, vector, vector),
        check_vma=False,
    )
```

```python
import functools

import jax
import jax.numpy as jnp
from jax import lax
from jax.experimental import pallas as pl
from jax.experimental.pallas import tpu as pltpu
from jax.sharding import Mesh
from jax.sharding import PartitionSpec as P

HEADS = 12
HEAD_DIM = 64
ZS = 4
BF = jnp.bfloat16
F32 = jnp.float32
NEG = -1e30
LANES = 128


def shift(value, axis, step):
    size = lax.axis_size(axis)
    return lax.ppermute(value, axis, [(a, (a + step) % size) for a in range(size)])


def gather(value, axis, dim, after=()):
    size = lax.axis_size(axis)
    return arrange([value] + [shift(value, axis, d) for d in range(1, size)], lax.axis_index(axis), dim, after)


def scatter_sum(value, axis, dim, last=BF, after=()):
    size = lax.axis_size(axis)
    place = lax.axis_index(axis)

    def cut(d):
        return lax.dynamic_slice_in_dim(value, lax.rem(place + d, size), 1, dim)

    came = [shift(cut(d), axis, d) for d in range(1, size)]

    def body(place_ref, value_ref, *refs):
        index = (slice(None),) * dim + (pl.ds(place_ref[0], 1),)
        total = value_ref[index].astype(F32)
        for ref in refs[:size - 1]:
            total = total + ref[...].astype(F32)
        refs[-1][...] = total.astype(last)

    vmem = pl.BlockSpec(memory_space=pltpu.VMEM)
    return pl.pallas_call(
        body,
        in_specs=[pl.BlockSpec(memory_space=pltpu.SMEM)] + [vmem] * size + [pl.BlockSpec(memory_space=pl.ANY)] * len(after),
        out_shape=jax.ShapeDtypeStruct(came[0].shape, last),
        compiler_params=params(),
        cost_estimate=SMALL,
        name="scatter_sum",
    )(place.astype(jnp.int32).reshape(1), value, *came, *after)


def spread_tokens(value):
    some = [value] + [shift(value, "x", d) for d in range(1, lax.axis_size("x"))]
    return some + [shift(member, "core", 1) for member in some]


def fold_tokens(kept, sent, after=()):
    came = shift(sent, "core", 1)
    size = kept.shape[0]
    shape = kept.shape[1:]

    def body(kept_ref, came_ref, *outs):
        for d in range(size):
            outs[d][...] = (kept_ref[d] + came_ref[d].astype(F32)).astype(outs[d].dtype)

    terms = call(body, (kept, came), [(shape, BF if d else F32) for d in range(size)], "fold_tokens", 0, after)
    return [terms[0]] + [shift(terms[d], "x", -d) for d in range(1, size)]


def dot(a, b):
    return jnp.dot(a, b, preferred_element_type=F32)


def dot_nt(a, b):
    return lax.dot_general(a, b, (((1,), (1,)), ((), ())), preferred_element_type=F32)


def dot_tn(a, b):
    return lax.dot_general(a, b, (((0,), (0,)), ((), ())), preferred_element_type=F32)


SMALL = pl.CostEstimate(flops=1, bytes_accessed=1, transcendentals=0)


def params(mib=6):
    return pltpu.CompilerParams(vmem_limit_bytes=mib * 1024 * 1024)


def pack_one(w_qkv, flat, seg, mask):
    rows, width = w_qkv.shape[0], w_qkv.shape[1] // 3
    group = width // ZS
    hd = HEAD_DIM
    upc = flat.shape[0] - 8

    def body(qkv_ref, flat_ref, seg_ref, mask_ref, one_ref, vec):
        vec[...] = jnp.zeros_like(vec)
        vec[0:8 + upc, 0:rows] = flat_ref[...].astype(F32)
        count = jnp.sum(mask_ref[...].astype(F32), -1, keepdims=True)
        lane = lax.broadcasted_iota(jnp.int32, (LANES, LANES), 1)
        vec[...] = jnp.where(lane == 8 + upc, count, vec[...].T)
        ids = seg_ref[...].astype(F32)
        vec[0:1, hd:] = ids[:, 0:hd]
        vec[1:2, hd:] = ids[:, hd:]
        cols = vec[0:rows, :].astype(BF)
        for g in range(ZS):
            k = width + g * group
            v = 2 * width + g * group
            one_ref[g, :, 0:3 * hd] = qkv_ref[:, k:k + 3 * hd]
            one_ref[g, :, 3 * hd:4 * hd] = qkv_ref[:, v + 2 * hd:v + 3 * hd]
            one_ref[g, :, 4 * hd:6 * hd] = qkv_ref[:, v:v + 2 * hd]
            one_ref[g, :, 6 * hd:9 * hd] = qkv_ref[:, g * group:g * group + 3 * hd]
            one_ref[g, :, 9 * hd:11 * hd] = cols

    specs = [pl.BlockSpec(a.shape, lambda i: (0, 0)) for a in (w_qkv, flat, seg, mask)]
    return pl.pallas_call(
        body,
        grid=(1,),
        in_specs=specs,
        out_specs=pl.BlockSpec((ZS, rows, 11 * hd), lambda i: (0, 0, 0)),
        out_shape=jax.ShapeDtypeStruct((ZS, rows, 11 * hd), BF),
        scratch_shapes=[pltpu.VMEM((LANES, LANES), F32)],
        compiler_params=params(),
        cost_estimate=SMALL,
        name="pack_one",
    )(w_qkv, flat, seg, mask)


def pack_up(w_up, w_out, ffd, sx):
    rows, width = w_out.shape
    blocks = w_up.shape[1] // (2 * sx * ffd)
    ff = blocks * ffd

    def body(up_ref, out_ref, to_ref):
        for c in range(2):
            for x in range(sx):
                for b in range(blocks):
                    at = ((b * sx + x) * 2 + c) * ffd
                    to_ref[c, x, :, b * ffd:(b + 1) * ffd] = up_ref[:, at:at + ffd]
                to_ref[c, x, :, ff:] = out_ref[...]

    return call(body, (w_up, w_out), [((2, sx, rows, ff + width), BF)], "pack_up")[0]


def held(value, after):
    def body(value_ref, *rest):
        rest[-1][...] = value_ref[...]

    return pl.pallas_call(
        body,
        in_specs=[pl.BlockSpec(memory_space=pltpu.VMEM)] + [pl.BlockSpec(memory_space=pl.ANY)] * len(after),
        out_shape=jax.ShapeDtypeStruct(value.shape, value.dtype),
        compiler_params=params(),
        cost_estimate=SMALL,
        name="held",
    )(value, *after)


def arrange(pieces, place, dim, after=()):
    size = len(pieces)
    shape = list(pieces[0].shape)
    shape[dim] = size

    def body(place_ref, *refs):
        out = refs[-1]
        for d in range(size):
            spot = lax.rem(place_ref[0] + size - d, size)
            index = (slice(None),) * dim + (pl.ds(spot, 1),)
            out[index] = refs[d][...]

    return pl.pallas_call(
        body,
        in_specs=[pl.BlockSpec(memory_space=pltpu.SMEM)] + [pl.BlockSpec(memory_space=pltpu.VMEM)] * size + [pl.BlockSpec(memory_space=pl.ANY)] * len(after),
        out_shape=jax.ShapeDtypeStruct(tuple(shape), pieces[0].dtype),
        compiler_params=params(),
        cost_estimate=SMALL,
        name="arrange",
    )(place.astype(jnp.int32).reshape(1), *pieces, *after)


def project_kernel(place, h0, h1, h2, h3, w_ref, gain_ref, shift_ref, bkv_ref, bq_ref, n1_ref, q_ref, kv_ref):
    rows = h0.shape[0]
    hd = HEAD_DIM
    for d, piece in enumerate((h0, h1, h2, h3)):
        spot = pl.ds(pl.multiple_of(lax.rem(place[0] + ZS - d, ZS) * rows, rows), rows)
        values = piece[...].astype(F32)
        centered = values - jnp.mean(values, -1, keepdims=True)
        rstd = lax.rsqrt(jnp.mean(centered * centered, -1, keepdims=True) + 1e-05)
        n1 = (centered * rstd * gain_ref[...] + shift_ref[...]).astype(BF)
        n1_ref[spot, :] = n1
        joined = dot(n1, w_ref[:, 0:9 * hd])
        kv_ref[spot, :] = (joined[:, 0:6 * hd] + bkv_ref[...]).astype(BF)
        q = (joined[:, 6 * hd:9 * hd] + bq_ref[...]).astype(BF).astype(F32) * 0.125
        q_ref[spot, 0:3 * hd] = q.astype(BF)
        q_ref[spot, 3 * hd:4 * hd] = jnp.zeros((rows, hd), BF)


def project(place, pieces, w, gain, shift_row, bkv, bq):
    total, width = ZS * pieces[0].shape[0], pieces[0].shape[1]
    outs = [((total, width), BF), ((total, 4 * HEAD_DIM), BF), ((total, 6 * HEAD_DIM), BF)]
    return call(project_kernel, (place, *pieces, w, gain, shift_row, bkv, bq), outs, "project", 1)


def fill_keys(kv_refs, keys, rows):
    for j, ref in enumerate(kv_refs):
        for z in range(ZS):
            at = (z * len(kv_refs) + j) * rows
            keys[at:at + rows, :] = ref[z * rows:(z + 1) * rows, :]


def turn_segments(order, seg_ref, turned, count):
    turned[...] = jnp.zeros_like(turned)
    for z in range(ZS):
        for j in range(count):
            turned[z * count + j:z * count + j + 1, :] = seg_ref[pl.ds(z * count + order[j], 1), :]
    queries = jnp.concatenate([turned[z * count:z * count + 1, :] for z in range(ZS)], 1)
    turned[...] = turned[...].T
    return queries


def fill_bias(order, queries, turned, bias, z, count, rows):
    for j in range(count):
        same = turned[:, z * count + j:z * count + j + 1] == queries[:, z * rows:]
        bias[j * rows:(j + 1) * rows, z * rows:] = jnp.where(same, 0.0, NEG)
        key = lax.broadcasted_iota(jnp.int32, (rows, rows), 0) + order[j] * rows
        query = lax.broadcasted_iota(jnp.int32, (rows, rows), 1) + order[0] * rows
        ok = same[:, 0:rows] & (key <= query)
        bias[j * rows:(j + 1) * rows, z * rows:(z + 1) * rows] = jnp.where(ok, 0.0, NEG)


def head_parts(q_ref, keys, z, span, lower_q, lower_k):
    at = slice(z * span, (z + 1) * span)
    k01, kv2, v01 = (keys[at, i * LANES:(i + 1) * LANES] for i in range(3))
    one = jnp.ones_like(k01)
    return (k01, k01, kv2), (jnp.where(lower_k, v01, one), jnp.where(lower_k, one, v01), jnp.where(lower_k, one, kv2))


def attend_kernel(order, q_ref, seg_ref, *rest):
    count = len(rest) - 10
    kv_refs, low_refs, (ctx_ref, tot_ref), (keys, bias, acc, turned) = rest[:count], rest[count:count + 4], rest[count + 4:count + 6], rest[count + 6:]
    total = q_ref.shape[0]
    rows = total // ZS
    span = count * rows
    fill_keys(kv_refs, keys, rows)
    queries = turn_segments(order, seg_ref, turned, count)
    lower_q = lax.broadcasted_iota(jnp.int32, (total, LANES), 1) < HEAD_DIM
    lower_k = lax.broadcasted_iota(jnp.int32, (span, LANES), 1) < HEAD_DIM
    q01, q2 = q_ref[:, 0:LANES], q_ref[:, LANES:2 * LANES]
    none = jnp.zeros_like(q01)
    qs = (jnp.where(lower_q, q01, none), jnp.where(lower_q, none, q01), q2)
    for z in range(ZS):
        fill_bias(order, queries, turned, bias, z, count, rows)
        ks, vs = head_parts(q_ref, keys, z, span, lower_q, lower_k)
        for h in range(3):
            scores = dot_nt(ks[h], qs[h][z * rows:, :]) + bias[:, z * rows:]
            expo = jnp.exp(scores).astype(BF)
            part = dot_tn(vs[h], expo)
            if z == 0:
                acc[h] = part
            else:
                acc[h, :, z * rows:] += part
    u0, u1, u2 = (acc[h].T for h in range(3))
    unnormed = jnp.where(lower_q, u0, u1)
    totals = jnp.where(lower_q, pltpu.roll(u0, HEAD_DIM, 1), pltpu.roll(u1, HEAD_DIM, 1))
    ctx = unnormed / totals
    tot_ref[:, 0:LANES] = totals
    ctx_ref[:, 0:LANES] = ctx
    ctx = pltpu.roll(u2, HEAD_DIM, 1) / u2
    tot_ref[:, LANES:] = u2
    ctx_ref[:, LANES:] = ctx
    for d in range(ZS):
        spot = pl.ds(pl.multiple_of(lax.rem(order[count] + d, ZS) * rows, rows), rows)
        low_refs[d][...] = ctx_ref[spot, 0:3 * HEAD_DIM].astype(BF)


def attend(order, q, seg, kvs, after=()):
    total = q.shape[0]
    span = len(kvs) * total // ZS
    outs = [((total // ZS, 3 * HEAD_DIM), BF)] * ZS + [((total, 2 * LANES), F32)] * 2
    scratch = [pltpu.VMEM((ZS * span, 3 * LANES), BF), pltpu.VMEM((span, total), F32), pltpu.VMEM((3, LANES, total), F32), pltpu.VMEM((LANES, LANES), F32)]
    return call(attend_kernel, (order, q, seg, *kvs), outs, "attend", 1, after, scratch, 28)


def attend_back_kernel(order, q_ref, gc0, gc1, gc2, gc3, ctx_ref, tot_ref, seg_ref, *rest):
    count = len(rest) - 9
    kv_refs, (dq_ref, kept_ref, sent_ref), (keys, bias, ge, acc, gctx_ref, turned) = rest[:count], rest[count:count + 3], rest[count + 3:]
    total = q_ref.shape[0]
    rows = total // ZS
    for d, ref in enumerate((gc0, gc1, gc2, gc3)):
        spot = pl.ds(pl.multiple_of(lax.rem(order[count] + ZS - d, ZS) * rows, rows), rows)
        gctx_ref[spot, :] = ref[...].astype(F32)
    span = count * rows
    fill_keys(kv_refs, keys, rows)
    queries = turn_segments(order, seg_ref, turned, count)
    lane = lax.broadcasted_iota(jnp.int32, (total, LANES), 1)
    lower_q = lane < HEAD_DIM
    lower_k = lax.broadcasted_iota(jnp.int32, (span, LANES), 1) < HEAD_DIM
    q01, q2 = q_ref[:, 0:LANES], q_ref[:, LANES:2 * LANES]
    none = jnp.zeros_like(q01)
    qs = (jnp.where(lower_q, q01, none), jnp.where(lower_q, none, q01), q2)
    gs = []
    g01 = gctx_ref[:, 0:LANES]
    g2 = jnp.concatenate([jnp.zeros((total, HEAD_DIM), F32), gctx_ref[:, LANES:]], 1)
    c2 = pltpu.roll(ctx_ref[:, LANES:], HEAD_DIM, 1)
    t2 = tot_ref[:, LANES:]
    t2 = jnp.where(lower_q, 1.0, pltpu.roll(t2, HEAD_DIM, 1))
    for h in range(3):
        grad = g2 if h == 2 else g01
        tot = t2 if h == 2 else tot_ref[:, 0:LANES]
        ctx = c2 if h == 2 else ctx_ref[:, 0:LANES]
        mine = lower_q if h == 0 else jnp.logical_not(lower_q)
        gu = jnp.where(mine, grad / tot, 0.0).astype(BF)
        gtot = -jnp.sum(jnp.where(mine, grad * ctx / tot, 0.0), -1, keepdims=True)
        high = gtot.astype(BF)
        low = (gtot - high.astype(F32)).astype(BF)
        first = HEAD_DIM if h == 0 else 0
        ge[h] = jnp.where(lane == first, high, jnp.where(lane == first + 1, low, gu))
        gs.append(gu)
    for z in range(ZS):
        fill_bias(order, queries, turned, bias, z, count, rows)
        ks, vs = head_parts(q_ref, keys, z, span, lower_q, lower_k)
        dk, dv = [], []
        for h in range(3):
            qz = qs[h][z * rows:, :]
            expo = jnp.exp(dot_nt(ks[h], qz) + bias[:, z * rows:])
            gprob = dot_nt(vs[h], ge[h, z * rows:, :])
            gscore = (expo * gprob).astype(BF)
            dv.append(dot(expo.astype(BF), gs[h][z * rows:, :]))
            dk.append(dot(gscore, qz))
            part = dot_tn(ks[h], gscore)
            if z == 0:
                acc[h] = part
            else:
                acc[h, :, z * rows:] += part
        parts = (dk[0] + dk[1], dk[2] + dv[2], dv[0] + dv[1])
        for j in range(count):
            to = kept_ref if j < count // 2 else sent_ref
            for i in range(3):
                to[j % (count // 2), z * rows:(z + 1) * rows, i * LANES:(i + 1) * LANES] = parts[i][j * rows:(j + 1) * rows, :].astype(to.dtype)
    upper = lax.broadcasted_iota(jnp.int32, (LANES, total), 0) >= HEAD_DIM
    dq_ref[:, 0:LANES] = (0.125 * jnp.where(upper, acc[1], acc[0])).T.astype(BF)
    dq_ref[:, LANES:] = (0.125 * acc[2]).T[:, 0:HEAD_DIM].astype(BF)


def attend_back(order, q, gctx, ctx, tot, seg, kvs, after=()):
    total = q.shape[0]
    count = len(kvs)
    span = count * total // ZS
    outs = [((total, 3 * HEAD_DIM), BF), ((count // 2, total, 6 * HEAD_DIM), F32), ((count // 2, total, 6 * HEAD_DIM), BF)]
    scratch = [
        pltpu.VMEM((ZS * span, 3 * LANES), BF),
        pltpu.VMEM((span, total), F32),
        pltpu.VMEM((3, total, LANES), BF),
        pltpu.VMEM((3, LANES, total), F32),
        pltpu.VMEM((total, 3 * HEAD_DIM), F32),
        pltpu.VMEM((LANES, LANES), F32),
    ]
    return call(attend_back_kernel, (order, q, *gctx, ctx, tot, seg, *kvs), outs, "attend_back", 1, after, scratch, 32)


def norm_parts(values):
    mean = jnp.mean(values, -1, keepdims=True)
    centered = values - mean
    rstd = lax.rsqrt(jnp.mean(centered * centered, -1, keepdims=True) + 1e-05)
    return centered * rstd, rstd


def norm_back(normed, rstd, grad, gain):
    q = grad * gain
    return rstd * (q - jnp.mean(q, -1, keepdims=True) - normed * jnp.mean(q * normed, -1, keepdims=True))


GC = 0.7978845608028654


def call(body, args, outs, name, smem=0, after=(), scratch=(), mib=16, keep=()):
    large = [i for i in keep]
    specs = [pl.BlockSpec(memory_space=pltpu.SMEM if i < smem else pl.ANY if i in large else pltpu.VMEM) for i in range(len(args))]
    count = len(args)
    fetched = [pltpu.VMEM(args[i].shape, args[i].dtype) for i in large]

    def whole(*refs):
        ins, rest = list(refs[:count]), refs[count + len(after):]
        if large:
            rest, slots, sems = rest[:-len(large) - 1], rest[-len(large) - 1:-1], rest[-1]
            copies = [pltpu.make_async_copy(ins[i], slot, sems.at[n]) for n, (i, slot) in enumerate(zip(large, slots))]
            for copy in copies:
                copy.start()
            for copy in copies:
                copy.wait()
            for i, slot in zip(large, slots):
                ins[i] = slot
        body(*ins, *rest)

    return pl.pallas_call(
        whole,
        in_specs=specs + [pl.BlockSpec(memory_space=pl.ANY)] * len(after),
        out_shape=[jax.ShapeDtypeStruct(*out) for out in outs],
        scratch_shapes=list(scratch) + fetched + ([pltpu.SemaphoreType.DMA((len(large),))] if large else []),
        compiler_params=params(mib),
        cost_estimate=SMALL,
        name=name,
    )(*args, *after)


def fold(own, came, place, dim, size, name="fold"):
    shape = list(own.shape)
    shape[dim] //= size
    part = shape[dim]

    def body(place_ref, own_ref, *refs):
        for d in range(size):
            spot = lax.rem(place_ref[0] + d, size) * part
            index = (slice(None),) * dim + (pl.ds(spot, part),)
            total = own_ref[index].astype(F32)
            for ref in refs[:len(came)]:
                total = total + ref[index].astype(F32)
            refs[len(came) + d][...] = total.astype(F32 if d == 0 else BF)

    outs = [(tuple(shape), BF if d else F32) for d in range(size)]
    return call(body, (place.astype(jnp.int32).reshape(1), own, *came), outs, name, 1)


def passed(pieces, axis):
    return [shift(pieces[d], axis, d) for d in range(1, len(pieces))]


def out_project(place, pieces, w_out, bias, hidden, gain, shift_row, at, after):
    rows, group = pieces[0].shape
    width = hidden.shape[1]

    def body(place_ref, p0, p1, p2, p3, w_ref, bias_ref, hidden_ref, gain_ref, shift_ref, res_ref, n2_ref):
        total = hidden_ref[...].astype(F32) + bias_ref[...]
        for d, piece in enumerate((p0, p1, p2, p3)):
            spot = pl.ds(pl.multiple_of(lax.rem(place_ref[0] + ZS - d, ZS) * group, group), group)
            total = total + dot(piece[...], w_ref[spot, at:at + width])
        res_ref[...] = total
        n2, _ = norm_parts(total)
        n2_ref[...] = (n2 * gain_ref[...] + shift_ref[...]).astype(BF)

    return call(body, (place, *pieces, w_out, bias, hidden, gain, shift_row), [((rows, width), F32), ((rows, width), BF)], "out_project", 1, after)


def mlp_up(blocks, weights, bias):
    rows, width = blocks[0].shape
    count = len(blocks)
    half = count // 2
    ff = bias.shape[1]

    def body(*refs):
        n2_refs, (bias_ref, w_ref), (kept_ref, sent_ref, act_ref, slope_ref) = refs[:count], refs[count:count + 2], refs[-4:]
        down_ref = refs[count + 2] if len(weights) == 2 else w_ref.at[:, ff + width:]
        for j in range(count):
            pre = dot(n2_refs[j][...], w_ref[:, 0:ff]) + bias_ref[...]
            square = pre * pre
            tanh = jnp.tanh(GC * pre * (1.0 + 0.044715 * square))
            half_one = 0.5 * (1.0 + tanh)
            act = (pre * half_one).astype(BF)
            slope_ref[j] = half_one + 0.5 * pre * (1.0 - tanh * tanh) * (GC + GC * 0.134145 * square)
            act_ref[j * rows:(j + 1) * rows, :] = act
            part = dot(act, down_ref[...])
            if j < half:
                kept_ref[j] = part
            else:
                sent_ref[j - half] = part.astype(BF)

    outs = [((half, rows, width), F32), ((half, rows, width), BF), ((count * rows, ff), BF), ((count, rows, ff), F32)]
    return call(body, (*blocks, bias, *weights), outs, "mlp_up")


def finish(terms, residual, bias, teacher, cotangent, mask, scale):
    rows, width = residual.shape
    size = len(terms)

    def body(scale_ref, *refs):
        res_ref, bias_ref, teacher_ref, cot_ref, mask_ref, out_ref, err_ref, gfin_ref, gmlp_ref = refs[size:]
        valid = jnp.broadcast_to(mask_ref[...].astype(F32), (LANES, rows)).T[:, 0:1]
        final = res_ref[...] + bias_ref[...]
        for ref in refs[:size]:
            final = final + ref[...].astype(F32)
        out_ref[...] = final.astype(BF)
        deviation = final - teacher_ref[...].astype(F32)
        err_ref[...] = jnp.sum(valid * deviation * deviation, 0, keepdims=True)
        grad = valid * (cot_ref[...].astype(F32) + deviation * scale_ref[0])
        gfin_ref[...] = grad
        gmlp_ref[...] = grad.astype(BF)

    outs = [((rows, width), BF), ((1, width), F32), ((rows, width), F32), ((rows, width), BF)]
    return call(body, (scale, *terms, residual, bias, teacher, cotangent, mask), outs, "finish", 1)


def mlp_back(grads, weights, slope):
    rows, width = grads[0].shape
    count = len(grads)
    half = count // 2
    ff = slope.shape[2]

    def body(*refs):
        g_refs, (slope_ref, w_ref), (kept_ref, sent_ref, gpre_ref) = refs[:count], refs[count:count + 2], refs[-3:]
        down_ref = refs[count + 2] if len(weights) == 2 else w_ref.at[:, ff + width:]
        for j in range(count):
            gpre = (dot_nt(g_refs[j][...], down_ref[...]) * slope_ref[j]).astype(BF)
            gpre_ref[j * rows:(j + 1) * rows, :] = gpre
            part = dot_nt(gpre, w_ref[:, 0:ff])
            if j < half:
                kept_ref[j] = part
            else:
                sent_ref[j - half] = part.astype(BF)

    outs = [((half, rows, width), F32), ((half, rows, width), BF), ((count * rows, ff), BF)]
    return call(body, (*grads, slope, *weights), outs, "mlp_back")


def mlp_weights(grads, act, blocks, gpre):
    rows, width = grads[0].shape
    count = len(grads)
    ff = act.shape[1]

    def body(*refs):
        g_refs, act_ref, n_refs, gpre_ref, outs, (g_all, n_all) = refs[:count], refs[count], refs[count + 1:2 * count + 1], refs[2 * count + 1], refs[2 * count + 2:-2], refs[-2:]
        down_ref, up_ref = (outs[0].at[:, 0:width], outs[0].at[:, width:]) if ff == width else outs[:2]
        for j in range(count):
            g_all[j * rows:(j + 1) * rows, :] = g_refs[j][...]
            n_all[j * rows:(j + 1) * rows, :] = n_refs[j][...]
        down_ref[...] = dot_tn(act_ref[...], g_all[...]).astype(BF)
        up_ref[...] = dot_tn(n_all[...], gpre_ref[...]).astype(BF)
        outs[-1][...] = jnp.sum(gpre_ref[...].astype(F32), 0, keepdims=True)

    outs = [((width, 2 * width), BF)] if ff == width else [((ff, width), BF), ((width, ff), BF)]
    scratch = [pltpu.VMEM((count * rows, width), BF)] * 2
    *grads, sums = call(body, (*grads, act, *blocks, gpre), outs + [((1, ff), F32)], "mlp_weights", scratch=scratch)
    return grads, sums


def out_back(place, terms, residual, gain, gfin, pieces, w_out, gmlp, at, after):
    rows, width = residual.shape
    group = pieces[0].shape[1]
    size = len(terms)

    def body(place_ref, *refs):
        res_ref, gain_ref, gfin_ref = refs[size:size + 3]
        p_refs, (w_ref, gmlp_ref), gres_ref, gctx_refs, (gw_ref, sums_ref) = refs[size + 3:size + 7], refs[size + 7:size + 9], refs[size + 9], refs[size + 10:size + 14], refs[size + 14:]
        gn2 = refs[0][...]
        for ref in refs[1:size]:
            gn2 = gn2 + ref[...].astype(F32)
        n2, rstd = norm_parts(res_ref[...])
        gres = gfin_ref[...] + norm_back(n2, rstd, gn2, gain_ref[...])
        gres_ref[...] = gres
        branch = gres.astype(BF)
        for d in range(ZS):
            spot = pl.ds(pl.multiple_of(lax.rem(place_ref[0] + d, ZS) * group, group), group)
            gctx_refs[d][...] = dot_nt(branch, w_ref[spot, at:at + width]).astype(BF)
        for d in range(ZS):
            spot = pl.ds(pl.multiple_of(lax.rem(place_ref[0] + ZS - d, ZS) * group, group), group)
            gw_ref[spot, :] = dot_tn(p_refs[d][...], branch).astype(BF)
        rowsum = lambda v: jnp.sum(v, 0, keepdims=True)
        sums_ref[0:1, :] = rowsum(branch.astype(F32))
        sums_ref[1:2, :] = rowsum(gmlp_ref[...].astype(F32))
        sums_ref[2:3, :] = rowsum(gn2 * n2)
        sums_ref[3:4, :] = rowsum(gn2)

    outs = [((rows, width), F32)] + [((rows, group), BF)] * ZS + [((width, width), BF), ((4, width), F32)]
    return call(body, (place, *terms, residual, gain, gfin, *pieces, w_out, gmlp), outs, "out_back", 1, after)


def join_back(place, terms, dq, w):
    total, group = dq.shape
    width = w.shape[0]
    rows = total // ZS
    size = len(terms)
    cols = 3 * group

    def body(place_ref, *refs):
        dq_ref, w_ref, gj_ref, gn1_ref = refs[size:size + 4]
        out_refs = refs[size + 4:]
        dkv = refs[0][...]
        for ref in refs[1:size]:
            dkv = dkv + ref[...].astype(F32)
        gj_ref[:, 0:2 * group] = dkv.astype(BF)
        gj_ref[:, 2 * group:] = dq_ref[...]
        gn1_ref[...] = dot_nt(gj_ref[...], w_ref[:, 0:cols])
        for d in range(ZS):
            spot = pl.ds(pl.multiple_of(lax.rem(place_ref[0] + d, ZS) * rows, rows), rows)
            out_refs[d][...] = gn1_ref[spot, :].astype(out_refs[d].dtype)

    outs = [((total, cols), BF), ((total, width), F32)] + [((rows, width), BF if d else F32) for d in range(ZS)]
    return call(body, (place, *terms, dq, w), outs, "join_back", 1)


def weights_back(place, n1, grad_joined, gn1, pieces, out_sums, up_rows, marks, gw_out, wr):
    total, cols = grad_joined.shape
    width = n1.shape[1]
    rows = total // ZS
    group = cols // 3
    upc = up_rows.shape[0]
    markc = marks.shape[0]
    chips = width // (2 * wr)
    wide = cols + LANES + width

    def body(place_ref, n1_ref, gj_ref, gn1_ref, h0, h1, h2, h3, sums_ref, up_ref, marks_ref, gw_ref, kept_ref, sent_ref, vec, full):
        gain_sum = jnp.zeros((1, width), F32)
        for d, piece in enumerate((h0, h1, h2, h3)):
            spot = pl.ds(pl.multiple_of(lax.rem(place_ref[0] + ZS - d, ZS) * rows, rows), rows)
            normed, _ = norm_parts(piece[...].astype(F32))
            gain_sum = gain_sum + jnp.sum(gn1_ref[spot, :] * normed, 0, keepdims=True)
        joined_sums = jnp.sum(gj_ref[...].astype(F32), 0, keepdims=True)
        vec[...] = jnp.zeros_like(vec)
        hd = HEAD_DIM
        for g in range(ZS):
            here = place_ref[0] == g
            at = g * group
            vec[0:1, at:at + group] = jnp.where(here, joined_sums[:, 2 * group:], 0.0)
            vec[1:2, at:at + 2 * hd] = jnp.where(here, joined_sums[:, 4 * hd:6 * hd], 0.0)
            vec[1:2, at + 2 * hd:at + 3 * hd] = jnp.where(here, joined_sums[:, 3 * hd:4 * hd], 0.0)
        vec[2:4, :] = sums_ref[0:2, :]
        vec[4:5, :] = gain_sum
        vec[5:6, :] = jnp.sum(gn1_ref[...], 0, keepdims=True)
        vec[6:8, :] = sums_ref[2:4, :]
        vec[8:8 + upc, :] = up_ref[...]
        vec[16:16 + markc, :] = marks_ref[...]
        full[:, 0:cols] = dot_tn(n1_ref[...], gj_ref[...])
        full[:, cols:cols + LANES] = vec[...].T
        full[:, cols + LANES:] = gw_ref[...].astype(F32)
        for c in range(2):
            @pl.when(place_ref[1] == c)
            def _():
                for chip in range(chips):
                    at = chip * 2 * wr
                    kept_ref[chip] = full[at + c * wr:at + (c + 1) * wr, :].astype(BF)
                    sent_ref[chip] = full[at + (1 - c) * wr:at + (2 - c) * wr, :].astype(BF)

    outs = [((chips, wr, wide), BF)] * 2
    scratch = [pltpu.VMEM((LANES, width), F32), pltpu.VMEM((width, wide), F32)]
    return call(body, (place, n1, grad_joined, gn1, *pieces, out_sums, up_rows, marks, gw_out), outs, "weights_back", 1, scratch=scratch, mib=28)


def input_back(terms, hidden, gain, grad_res):
    rows, width = hidden.shape

    def body(t0, t1, t2, t3, hidden_ref, gain_ref, gres_ref, out_ref):
        back = t0[...] + t1[...].astype(F32) + t2[...].astype(F32) + t3[...].astype(F32)
        normed, rstd = norm_parts(hidden_ref[...].astype(F32))
        out_ref[...] = gres_ref[...] + norm_back(normed, rstd, back, gain_ref[...])

    return call(body, (*terms, hidden, gain, grad_res), [((rows, width), F32)], "input_back")[0]


def unpack_one(place, pieces):
    rows, wide = pieces[0].shape[-2:]
    hd = HEAD_DIM
    group = 3 * hd
    width = ZS * group

    def body(place_ref, p0, p1, p2, p3, qkv_ref, vec_ref, out_ref, held_ref):
        for d, piece in enumerate((p0, p1, p2, p3)):
            held_ref[pl.ds(lax.rem(place_ref[0] + ZS - d, ZS), 1)] = piece[...].reshape(1, rows, wide).astype(F32)
        total = jnp.zeros((rows, LANES + width), F32)
        for g in range(ZS):
            k = width + g * group
            v = 2 * width + g * group
            qkv_ref[:, k:k + 3 * hd] = held_ref[g, :, 0:3 * hd]
            qkv_ref[:, v + 2 * hd:v + 3 * hd] = held_ref[g, :, 3 * hd:4 * hd]
            qkv_ref[:, v:v + 2 * hd] = held_ref[g, :, 4 * hd:6 * hd]
            qkv_ref[:, g * group:g * group + 3 * hd] = held_ref[g, :, 6 * hd:9 * hd]
            total = total + held_ref[g, :, 9 * hd:]
        vec_ref[...] = total[:, 0:LANES]
        out_ref[...] = total[:, LANES:]

    outs = [((rows, 3 * width), F32), ((rows, LANES), F32), ((rows, width), F32)]
    return call(body, (place, *pieces), outs, "unpack_one", 1, scratch=[pltpu.VMEM((ZS, rows, wide), F32)])


def per_device(hidden_in, w_qkv, q_bias, v_bias, w_out, out_bias, w_up, up_bias, w_down, down_bias, ln1_gain, ln1_bias, ln2_gain, ln2_bias, segment_ids, padding_mask, teacher, cotangent):
    sy, sz, sx = (lax.axis_size(a) for a in ("y", "z", "x"))
    iy, iz, ix, core = (lax.axis_index(a) for a in ("y", "z", "x", "core"))
    device = ((iy * sz + iz) * sx + ix) * 2 + core
    devices = sy * sz * sx * 2
    rows, width = hidden_in.shape[1:]
    wr = w_qkv.shape[0]
    ffd = w_down.shape[0]
    ff = sy * sz * ffd
    upc = ffd // wr
    wcols = 9 * HEAD_DIM
    group = width // sz
    place = iz.astype(jnp.int32).reshape(1)

    def from_z(value):
        return [value] + [shift(value, "z", d) for d in range(1, sz)]

    def to_z(pieces):
        return [pieces[0]] + [shift(pieces[d], "z", d) for d in range(1, sz)]

    def cut_z(value):
        return [lax.dynamic_slice_in_dim(value, lax.rem(iz + d, sz), 1, 0) for d in range(sz)]

    flat = jnp.concatenate([jnp.stack([q_bias, v_bias, out_bias, down_bias, ln1_gain, ln1_bias, ln2_gain, ln2_bias]), up_bias.reshape(upc, wr)])
    one_z = to_z(cut_z(pack_one(w_qkv, flat, segment_ids, padding_mask)))
    hidden = hidden_in[0]
    pieces = from_z(hidden)
    one = arrange(one_z, iz, 0)
    one = gather(one[None, :, None], "x", 2)
    one = gather(one, "y", 0)[:, :, :, None]
    one = gather(one, "core", 3).reshape(width, -1)

    mid = pack_up(w_up, w_out, ffd, sx)
    mid = arrange([lax.dynamic_slice_in_dim(mid, core, 1, 0), shift(lax.dynamic_slice_in_dim(mid, 1 - core, 1, 0), "core", 1)], core, 0)
    mid_x = [lax.dynamic_slice_in_dim(mid, lax.rem(ix + d, sx), 1, 1) for d in range(sx)]
    mid = arrange([mid_x[0]] + [shift(mid_x[d], "x", d) for d in range(1, sx)], ix, 1)
    weights = [mid.transpose(1, 0, 2, 3).reshape(2 * sx * wr, ff + width), w_down]
    if ff == width:
        weights = [jnp.concatenate(weights, 1)]
    weights = [lax.all_gather(member, ("y", "z"), axis=0, tiled=True) for member in weights]
    mid = weights[0]

    vec = one[:, wcols:wcols + LANES]
    vec_rows = vec[:, :16].T.astype(F32)
    qb, vb, ob, db, g1, b1, g2, b2 = (vec_rows[i][None] for i in range(8))
    ub = vec_rows[8:8 + upc].reshape(upc, sy * sz, sx * 2, wr)
    ub = lax.dynamic_index_in_dim(ub, ix * 2 + core, 2, keepdims=False).transpose(1, 0, 2).reshape(1, ff)
    count = jnp.sum(vec_rows[8 + upc]) / wr
    seg = lax.dynamic_index_in_dim(vec.reshape(sy, sz * sx * 2, wr, LANES), iy, 0, keepdims=False)[:, :2, HEAD_DIM:].astype(F32).reshape(sz * sx * 2, rows)
    qb_g = lax.dynamic_slice_in_dim(qb, iz * group, group, 1)
    vb_g = lax.dynamic_slice_in_dim(vb, iz * group, group, 1)
    bkv = jnp.concatenate([jnp.zeros((1, group), F32), vb_g[:, 2 * HEAD_DIM:], vb_g[:, :2 * HEAD_DIM]], 1)
    spots = [(lax.rem(ix + sx - d, sx), core) for d in range(sx)]
    spots = spots + [(at, 1 - core) for at, _ in spots]
    order = jnp.stack([at * 2 + c for at, c in spots] + [iz]).astype(jnp.int32)
    yplace = iy.astype(jnp.int32).reshape(1)

    n1_low, q, kv = project(place, pieces, one, g1, b1, bkv, qb_g)
    kvs = spread_tokens(kv)
    *ctx_parts, ctx, tot = attend(order, q, seg, kvs)
    ctx_parts = to_z(ctx_parts)
    residual, n2_low = out_project(place, ctx_parts, mid, ob, hidden, g2, b2, ff, after=[ub])
    n2_all = spread_tokens(n2_low)
    kept, sent, act, slope = mlp_up(n2_all, weights, ub)
    layer_out, errors, grad_final, grad_mlp = finish(fold_tokens(kept, sent), residual, db, teacher[0], cotangent[0], padding_mask, (2.0 / (count * width)).reshape(1))

    grads = spread_tokens(grad_mlp)
    kept, sent, grad_pre = mlp_back(grads, weights, slope)
    gn2_terms = fold_tokens(kept, sent)
    gw_mlp, up_sums = mlp_weights(grads, act, n2_all, grad_pre)
    gw_sums = [lax.psum_scatter(member, ("y", "z"), scatter_dimension=0, tiled=True) for member in gw_mlp]
    grad_res, *gctx, gw_out, out_sums = out_back(place, gn2_terms, residual, g2, grad_final, ctx_parts, mid, grad_mlp, ff, after=gw_mlp)
    dq, dkv_kept, dkv_sent = attend_back(order, q, to_z(gctx), ctx, tot, seg, kvs)
    dkv_terms = fold_tokens(dkv_kept, dkv_sent)
    grad_joined, gn1, *gn1_parts = join_back(place, dkv_terms, dq, one)
    input_grad = input_back(to_z(gn1_parts), hidden, g1, grad_res)

    up_rows = jnp.zeros((upc, sy * sz, sx * 2, wr), F32)
    up_rows = lax.dynamic_update_slice_in_dim(up_rows, up_sums.reshape(sy * sz, upc, wr).transpose(1, 0, 2)[:, :, None], ix * 2 + core, 2).reshape(upc, width)
    slots = -(-devices // wr)
    error = jnp.sum(errors)
    high = error.astype(BF).astype(F32)
    turn = lax.broadcasted_iota(jnp.int32, (slots, width), 1) % wr
    at = turn + wr * lax.broadcasted_iota(jnp.int32, (slots, width), 0)
    marks = jnp.concatenate([jnp.where(at == device, high, 0.0), jnp.where(turn[:1] == 0, error - high, 0.0)])
    at_zc = jnp.stack([iz, core]).astype(jnp.int32)
    kept, sent = weights_back(at_zc, n1_low, grad_joined, gn1, pieces, out_sums, up_rows, marks, gw_out, wr)
    grid = (sy, sz, sx, wr, kept.shape[-1])
    third = fold(kept.reshape(grid), [shift(sent, "core", 1).reshape(grid)], iy, 0, sy, "fold_core")
    third = fold(third[0], passed(third, "y"), ix, 2, sx, "fold_y")
    third = fold(third[0], passed(third, "x"), iz, 1, sz, "fold_x")
    third = [third[0]] + passed(third, "z")
    grad_w_qkv, sums, gw_out = unpack_one(place, third)
    sums = sums.T
    loss = jnp.sum(sums[16:17 + slots]) / (count * width)

    gw_down = gw_sums[0][:, :width].astype(F32)
    gw_up = gw_sums[-1][:, -ff:]
    gw_up = gw_up.reshape(1, 1, sx, 2, wr, ff)
    up_x = [lax.dynamic_slice_in_dim(gw_up, lax.rem(ix + d, sx), 1, 2) for d in range(sx)]
    gw_up = arrange([up_x[0]] + [shift(up_x[d], "x", d) for d in range(1, sx)], ix, 2)
    gw_up = arrange([lax.dynamic_slice_in_dim(gw_up, core, 1, 3), shift(lax.dynamic_slice_in_dim(gw_up, 1 - core, 1, 3), "core", 1)], core, 3)
    gw_up = gw_up.reshape(sx, 2, wr, sy * sz, ffd).transpose(2, 3, 0, 1, 4).reshape(wr, -1).astype(F32)
    return (
        layer_out[None], loss, input_grad[None], grad_w_qkv, sums[0], sums[1], gw_out, sums[2],
        gw_up, sums[8:8 + upc].reshape(-1), gw_down, sums[3], sums[4], sums[5], sums[6], sums[7],
    )


def solution(mesh):
    seq, ctx = mesh.shape["seq"], mesh.shape["ctx"]
    grid = Mesh(mesh.devices.reshape(seq, ZS, ctx // (2 * ZS), 2), ("y", "z", "x", "core"))
    every = ("y", "z", "x", "core")
    matrix, vector = P(every, None), P(every)
    tokens = P("y", ("z", "x", "core"), None)
    marks = P("y", ("z", "x", "core"))
    return jax.shard_map(
        per_device,
        mesh=grid,
        in_specs=(tokens, matrix, vector, vector, matrix, vector, matrix, vector, matrix, vector, vector, vector, vector, vector, marks, marks, tokens, tokens),
        out_specs=(tokens, P(), tokens, matrix, vector, vector, matrix, vector, matrix, vector, matrix, vector, vector, vector, vector, vector),
        check_vma=False,
    )
```

```python
import functools

import jax
import jax.numpy as jnp
from jax import lax
from jax.experimental import pallas as pl
from jax.experimental.pallas import tpu as pltpu
from jax.sharding import Mesh
from jax.sharding import PartitionSpec as P

HEADS = 12
HEAD_DIM = 64
ZS = 4
BF = jnp.bfloat16
F32 = jnp.float32
NEG = -1e30
LANES = 128


def shift(value, axis, step):
    size = lax.axis_size(axis)
    return lax.ppermute(value, axis, [(a, (a + step) % size) for a in range(size)])


def gather(value, axis, dim, after=()):
    size = lax.axis_size(axis)
    return arrange([value] + [shift(value, axis, d) for d in range(1, size)], lax.axis_index(axis), dim, after)


def scatter_sum(value, axis, dim, last=BF, after=()):
    size = lax.axis_size(axis)
    place = lax.axis_index(axis)

    def cut(d):
        return lax.dynamic_slice_in_dim(value, lax.rem(place + d, size), 1, dim)

    came = [shift(cut(d), axis, d) for d in range(1, size)]

    def body(place_ref, value_ref, *refs):
        index = (slice(None),) * dim + (pl.ds(place_ref[0], 1),)
        total = value_ref[index].astype(F32)
        for ref in refs[:size - 1]:
            total = total + ref[...].astype(F32)
        refs[-1][...] = total.astype(last)

    vmem = pl.BlockSpec(memory_space=pltpu.VMEM)
    return pl.pallas_call(
        body,
        in_specs=[pl.BlockSpec(memory_space=pltpu.SMEM)] + [vmem] * size + [pl.BlockSpec(memory_space=pl.ANY)] * len(after),
        out_shape=jax.ShapeDtypeStruct(came[0].shape, last),
        compiler_params=params(),
        cost_estimate=SMALL,
        name="scatter_sum",
    )(place.astype(jnp.int32).reshape(1), value, *came, *after)


def spread_tokens(value):
    some = [value] + [shift(value, "x", d) for d in range(1, lax.axis_size("x"))]
    return some + [shift(member, "core", 1) for member in some]


def fold_tokens(kept, sent, after=()):
    came = shift(sent, "core", 1)
    size = kept.shape[0]
    shape = kept.shape[1:]

    def body(kept_ref, came_ref, *outs):
        for d in range(size):
            outs[d][...] = (kept_ref[d] + came_ref[d].astype(F32)).astype(outs[d].dtype)

    terms = call(body, (kept, came), [(shape, BF if d else F32) for d in range(size)], "fold_tokens", 0, after)
    return [terms[0]] + [shift(terms[d], "x", -d) for d in range(1, size)]


def dot(a, b):
    return jnp.dot(a, b, preferred_element_type=F32)


def dot_nt(a, b):
    return lax.dot_general(a, b, (((1,), (1,)), ((), ())), preferred_element_type=F32)


def dot_tn(a, b):
    return lax.dot_general(a, b, (((0,), (0,)), ((), ())), preferred_element_type=F32)


SMALL = pl.CostEstimate(flops=1, bytes_accessed=1, transcendentals=0)


def params(mib=6):
    return pltpu.CompilerParams(vmem_limit_bytes=mib * 1024 * 1024)


def pack_one(w_qkv, flat, seg, mask):
    rows, width = w_qkv.shape[0], w_qkv.shape[1] // 3
    group = width // ZS
    hd = HEAD_DIM
    upc = flat.shape[0] - 8

    def body(qkv_ref, flat_ref, seg_ref, mask_ref, one_ref, vec):
        vec[...] = jnp.zeros_like(vec)
        vec[0:8 + upc, 0:rows] = flat_ref[...].astype(F32)
        count = jnp.sum(mask_ref[...].astype(F32), -1, keepdims=True)
        lane = lax.broadcasted_iota(jnp.int32, (LANES, LANES), 1)
        vec[...] = jnp.where(lane == 8 + upc, count, vec[...].T)
        ids = seg_ref[...].astype(F32)
        vec[0:1, hd:] = ids[:, 0:hd]
        vec[1:2, hd:] = ids[:, hd:]
        cols = vec[0:rows, :].astype(BF)
        for g in range(ZS):
            k = width + g * group
            v = 2 * width + g * group
            one_ref[g, :, 0:3 * hd] = qkv_ref[:, k:k + 3 * hd]
            one_ref[g, :, 3 * hd:4 * hd] = qkv_ref[:, v + 2 * hd:v + 3 * hd]
            one_ref[g, :, 4 * hd:6 * hd] = qkv_ref[:, v:v + 2 * hd]
            one_ref[g, :, 6 * hd:9 * hd] = qkv_ref[:, g * group:g * group + 3 * hd]
            one_ref[g, :, 9 * hd:11 * hd] = cols

    outs = [((ZS, rows, 11 * hd), BF)]
    return call(body, (w_qkv, flat, seg, mask), outs, "pack_one", scratch=[pltpu.VMEM((LANES, LANES), F32)])[0]


def pack_up(w_up, w_out, ffd, sx):
    rows, width = w_out.shape
    blocks = w_up.shape[1] // (2 * sx * ffd)
    ff = blocks * ffd

    def body(up_ref, out_ref, to_ref):
        for c in range(2):
            for x in range(sx):
                for b in range(blocks):
                    at = ((b * sx + x) * 2 + c) * ffd
                    to_ref[c, x, :, b * ffd:(b + 1) * ffd] = up_ref[:, at:at + ffd]
                to_ref[c, x, :, ff:] = out_ref[...]

    return call(body, (w_up, w_out), [((2, sx, rows, ff + width), BF)], "pack_up")[0]


def held(value, after):
    def body(value_ref, *rest):
        rest[-1][...] = value_ref[...]

    return pl.pallas_call(
        body,
        in_specs=[pl.BlockSpec(memory_space=pltpu.VMEM)] + [pl.BlockSpec(memory_space=pl.ANY)] * len(after),
        out_shape=jax.ShapeDtypeStruct(value.shape, value.dtype),
        compiler_params=params(),
        cost_estimate=SMALL,
        name="held",
    )(value, *after)


def arrange(pieces, place, dim, after=()):
    size = len(pieces)
    shape = list(pieces[0].shape)
    shape[dim] = size

    def body(place_ref, *refs):
        out = refs[-1]
        for d in range(size):
            spot = lax.rem(place_ref[0] + size - d, size)
            index = (slice(None),) * dim + (pl.ds(spot, 1),)
            out[index] = refs[d][...]

    return pl.pallas_call(
        body,
        in_specs=[pl.BlockSpec(memory_space=pltpu.SMEM)] + [pl.BlockSpec(memory_space=pltpu.VMEM)] * size + [pl.BlockSpec(memory_space=pl.ANY)] * len(after),
        out_shape=jax.ShapeDtypeStruct(tuple(shape), pieces[0].dtype),
        compiler_params=params(),
        cost_estimate=SMALL,
        name="arrange",
    )(place.astype(jnp.int32).reshape(1), *pieces, *after)


def project(place, pieces, one, vectors):
    rows, width = pieces[0].shape
    total = ZS * rows
    hd = HEAD_DIM
    group = 3 * hd

    def body(place_ref, h0, h1, h2, h3, w_ref, vec_ref, n1_ref, q_ref, kv_ref, all_ref):
        qb = jnp.zeros((1, group), F32)
        vb = jnp.zeros((1, group), F32)
        for g in range(ZS):
            here = place_ref[0] == g
            qb = jnp.where(here, vec_ref[0:1, g * group:(g + 1) * group], qb)
            vb = jnp.where(here, vec_ref[1:2, g * group:(g + 1) * group], vb)
        for d, piece in enumerate((h0, h1, h2, h3)):
            spot = pl.ds(pl.multiple_of(lax.rem(place_ref[0] + ZS - d, ZS) * rows, rows), rows)
            all_ref[spot, :] = piece[...]
            normed, _ = norm_parts(piece[...].astype(F32))
            n1 = (normed * vec_ref[4:5, :] + vec_ref[5:6, :]).astype(BF)
            n1_ref[spot, :] = n1
            joined = dot(n1, w_ref[:, 0:9 * hd])
            kv_ref[spot, 0:3 * hd] = joined[:, 0:3 * hd].astype(BF)
            kv_ref[spot, 3 * hd:4 * hd] = (joined[:, 3 * hd:4 * hd] + vb[:, 2 * hd:]).astype(BF)
            kv_ref[spot, 4 * hd:6 * hd] = (joined[:, 4 * hd:6 * hd] + vb[:, 0:2 * hd]).astype(BF)
            q = (joined[:, 6 * hd:9 * hd] + qb).astype(BF).astype(F32) * 0.125
            q_ref[spot, 0:3 * hd] = q.astype(BF)
            q_ref[spot, 3 * hd:4 * hd] = jnp.zeros((rows, hd), BF)

    outs = [((total, width), BF), ((total, 4 * hd), BF), ((total, 6 * hd), BF), ((total, width), BF)]
    return call(body, (place, pieces[0], *pieces[1:], one, vectors), outs, "project", 1)


def fill_keys(kv_refs, keys, rows):
    for j, ref in enumerate(kv_refs):
        for z in range(ZS):
            at = (z * len(kv_refs) + j) * rows
            keys[at:at + rows, :] = ref[z * rows:(z + 1) * rows, :]


def turn_segments(order, seg_ref, turned, count):
    turned[...] = jnp.zeros_like(turned)
    for z in range(ZS):
        for j in range(count):
            turned[z * count + j:z * count + j + 1, :] = seg_ref[pl.ds(z * count + order[j], 1), :]
    queries = jnp.concatenate([turned[z * count:z * count + 1, :] for z in range(ZS)], 1)
    turned[...] = turned[...].T
    return queries


def fill_bias(order, queries, turned, bias, z, count, rows):
    for j in range(count):
        same = turned[:, z * count + j:z * count + j + 1] == queries[:, z * rows:]
        bias[j * rows:(j + 1) * rows, z * rows:] = jnp.where(same, 0.0, NEG)
        key = lax.broadcasted_iota(jnp.int32, (rows, rows), 0) + order[j] * rows
        query = lax.broadcasted_iota(jnp.int32, (rows, rows), 1) + order[0] * rows
        ok = same[:, 0:rows] & (key <= query)
        bias[j * rows:(j + 1) * rows, z * rows:(z + 1) * rows] = jnp.where(ok, 0.0, NEG)


def head_parts(q_ref, keys, z, span, lower_q, lower_k):
    at = slice(z * span, (z + 1) * span)
    k01, kv2, v01 = (keys[at, i * LANES:(i + 1) * LANES] for i in range(3))
    one = jnp.ones_like(k01)
    return (k01, k01, kv2), (jnp.where(lower_k, v01, one), jnp.where(lower_k, one, v01), jnp.where(lower_k, one, kv2))


def attend_kernel(order, q_ref, seg_ref, *rest):
    count = len(rest) - 10
    kv_refs, low_refs, (ctx_ref, tot_ref), (keys, bias, acc, turned) = rest[:count], rest[count:count + 4], rest[count + 4:count + 6], rest[count + 6:]
    total = q_ref.shape[0]
    rows = total // ZS
    span = count * rows
    fill_keys(kv_refs, keys, rows)
    queries = turn_segments(order, seg_ref, turned, count)
    lower_q = lax.broadcasted_iota(jnp.int32, (total, LANES), 1) < HEAD_DIM
    lower_k = lax.broadcasted_iota(jnp.int32, (span, LANES), 1) < HEAD_DIM
    q01, q2 = q_ref[:, 0:LANES], q_ref[:, LANES:2 * LANES]
    none = jnp.zeros_like(q01)
    qs = (jnp.where(lower_q, q01, none), jnp.where(lower_q, none, q01), q2)
    for z in range(ZS):
        fill_bias(order, queries, turned, bias, z, count, rows)
        ks, vs = head_parts(q_ref, keys, z, span, lower_q, lower_k)
        for h in range(3):
            scores = dot_nt(ks[h], qs[h][z * rows:, :]) + bias[:, z * rows:]
            expo = jnp.exp(scores).astype(BF)
            part = dot_tn(vs[h], expo)
            if z == 0:
                acc[h] = part
            else:
                acc[h, :, z * rows:] += part
    u0, u1, u2 = (acc[h].T for h in range(3))
    unnormed = jnp.where(lower_q, u0, u1)
    totals = jnp.where(lower_q, pltpu.roll(u0, HEAD_DIM, 1), pltpu.roll(u1, HEAD_DIM, 1))
    ctx = unnormed / totals
    tot_ref[:, 0:LANES] = totals
    ctx_ref[:, 0:LANES] = ctx
    ctx = pltpu.roll(u2, HEAD_DIM, 1) / u2
    tot_ref[:, LANES:] = u2
    ctx_ref[:, LANES:] = ctx
    for d in range(ZS):
        spot = pl.ds(pl.multiple_of(lax.rem(order[count] + d, ZS) * rows, rows), rows)
        low_refs[d][...] = ctx_ref[spot, 0:3 * HEAD_DIM].astype(BF)


def attend(order, q, seg, kvs, after=()):
    total = q.shape[0]
    span = len(kvs) * total // ZS
    outs = [((total // ZS, 3 * HEAD_DIM), BF)] * ZS + [((total, 2 * LANES), F32)] * 2
    scratch = [pltpu.VMEM((ZS * span, 3 * LANES), BF), pltpu.VMEM((span, total), F32), pltpu.VMEM((3, LANES, total), F32), pltpu.VMEM((LANES, LANES), F32)]
    return call(attend_kernel, (order, q, seg, *kvs), outs, "attend", 1, after, scratch, 20)


def attend_back_kernel(order, q_ref, gc0, gc1, gc2, gc3, ctx_ref, tot_ref, seg_ref, *rest):
    count = len(rest) - 9
    kv_refs, (dq_ref, kept_ref, sent_ref), (keys, bias, ge, acc, gctx_ref, turned) = rest[:count], rest[count:count + 3], rest[count + 3:]
    total = q_ref.shape[0]
    rows = total // ZS
    for d, ref in enumerate((gc0, gc1, gc2, gc3)):
        spot = pl.ds(pl.multiple_of(lax.rem(order[count] + ZS - d, ZS) * rows, rows), rows)
        gctx_ref[spot, :] = ref[...].astype(F32)
    span = count * rows
    fill_keys(kv_refs, keys, rows)
    queries = turn_segments(order, seg_ref, turned, count)
    lane = lax.broadcasted_iota(jnp.int32, (total, LANES), 1)
    lower_q = lane < HEAD_DIM
    lower_k = lax.broadcasted_iota(jnp.int32, (span, LANES), 1) < HEAD_DIM
    q01, q2 = q_ref[:, 0:LANES], q_ref[:, LANES:2 * LANES]
    none = jnp.zeros_like(q01)
    qs = (jnp.where(lower_q, q01, none), jnp.where(lower_q, none, q01), q2)
    gs = []
    g01 = gctx_ref[:, 0:LANES]
    g2 = jnp.concatenate([jnp.zeros((total, HEAD_DIM), F32), gctx_ref[:, LANES:]], 1)
    c2 = pltpu.roll(ctx_ref[:, LANES:], HEAD_DIM, 1)
    t2 = tot_ref[:, LANES:]
    t2 = jnp.where(lower_q, 1.0, pltpu.roll(t2, HEAD_DIM, 1))
    for h in range(3):
        grad = g2 if h == 2 else g01
        tot = t2 if h == 2 else tot_ref[:, 0:LANES]
        ctx = c2 if h == 2 else ctx_ref[:, 0:LANES]
        mine = lower_q if h == 0 else jnp.logical_not(lower_q)
        gu = jnp.where(mine, grad / tot, 0.0).astype(BF)
        gtot = -jnp.sum(jnp.where(mine, grad * ctx / tot, 0.0), -1, keepdims=True)
        high = gtot.astype(BF)
        low = (gtot - high.astype(F32)).astype(BF)
        first = HEAD_DIM if h == 0 else 0
        ge[h] = jnp.where(lane == first, high, jnp.where(lane == first + 1, low, gu))
        gs.append(gu)
    for z in range(ZS):
        fill_bias(order, queries, turned, bias, z, count, rows)
        ks, vs = head_parts(q_ref, keys, z, span, lower_q, lower_k)
        dk, dv = [], []
        for h in range(3):
            qz = qs[h][z * rows:, :]
            expo = jnp.exp(dot_nt(ks[h], qz) + bias[:, z * rows:])
            gprob = dot_nt(vs[h], ge[h, z * rows:, :])
            gscore = (expo * gprob).astype(BF)
            dv.append(dot(expo.astype(BF), gs[h][z * rows:, :]))
            dk.append(dot(gscore, qz))
            part = dot_tn(ks[h], gscore)
            if z == 0:
                acc[h] = part
            else:
                acc[h, :, z * rows:] += part
        parts = (dk[0] + dk[1], dk[2] + dv[2], dv[0] + dv[1])
        for j in range(count):
            to = kept_ref if j < count // 2 else sent_ref
            for i in range(3):
                to[j % (count // 2), z * rows:(z + 1) * rows, i * LANES:(i + 1) * LANES] = parts[i][j * rows:(j + 1) * rows, :].astype(to.dtype)
    upper = lax.broadcasted_iota(jnp.int32, (LANES, total), 0) >= HEAD_DIM
    dq_ref[:, 0:LANES] = (0.125 * jnp.where(upper, acc[1], acc[0])).T.astype(BF)
    dq_ref[:, LANES:] = (0.125 * acc[2]).T[:, 0:HEAD_DIM].astype(BF)


def attend_back(order, q, gctx, ctx, tot, seg, kvs, after=()):
    total = q.shape[0]
    count = len(kvs)
    span = count * total // ZS
    outs = [((total, 3 * HEAD_DIM), BF), ((count // 2, total, 6 * HEAD_DIM), F32), ((count // 2, total, 6 * HEAD_DIM), BF)]
    scratch = [
        pltpu.VMEM((ZS * span, 3 * LANES), BF),
        pltpu.VMEM((span, total), F32),
        pltpu.VMEM((3, total, LANES), BF),
        pltpu.VMEM((3, LANES, total), F32),
        pltpu.VMEM((total, 3 * HEAD_DIM), F32),
        pltpu.VMEM((LANES, LANES), F32),
    ]
    return call(attend_back_kernel, (order, q, *gctx, ctx, tot, seg, *kvs), outs, "attend_back", 1, after, scratch, 24)


def norm_parts(values):
    mean = jnp.mean(values, -1, keepdims=True)
    centered = values - mean
    rstd = lax.rsqrt(jnp.mean(centered * centered, -1, keepdims=True) + 1e-05)
    return centered * rstd, rstd


def norm_back(normed, rstd, grad, gain):
    q = grad * gain
    return rstd * (q - jnp.mean(q, -1, keepdims=True) - normed * jnp.mean(q * normed, -1, keepdims=True))


GC = 0.7978845608028654


class Part:
    def __init__(self, value, first, last):
        self.value, self.first, self.last = value, first, last


def call(body, args, outs, name, smem=0, after=(), scratch=(), mib=12):
    values = [arg.value if isinstance(arg, Part) else arg for arg in args]
    count, waits = len(values), len(after)

    def whole(*refs):
        ins = [ref.at[:, arg.first:arg.last] if isinstance(arg, Part) else ref for arg, ref in zip(args, refs)]
        body(*ins, *refs[count + waits:])

    specs = [pl.BlockSpec(memory_space=pltpu.SMEM if i < smem else pltpu.VMEM) for i in range(count)]
    return pl.pallas_call(
        whole,
        in_specs=specs + [pl.BlockSpec(memory_space=pl.ANY)] * waits,
        out_shape=[jax.ShapeDtypeStruct(*out) for out in outs],
        scratch_shapes=list(scratch),
        compiler_params=params(mib),
        cost_estimate=SMALL,
        name=name,
    )(*values, *after)


def fold_both(kept, came, ix, iy, width):
    sy, sz, sx, wr, wide = kept.shape

    def body(at_ref, kept_ref, came_ref, *outs):
        for d in range(sx):
            x = lax.rem(at_ref[0] + d, sx)
            outs[d][...] = (kept_ref[:, :, pl.ds(x, 1), :, 0:width].astype(F32) + came_ref[:, :, pl.ds(x, 1), :, 0:width].astype(F32)).astype(BF)
        for d in range(sy):
            y = lax.rem(at_ref[1] + d, sy)
            outs[sx + d][...] = (kept_ref[pl.ds(y, 1), :, :, :, width:].astype(F32) + came_ref[pl.ds(y, 1), :, :, :, width:].astype(F32)).astype(BF)

    outs = [((sy, sz, 1, wr, width), BF)] * sx + [((1, sz, sx, wr, wide - width), BF)] * sy
    return call(body, (jnp.stack([ix, iy]).astype(jnp.int32), kept, came), outs, "fold_both", 1)


def fold_cross(first, first_came, second, second_came, ix, iy):
    sx, sy = len(first), len(second)
    sz, wr, width = first[0].shape[1], first[0].shape[3], first[0].shape[4]
    other = second[0].shape[4]

    def body(at_ref, *refs):
        one, two, outs = refs[:sx], refs[sx:sx + sy], refs[sx + sy:]
        for d in range(sy):
            y = lax.rem(at_ref[1] + d, sy)
            total = one[0][pl.ds(y, 1)].astype(F32)
            for ref in one[1:]:
                total = total + ref[pl.ds(y, 1)].astype(F32)
            outs[d][...] = total.astype(BF)
        for d in range(sx):
            x = lax.rem(at_ref[0] + d, sx)
            total = two[0][:, :, pl.ds(x, 1)].astype(F32)
            for ref in two[1:]:
                total = total + ref[:, :, pl.ds(x, 1)].astype(F32)
            outs[sy + d][...] = total.astype(BF)

    outs = [((1, sz, 1, wr, width), BF)] * sy + [((1, sz, 1, wr, other), BF)] * sx
    args = (jnp.stack([ix, iy]).astype(jnp.int32), first[0], *first_came, second[0], *second_came)
    return call(body, args, outs, "fold_cross", 1)


def fold_last(first, first_came, second, second_came, iz, after):
    sy, sx = len(first), len(second)
    wr, width = first[0].shape[3:]
    wide = width + second[0].shape[4]

    def body(at_ref, *refs):
        one, two, outs = refs[:sy], refs[sy:sy + sx], refs[sy + sx:]
        for d in range(ZS):
            z = lax.rem(at_ref[0] + d, ZS)
            for sums, cols in ((one, slice(0, width)), (two, slice(width, wide))):
                total = sums[0][:, pl.ds(z, 1)].astype(F32)
                for ref in sums[1:]:
                    total = total + ref[:, pl.ds(z, 1)].astype(F32)
                outs[d][:, :, :, :, cols] = total.astype(BF)

    outs = [((1, 1, 1, wr, wide), BF)] * ZS
    args = (iz.astype(jnp.int32).reshape(1), first[0], *first_came, second[0], *second_came)
    return call(body, args, outs, "fold_last", 1, after)


def passed(pieces, axis):
    return [shift(pieces[d], axis, d) for d in range(1, len(pieces))]


def out_project(place, pieces, mid, ff, hidden, vectors, after):
    rows, group = pieces[0].shape
    width = hidden.shape[1]

    def body(place_ref, p0, p1, p2, p3, w_ref, hidden_ref, vec_ref, res_ref, n2_ref, cat_ref):
        total = hidden_ref[...].astype(F32) + vec_ref[2:3, :]
        for d, piece in enumerate((p0, p1, p2, p3)):
            spot = pl.ds(pl.multiple_of(lax.rem(place_ref[0] + ZS - d, ZS) * group, group), group)
            total = total + dot(piece[...], w_ref[spot, :])
            cat_ref[:, d * group:(d + 1) * group] = piece[...]
        res_ref[:, 0:width] = total
        res_ref[:, width:] = jnp.broadcast_to(vec_ref[15:16, 0:rows], (LANES, rows)).T
        n2, _ = norm_parts(total)
        n2_ref[...] = (n2 * vec_ref[6:7, :] + vec_ref[7:8, :]).astype(BF)

    outs = [((rows, width + LANES), F32), ((rows, width), BF), ((rows, width), BF)]
    args = (place, *pieces, Part(mid, ff, ff + width), hidden, vectors)
    return call(body, args, outs, "out_project", 1, after)


def mlp_parts(weights, ff):
    width = weights[0].shape[0]
    if len(weights) == 2:
        return Part(weights[0], 0, ff), weights[1]
    return Part(weights[0], 0, ff), Part(weights[0], ff + width, ff + 2 * width)


def mlp_up(blocks, weights, bias, ff):
    rows, width = blocks[0].shape
    count = len(blocks)
    half = count // 2

    def body(*refs):
        n2_refs, (bias_ref, up_ref, down_ref), (kept_ref, sent_ref, act_ref, slope_ref, n2_all) = refs[:count], refs[count:count + 3], refs[-5:]
        for j in range(count):
            n2_all[j * rows:(j + 1) * rows, :] = n2_refs[j][...]
            pre = dot(n2_refs[j][...], up_ref[...]) + bias_ref[0:1, 0:ff]
            square = pre * pre
            tanh = jnp.tanh(GC * pre * (1.0 + 0.044715 * square))
            half_one = 0.5 * (1.0 + tanh)
            act = (pre * half_one).astype(BF)
            slope_ref[j] = (half_one + 0.5 * pre * (1.0 - tanh * tanh) * (GC + GC * 0.134145 * square)).astype(BF)
            act_ref[j * rows:(j + 1) * rows, :] = act
            part = dot(act, down_ref[...])
            if j < half:
                kept_ref[j] = part + bias_ref[1:2, 0:width] if j == 0 else part
            else:
                sent_ref[j - half] = part.astype(BF)

    outs = [((half, rows, width), F32), ((half, rows, width), BF), ((count * rows, ff), BF), ((count, rows, ff), BF), ((count * rows, width), BF)]
    return call(body, (*blocks, bias, *mlp_parts(weights, ff)), outs, "mlp_up")


def finish(terms, residual, targets, scale):
    rows, width = targets.shape[1:]
    size = len(terms)

    def body(scale_ref, *refs):
        res_ref, target_ref, out_ref, err_ref, both_ref, gmlp_ref = refs[size:]
        valid = res_ref[:, width:width + 1]
        final = res_ref[:, 0:width]
        for ref in refs[:size]:
            final = final + ref[...].astype(F32)
        out_ref[...] = final.astype(BF)
        deviation = final - target_ref[0].astype(F32)
        grad = valid * (target_ref[1].astype(F32) + deviation * scale_ref[0])
        both_ref[0] = res_ref[:, 0:width]
        both_ref[1] = grad
        low = grad.astype(BF)
        gmlp_ref[...] = low
        err_ref[0:1, :] = jnp.sum(valid * deviation * deviation, 0, keepdims=True)
        err_ref[1:2, :] = jnp.sum(low.astype(F32), 0, keepdims=True)

    outs = [((rows, width), BF), ((2, width), F32), ((2, rows, width), F32), ((rows, width), BF)]
    return call(body, (scale, *terms, residual, targets), outs, "finish", 1)


def mlp_back(grads, weights, slope):
    rows, width = grads[0].shape
    count = len(grads)
    half = count // 2
    ff = slope.shape[2]

    def body(*refs):
        g_refs, (slope_ref, up_ref, down_ref), (kept_ref, sent_ref, gpre_ref, g_all) = refs[:count], refs[count:count + 3], refs[-4:]
        for j in range(count):
            g_all[j * rows:(j + 1) * rows, :] = g_refs[j][...]
            gpre = (dot_nt(g_refs[j][...], down_ref[...]) * slope_ref[j].astype(F32)).astype(BF)
            gpre_ref[j * rows:(j + 1) * rows, :] = gpre
            part = dot_nt(gpre, up_ref[...])
            if j < half:
                kept_ref[j] = part
            else:
                sent_ref[j - half] = part.astype(BF)

    outs = [((half, rows, width), F32), ((half, rows, width), BF), ((count * rows, ff), BF), ((count * rows, width), BF)]
    return call(body, (*grads, slope, *mlp_parts(weights, ff)), outs, "mlp_back")


def mlp_weights(grads, act, n2, gpre, after):
    width = grads.shape[1]
    ff = act.shape[1]

    def body(g_ref, act_ref, n2_ref, gpre_ref, *outs):
        down_ref, up_ref = (outs[0].at[:, 0:width], outs[0].at[:, width:]) if ff == width else outs[:2]
        down_ref[...] = dot_tn(act_ref[...], g_ref[...]).astype(BF)
        up_ref[...] = dot_tn(n2_ref[...], gpre_ref[...]).astype(BF)
        outs[-1][...] = jnp.sum(gpre_ref[...].astype(F32), 0, keepdims=True)

    outs = [((width, 2 * width), BF)] if ff == width else [((ff, width), BF), ((width, ff), BF)]
    *grads, sums = call(body, (grads, act, n2, gpre), outs + [((1, ff), F32)], "mlp_weights", after=after)
    return grads, sums


def out_back(place, terms, res_and_grad, vectors, ctx_cat, mid, ff, after):
    rows, width = res_and_grad.shape[1:]
    group = width // ZS
    size = len(terms)

    def body(place_ref, *refs):
        (both_ref, vec_ref, cat_ref, w_ref, gres_ref), gctx_refs, (gw_ref, sums_ref) = refs[size:size + 5], refs[size + 5:size + 9], refs[size + 9:]
        gn2 = refs[0][...]
        for ref in refs[1:size]:
            gn2 = gn2 + ref[...].astype(F32)
        n2, rstd = norm_parts(both_ref[0])
        gres = both_ref[1] + norm_back(n2, rstd, gn2, vec_ref[6:7, :])
        gres_ref[...] = gres
        branch = gres.astype(BF)
        for d in range(ZS):
            spot = pl.ds(pl.multiple_of(lax.rem(place_ref[0] + d, ZS) * group, group), group)
            gctx_refs[d][...] = dot_nt(branch, w_ref[spot, :]).astype(BF)
        for d in range(ZS):
            spot = pl.ds(pl.multiple_of(lax.rem(place_ref[0] + ZS - d, ZS) * group, group), group)
            gw_ref[spot, :] = dot_tn(cat_ref[:, d * group:(d + 1) * group], branch).astype(BF)
        rowsum = lambda v: jnp.sum(v, 0, keepdims=True)
        sums_ref[0:1, :] = rowsum(branch.astype(F32))
        sums_ref[1:2, :] = rowsum(gn2 * n2)
        sums_ref[2:3, :] = rowsum(gn2)

    outs = [((rows, width), F32)] + [((rows, group), BF)] * ZS + [((width, width), BF), ((3, width), F32)]
    args = (place, *terms, res_and_grad, vectors, ctx_cat, Part(mid, ff, ff + width))
    return call(body, args, outs, "out_back", 1, after)


def join_back(place, terms, dq, one):
    total, group = dq.shape
    width = one.shape[0]
    rows = total // ZS
    size = len(terms)
    cols = 3 * group

    def body(place_ref, *refs):
        dq_ref, w_ref, gj_ref, gn1_ref = refs[size:size + 4]
        out_refs = refs[size + 4:]
        dkv = refs[0][...]
        for ref in refs[1:size]:
            dkv = dkv + ref[...].astype(F32)
        gj_ref[:, 0:2 * group] = dkv.astype(BF)
        gj_ref[:, 2 * group:] = dq_ref[...]
        gn1_ref[...] = dot_nt(gj_ref[...], w_ref[:, 0:cols])
        for d in range(ZS):
            spot = pl.ds(pl.multiple_of(lax.rem(place_ref[0] + d, ZS) * rows, rows), rows)
            out_refs[d][...] = gn1_ref[spot, :].astype(out_refs[d].dtype)

    outs = [((total, cols), BF), ((total, width), F32), ((rows, width), F32)] + [((rows, width), BF)] * (ZS - 1)
    return call(body, (place, *terms, dq, one), outs, "join_back", 1)


def weights_back(place, n1, grad_joined, gn1, hidden, out_sums, fin_sums, up_rows, gw_out, wr, devices):
    total, cols = grad_joined.shape
    width = n1.shape[1]
    rows = total // ZS
    group = cols // 3
    upc = up_rows.shape[0]
    chips = width // (2 * wr)
    wide = width + cols + HEAD_DIM + LANES
    slots = -(-devices // wr)

    def body(place_ref, n1_ref, gj_ref, gn1_ref, hidden_ref, sums_ref, fin_ref, up_ref, gw_ref, kept_ref, sent_ref, vec, full):
        gain_sum = jnp.zeros((1, width), F32)
        for z in range(ZS):
            spot = slice(z * rows, (z + 1) * rows)
            normed, _ = norm_parts(hidden_ref[spot, :].astype(F32))
            gain_sum = gain_sum + jnp.sum(gn1_ref[spot, :] * normed, 0, keepdims=True)
        joined_sums = jnp.sum(gj_ref[...].astype(F32), 0, keepdims=True)
        vec[...] = jnp.zeros_like(vec)
        hd = HEAD_DIM
        for g in range(ZS):
            here = place_ref[0] == g
            at = g * group
            vec[0:1, at:at + group] = jnp.where(here, joined_sums[:, 2 * group:], 0.0)
            vec[1:2, at:at + 2 * hd] = jnp.where(here, joined_sums[:, 4 * hd:6 * hd], 0.0)
            vec[1:2, at + 2 * hd:at + 3 * hd] = jnp.where(here, joined_sums[:, 3 * hd:4 * hd], 0.0)
        vec[2:3, :] = sums_ref[0:1, :]
        vec[3:4, :] = fin_ref[1:2, :]
        vec[4:5, :] = gain_sum
        vec[5:6, :] = jnp.sum(gn1_ref[...], 0, keepdims=True)
        vec[6:8, :] = sums_ref[1:3, :]
        vec[8:8 + upc, :] = up_ref[...]
        error = jnp.sum(fin_ref[0:1, :], -1, keepdims=True)
        high = error.astype(BF).astype(F32)
        turn = lax.rem(lax.broadcasted_iota(jnp.int32, (1, width), 1), wr)
        for s in range(slots):
            vec[16 + s:17 + s, :] = jnp.where(turn + s * wr == place_ref[2], high, 0.0)
        vec[16 + slots:17 + slots, :] = jnp.where(turn == 0, error - high, 0.0)
        full[:, 0:width] = gw_ref[...].astype(F32)
        full[:, width:width + cols] = dot_tn(n1_ref[...], gj_ref[...])
        full[:, width + cols:width + cols + hd] = jnp.zeros((width, hd), F32)
        full[:, width + cols + hd:] = vec[...].T
        for c in range(2):
            @pl.when(place_ref[1] == c)
            def _():
                for chip in range(chips):
                    at = chip * 2 * wr
                    kept_ref[chip] = full[at + c * wr:at + (c + 1) * wr, :].astype(BF)
                    sent_ref[chip] = full[at + (1 - c) * wr:at + (2 - c) * wr, :].astype(BF)

    outs = [((chips, wr, wide), BF)] * 2
    scratch = [pltpu.VMEM((LANES, width), F32), pltpu.VMEM((width, wide), F32)]
    return call(body, (place, n1, grad_joined, gn1, hidden, out_sums, fin_sums, up_rows, gw_out), outs, "weights_back", 1, scratch=scratch, mib=20)


def input_back(terms, hidden, vectors, grad_res):
    rows, width = hidden.shape

    def body(t0, t1, t2, t3, hidden_ref, gain_ref, gres_ref, out_ref, done_ref):
        back = t0[...] + t1[...].astype(F32) + t2[...].astype(F32) + t3[...].astype(F32)
        normed, rstd = norm_parts(hidden_ref[...].astype(F32))
        out_ref[...] = gres_ref[...] + norm_back(normed, rstd, back, gain_ref[4:5, :])
        done_ref[...] = jnp.zeros_like(done_ref)

    return call(body, (terms[0], *terms[1:], hidden, vectors, grad_res), [((rows, width), F32), ((8, LANES), F32)], "input_back")


def unpack_one(place, pieces, after):
    rows, wide = pieces[0].shape[-2:]
    hd = HEAD_DIM
    group = 3 * hd
    width = ZS * group

    def body(place_ref, p0, p1, p2, p3, qkv_ref, vec_ref, out_ref, held_ref):
        for d, piece in enumerate((p0, p1, p2, p3)):
            held_ref[pl.ds(lax.rem(place_ref[0] + ZS - d, ZS), 1)] = piece[...].reshape(1, rows, wide).astype(F32)
        vec_total = jnp.zeros((rows, LANES), F32)
        out_total = jnp.zeros((rows, width), F32)
        for g in range(ZS):
            k = width + g * group
            v = 2 * width + g * group
            at = width
            qkv_ref[:, k:k + 3 * hd] = held_ref[g, :, at:at + 3 * hd]
            qkv_ref[:, v + 2 * hd:v + 3 * hd] = held_ref[g, :, at + 3 * hd:at + 4 * hd]
            qkv_ref[:, v:v + 2 * hd] = held_ref[g, :, at + 4 * hd:at + 6 * hd]
            qkv_ref[:, g * group:g * group + 3 * hd] = held_ref[g, :, at + 6 * hd:at + 9 * hd]
            vec_total = vec_total + held_ref[g, :, at + 10 * hd:]
            out_total = out_total + held_ref[g, :, 0:width]
        vec_ref[...] = vec_total
        out_ref[...] = out_total

    outs = [((rows, 3 * width), F32), ((rows, LANES), F32), ((rows, width), F32)]
    return call(body, (place, *pieces), outs, "unpack_one", 1, after, scratch=[pltpu.VMEM((ZS, rows, wide), F32)])


def per_device(hidden_in, w_qkv, q_bias, v_bias, w_out, out_bias, w_up, up_bias, w_down, down_bias, ln1_gain, ln1_bias, ln2_gain, ln2_bias, segment_ids, padding_mask, teacher, cotangent):
    sy, sz, sx = (lax.axis_size(a) for a in ("y", "z", "x"))
    iy, iz, ix, core = (lax.axis_index(a) for a in ("y", "z", "x", "core"))
    device = ((iy * sz + iz) * sx + ix) * 2 + core
    devices = sy * sz * sx * 2
    rows, width = hidden_in.shape[1:]
    wr = w_qkv.shape[0]
    ffd = w_down.shape[0]
    ff = sy * sz * ffd
    upc = ffd // wr
    wcols = 9 * HEAD_DIM
    group = width // sz
    place = iz.astype(jnp.int32).reshape(1)

    def from_z(value):
        return [value] + [shift(value, "z", d) for d in range(1, sz)]

    def to_z(pieces):
        return [pieces[0]] + [shift(pieces[d], "z", d) for d in range(1, sz)]

    def cut_z(value):
        return [lax.dynamic_slice_in_dim(value, lax.rem(iz + d, sz), 1, 0) for d in range(sz)]

    flat = jnp.concatenate([jnp.stack([q_bias, v_bias, out_bias, down_bias, ln1_gain, ln1_bias, ln2_gain, ln2_bias]), up_bias.reshape(upc, wr)])
    hidden = hidden_in[0]
    pieces = from_z(hidden)
    targets = jnp.concatenate([teacher, cotangent], 0)
    one = arrange(to_z(cut_z(pack_one(w_qkv, flat, segment_ids, padding_mask))), iz, 0)
    one = gather(one[None, :, None], "x", 2)
    one = gather(one, "y", 0)[:, :, :, None]
    one = gather(one, "core", 3).reshape(width, -1)

    up = pack_up(w_up, w_out, ffd, sx)
    up = arrange([lax.dynamic_slice_in_dim(up, core, 1, 0), shift(lax.dynamic_slice_in_dim(up, 1 - core, 1, 0), "core", 1)], core, 0)
    up_x = [lax.dynamic_slice_in_dim(up, lax.rem(ix + d, sx), 1, 1) for d in range(sx)]
    up = arrange([up_x[0]] + [shift(up_x[d], "x", d) for d in range(1, sx)], ix, 1)
    weights = [up.transpose(1, 0, 2, 3).reshape(2 * sx * wr, ff + width), w_down]
    if ff == width:
        weights = [jnp.concatenate(weights, 1)]
    weights = [lax.all_gather(member, ("y", "z"), axis=0, tiled=True) for member in weights]

    vec = one[:, wcols:]
    vectors = jnp.concatenate([vec[:, :15].T.astype(F32), jnp.pad(padding_mask.astype(F32), ((0, 0), (0, width - rows)))])
    ub = vectors[8:8 + upc].reshape(upc, sy * sz, sx * 2, wr)
    ub = lax.dynamic_index_in_dim(ub, ix * 2 + core, 2, keepdims=False).transpose(1, 0, 2).reshape(1, ff)
    wide = max(ff, width)
    biases = jnp.concatenate([jnp.pad(ub, ((0, 0), (0, wide - ff))), jnp.pad(vectors[3:4], ((0, 0), (0, wide - width)))])
    count = jnp.sum(vectors[8 + upc]) / wr
    seg = lax.dynamic_index_in_dim(vec.reshape(sy, sz * sx * 2, wr, LANES), iy, 0, keepdims=False)[:, :2, HEAD_DIM:].astype(F32).reshape(sz * sx * 2, rows)
    spots = [(lax.rem(ix + sx - d, sx), core) for d in range(sx)]
    spots = spots + [(at, 1 - core) for at, _ in spots]
    order = jnp.stack([at * 2 + c for at, c in spots] + [iz]).astype(jnp.int32)

    n1_low, q, kv, hidden_all = project(place, pieces, one, vectors)
    kvs = spread_tokens(kv)
    *ctx_parts, ctx, tot = attend(order, q, seg, kvs)
    residual, n2_low, ctx_cat = out_project(place, to_z(ctx_parts), weights[0], ff, hidden, vectors, after=[biases])
    kept, sent, act, slope, n2_all = mlp_up(spread_tokens(n2_low), weights, biases, ff)
    layer_out, fin_sums, res_and_grad, grad_mlp = finish(fold_tokens(kept, sent), residual, targets, (2.0 / (count * width)).reshape(1))

    kept, sent, grad_pre, grads = mlp_back(spread_tokens(grad_mlp), weights, slope)
    gn2_terms = fold_tokens(kept, sent)
    gw_mlp, up_sums = mlp_weights(grads, act, n2_all, grad_pre, after=gn2_terms[:1])
    gw_sums = [lax.psum_scatter(member, ("y", "z"), scatter_dimension=0, tiled=True) for member in gw_mlp]
    grad_res, *gctx, gw_out, out_sums = out_back(place, gn2_terms, res_and_grad, vectors, ctx_cat, weights[0], ff, after=[up_sums])
    dq, dkv_kept, dkv_sent = attend_back(order, q, to_z(gctx), ctx, tot, seg, kvs)
    grad_joined, gn1, *gn1_parts = join_back(place, fold_tokens(dkv_kept, dkv_sent), dq, one)
    input_grad, back_done = input_back(to_z(gn1_parts), hidden, vectors, grad_res)

    up_rows = jnp.zeros((upc, sy * sz, sx * 2, wr), F32)
    up_rows = lax.dynamic_update_slice_in_dim(up_rows, up_sums.reshape(sy * sz, upc, wr).transpose(1, 0, 2)[:, :, None], ix * 2 + core, 2).reshape(upc, width)
    places = jnp.stack([iz, core, device]).astype(jnp.int32)
    kept, sent = weights_back(places, n1_low, grad_joined, gn1, hidden_all, out_sums, fin_sums, up_rows, gw_out, wr, devices)
    third = fold_both(kept.reshape(sy, sz, sx, wr, -1), shift(sent, "core", 1).reshape(sy, sz, sx, wr, -1), ix, iy, width)
    third = fold_cross(third[:sx], passed(third[:sx], "x"), third[sx:], passed(third[sx:], "y"), ix, iy)
    third = fold_last(third[:sy], passed(third[:sy], "y"), third[sy:], passed(third[sy:], "x"), iz, after=[back_done])
    ready = third[0][0, 0, 0, :, :LANES]
    gw_sums = [held(member, [ready]) for member in gw_sums]
    third = [third[0]] + passed(third, "z")

    gw_down = gw_sums[0][:, :width].astype(F32)
    gw_up = gw_sums[-1][:, -ff:].reshape(1, 1, sx, 2, wr, ff)
    up_x = [lax.dynamic_slice_in_dim(gw_up, lax.rem(ix + d, sx), 1, 2) for d in range(sx)]
    gw_up = arrange([up_x[0]] + [shift(up_x[d], "x", d) for d in range(1, sx)], ix, 2)
    gw_up = arrange([lax.dynamic_slice_in_dim(gw_up, core, 1, 3), shift(lax.dynamic_slice_in_dim(gw_up, 1 - core, 1, 3), "core", 1)], core, 3)
    gw_up = gw_up.reshape(sx, 2, wr, sy * sz, ffd).transpose(2, 3, 0, 1, 4).reshape(wr, -1).astype(F32)

    grad_w_qkv, sums, gw_out = unpack_one(place, third, after=[gw_up])
    sums = sums.T
    loss = jnp.sum(sums[16:17 + -(-devices // wr)]) / (count * width)
    return (
        layer_out[None], loss, input_grad[None], grad_w_qkv, sums[0], sums[1], gw_out, sums[2],
        gw_up, sums[8:8 + upc].reshape(-1), gw_down, sums[3], sums[4], sums[5], sums[6], sums[7],
    )


def solution(mesh):
    seq, ctx = mesh.shape["seq"], mesh.shape["ctx"]
    grid = Mesh(mesh.devices.reshape(seq, ZS, ctx // (2 * ZS), 2), ("y", "z", "x", "core"))
    every = ("y", "z", "x", "core")
    matrix, vector = P(every, None), P(every)
    tokens = P("y", ("z", "x", "core"), None)
    marks = P("y", ("z", "x", "core"))
    return jax.shard_map(
        per_device,
        mesh=grid,
        in_specs=(tokens, matrix, vector, vector, matrix, vector, matrix, vector, matrix, vector, vector, vector, vector, vector, marks, marks, tokens, tokens),
        out_specs=(tokens, P(), tokens, matrix, vector, vector, matrix, vector, matrix, vector, matrix, vector, vector, vector, vector, vector),
        check_vma=False,
    )
```

```python
import functools

import jax
import jax.numpy as jnp
from jax import lax
from jax.experimental import pallas as pl
from jax.experimental.pallas import tpu as pltpu
from jax.sharding import Mesh
from jax.sharding import PartitionSpec as P

HEADS = 12
HEAD_DIM = 64
ZS = 4
BF = jnp.bfloat16
F32 = jnp.float32
NEG = -1e30
LANES = 128


def shift(value, axis, step):
    size = lax.axis_size(axis)
    return lax.ppermute(value, axis, [(a, (a + step) % size) for a in range(size)])


def gather(value, axis, dim, after=()):
    size = lax.axis_size(axis)
    return arrange([value] + [shift(value, axis, d) for d in range(1, size)], lax.axis_index(axis), dim, after)


def scatter_sum(value, axis, dim, last=BF, after=()):
    size = lax.axis_size(axis)
    place = lax.axis_index(axis)

    def cut(d):
        return lax.dynamic_slice_in_dim(value, lax.rem(place + d, size), 1, dim)

    came = [shift(cut(d), axis, d) for d in range(1, size)]

    def body(place_ref, value_ref, *refs):
        index = (slice(None),) * dim + (pl.ds(place_ref[0], 1),)
        total = value_ref[index].astype(F32)
        for ref in refs[:size - 1]:
            total = total + ref[...].astype(F32)
        refs[-1][...] = total.astype(last)

    vmem = pl.BlockSpec(memory_space=pltpu.VMEM)
    return pl.pallas_call(
        body,
        in_specs=[pl.BlockSpec(memory_space=pltpu.SMEM)] + [vmem] * size + [pl.BlockSpec(memory_space=pl.ANY)] * len(after),
        out_shape=jax.ShapeDtypeStruct(came[0].shape, last),
        compiler_params=params(),
        cost_estimate=SMALL,
        name="scatter_sum",
    )(place.astype(jnp.int32).reshape(1), value, *came, *after)


def spread_tokens(value):
    some = [value] + [shift(value, "x", d) for d in range(1, lax.axis_size("x"))]
    return some + [shift(member, "core", 1) for member in some]


def fold_tokens(kept, sent, after=()):
    came = shift(sent, "core", 1)
    size = kept.shape[0]
    shape = kept.shape[1:]

    def body(kept_ref, came_ref, *outs):
        for d in range(size):
            outs[d][...] = (kept_ref[d] + came_ref[d].astype(F32)).astype(outs[d].dtype)

    terms = call(body, (kept, came), [(shape, BF if d else F32) for d in range(size)], "fold_tokens", 0, after)
    return [terms[0]] + [shift(terms[d], "x", -d) for d in range(1, size)]


def dot(a, b):
    return jnp.dot(a, b, preferred_element_type=F32)


def dot_nt(a, b):
    return lax.dot_general(a, b, (((1,), (1,)), ((), ())), preferred_element_type=F32)


def dot_tn(a, b):
    return lax.dot_general(a, b, (((0,), (0,)), ((), ())), preferred_element_type=F32)


SMALL = pl.CostEstimate(flops=1, bytes_accessed=1, transcendentals=0)


def params(mib=6):
    return pltpu.CompilerParams(vmem_limit_bytes=mib * 1024 * 1024)


def pack_one(w_qkv, flat, seg, mask):
    rows, width = w_qkv.shape[0], w_qkv.shape[1] // 3
    group = width // ZS
    hd = HEAD_DIM
    upc = flat.shape[0] - 8

    def body(qkv_ref, flat_ref, seg_ref, mask_ref, one_ref, vec):
        vec[...] = jnp.zeros_like(vec)
        vec[0:8 + upc, 0:rows] = flat_ref[...].astype(F32)
        count = jnp.sum(mask_ref[...].astype(F32), -1, keepdims=True)
        lane = lax.broadcasted_iota(jnp.int32, (LANES, LANES), 1)
        vec[...] = jnp.where(lane == 8 + upc, count, vec[...].T)
        ids = seg_ref[...].astype(F32)
        vec[0:1, hd:] = ids[:, 0:hd]
        vec[1:2, hd:] = ids[:, hd:]
        cols = vec[0:rows, :].astype(BF)
        for g in range(ZS):
            k = width + g * group
            v = 2 * width + g * group
            one_ref[g, :, 0:3 * hd] = qkv_ref[:, k:k + 3 * hd]
            one_ref[g, :, 3 * hd:4 * hd] = qkv_ref[:, v + 2 * hd:v + 3 * hd]
            one_ref[g, :, 4 * hd:6 * hd] = qkv_ref[:, v:v + 2 * hd]
            one_ref[g, :, 6 * hd:9 * hd] = qkv_ref[:, g * group:g * group + 3 * hd]
            one_ref[g, :, 9 * hd:11 * hd] = cols

    outs = [((ZS, rows, 11 * hd), BF)]
    return call(body, (w_qkv, flat, seg, mask), outs, "pack_one", scratch=[pltpu.VMEM((LANES, LANES), F32)])[0]


def pack_up(place, w_up, w_out, ffd, sx):
    rows, width = w_out.shape
    half = width // 2
    blocks = w_up.shape[1] // (2 * sx * ffd)
    ff = blocks * ffd

    def body(at_ref, up_ref, out_ref, *refs):
        outs, every = refs[:-1], refs[-1]
        for c in range(2):
            for x in range(sx):
                for b in range(blocks):
                    at = ((b * sx + x) * 2 + c) * ffd
                    every[c * sx + x, :, b * ffd:(b + 1) * ffd] = up_ref[:, at:at + ffd]
                every[c * sx + x, :, ff:] = out_ref[:, c * half:(c + 1) * half]
        for dc in range(2):
            core = at_ref[1] if dc == 0 else 1 - at_ref[1]
            for dx in range(sx):
                outs[dc * sx + dx][...] = every[core * sx + lax.rem(at_ref[0] + dx, sx)]

    outs = [((rows, ff + half), BF)] * (2 * sx)
    return call(body, (place, w_up, w_out), outs, "pack_up", 1, scratch=[pltpu.VMEM((2 * sx, rows, ff + half), BF)])


def join_up(place, pieces, w_down):
    sx = len(pieces) // 2
    rows, cols = pieces[0].shape
    joined = w_down.shape[0] == 2 * sx * rows
    wide = cols + w_down.shape[1] if joined else cols

    def body(at_ref, *refs):
        out = refs[-1]
        for dc in range(2):
            core = at_ref[1] if dc == 0 else 1 - at_ref[1]
            for dx in range(sx):
                spot = lax.rem(at_ref[0] + sx - dx, sx) * 2 + core
                out[pl.ds(spot, 1), :, 0:cols] = refs[dc * sx + dx][...].reshape(1, rows, cols)
        if joined:
            out[:, :, cols:] = refs[2 * sx][...]

    args = (place, *pieces, w_down.reshape(2 * sx, rows, -1)) if joined else (place, *pieces)
    return call(body, args, [((2 * sx, rows, wide), BF)], "join_up", 1)[0].reshape(2 * sx * rows, wide)


def held(value, after):
    def body(value_ref, out_ref):
        out_ref[...] = value_ref[...]

    array = value.value if isinstance(value, Part) else value
    shape = (array.shape[0], value.last - value.first) if isinstance(value, Part) else array.shape
    return call(body, (value,), [(shape, array.dtype)], "held", 0, after)[0]


def arrange(pieces, place, dim, after=()):
    size = len(pieces)
    shape = list(pieces[0].shape)
    shape[dim] = size

    def body(place_ref, *refs):
        out = refs[-1]
        for d in range(size):
            spot = lax.rem(place_ref[0] + size - d, size)
            index = (slice(None),) * dim + (pl.ds(spot, 1),)
            out[index] = refs[d][...]

    return pl.pallas_call(
        body,
        in_specs=[pl.BlockSpec(memory_space=pltpu.SMEM)] + [pl.BlockSpec(memory_space=pltpu.VMEM)] * size + [pl.BlockSpec(memory_space=pl.ANY)] * len(after),
        out_shape=jax.ShapeDtypeStruct(tuple(shape), pieces[0].dtype),
        compiler_params=params(),
        cost_estimate=SMALL,
        name="arrange",
    )(place.astype(jnp.int32).reshape(1), *pieces, *after)


def project(place, pieces, one, vectors):
    rows, width = pieces[0].shape
    total = ZS * rows
    hd = HEAD_DIM
    group = 3 * hd

    def body(place_ref, h0, h1, h2, h3, w_ref, vec_ref, n1_ref, q_ref, kv_ref, all_ref):
        qb = jnp.zeros((1, group), F32)
        vb = jnp.zeros((1, group), F32)
        for g in range(ZS):
            here = place_ref[0] == g
            qb = jnp.where(here, vec_ref[0:1, g * group:(g + 1) * group], qb)
            vb = jnp.where(here, vec_ref[1:2, g * group:(g + 1) * group], vb)
        for d, piece in enumerate((h0, h1, h2, h3)):
            spot = pl.ds(pl.multiple_of(lax.rem(place_ref[0] + ZS - d, ZS) * rows, rows), rows)
            all_ref[spot, :] = piece[...]
            normed, _ = norm_parts(piece[...].astype(F32))
            n1 = (normed * vec_ref[4:5, :] + vec_ref[5:6, :]).astype(BF)
            n1_ref[spot, :] = n1
            joined = dot(n1, w_ref[:, 0:9 * hd])
            kv_ref[spot, 0:3 * hd] = joined[:, 0:3 * hd].astype(BF)
            kv_ref[spot, 3 * hd:4 * hd] = (joined[:, 3 * hd:4 * hd] + vb[:, 2 * hd:]).astype(BF)
            kv_ref[spot, 4 * hd:6 * hd] = (joined[:, 4 * hd:6 * hd] + vb[:, 0:2 * hd]).astype(BF)
            q = (joined[:, 6 * hd:9 * hd] + qb).astype(BF).astype(F32) * 0.125
            q_ref[spot, 0:3 * hd] = q.astype(BF)
            q_ref[spot, 3 * hd:4 * hd] = jnp.zeros((rows, hd), BF)

    outs = [((total, width), BF), ((total, 4 * hd), BF), ((total, 6 * hd), BF), ((total, width), BF)]
    return call(body, (place, pieces[0], *pieces[1:], one, vectors), outs, "project", 1)


def fill_keys(kv_refs, keys, rows):
    for j, ref in enumerate(kv_refs):
        for z in range(ZS):
            at = (z * len(kv_refs) + j) * rows
            keys[at:at + rows, :] = ref[z * rows:(z + 1) * rows, :]


def turn_segments(order, seg_ref, turned, count):
    turned[...] = jnp.zeros_like(turned)
    for z in range(ZS):
        for j in range(count):
            turned[z * count + j:z * count + j + 1, :] = seg_ref[pl.ds(z * count + order[j], 1), :]
    queries = jnp.concatenate([turned[z * count:z * count + 1, :] for z in range(ZS)], 1)
    turned[...] = turned[...].T
    return queries


def fill_bias(order, queries, turned, bias, z, count, rows):
    for j in range(count):
        same = turned[:, z * count + j:z * count + j + 1] == queries[:, z * rows:]
        bias[j * rows:(j + 1) * rows, z * rows:] = jnp.where(same, 0.0, NEG)
        key = lax.broadcasted_iota(jnp.int32, (rows, rows), 0) + order[j] * rows
        query = lax.broadcasted_iota(jnp.int32, (rows, rows), 1) + order[0] * rows
        ok = same[:, 0:rows] & (key <= query)
        bias[j * rows:(j + 1) * rows, z * rows:(z + 1) * rows] = jnp.where(ok, 0.0, NEG)


def head_parts(q_ref, keys, z, span, lower_q, lower_k):
    at = slice(z * span, (z + 1) * span)
    k01, kv2, v01 = (keys[at, i * LANES:(i + 1) * LANES] for i in range(3))
    one = jnp.ones_like(k01)
    return (k01, k01, kv2), (jnp.where(lower_k, v01, one), jnp.where(lower_k, one, v01), jnp.where(lower_k, one, kv2))


def attend_kernel(order, q_ref, seg_ref, *rest):
    count = len(rest) - 9
    kv_refs, low_refs, both_ref, (keys, bias, acc, turned) = rest[:count], rest[count:count + 4], rest[count + 4], rest[count + 5:]
    ctx_ref, tot_ref = both_ref.at[0], both_ref.at[1]
    total = q_ref.shape[0]
    rows = total // ZS
    span = count * rows
    fill_keys(kv_refs, keys, rows)
    queries = turn_segments(order, seg_ref, turned, count)
    lower_q = lax.broadcasted_iota(jnp.int32, (total, LANES), 1) < HEAD_DIM
    lower_k = lax.broadcasted_iota(jnp.int32, (span, LANES), 1) < HEAD_DIM
    q01, q2 = q_ref[:, 0:LANES], q_ref[:, LANES:2 * LANES]
    none = jnp.zeros_like(q01)
    qs = (jnp.where(lower_q, q01, none), jnp.where(lower_q, none, q01), q2)
    for z in range(ZS):
        fill_bias(order, queries, turned, bias, z, count, rows)
        ks, vs = head_parts(q_ref, keys, z, span, lower_q, lower_k)
        for h in range(3):
            scores = dot_nt(ks[h], qs[h][z * rows:, :]) + bias[:, z * rows:]
            expo = jnp.exp(scores).astype(BF)
            part = dot_tn(vs[h], expo)
            if z == 0:
                acc[h] = part
            else:
                acc[h, :, z * rows:] += part
    u0, u1, u2 = (acc[h].T for h in range(3))
    unnormed = jnp.where(lower_q, u0, u1)
    totals = jnp.where(lower_q, pltpu.roll(u0, HEAD_DIM, 1), pltpu.roll(u1, HEAD_DIM, 1))
    ctx = unnormed / totals
    tot_ref[:, 0:LANES] = totals
    ctx_ref[:, 0:LANES] = ctx
    ctx = pltpu.roll(u2, HEAD_DIM, 1) / u2
    tot_ref[:, LANES:] = u2
    ctx_ref[:, LANES:] = ctx
    for d in range(ZS):
        spot = pl.ds(pl.multiple_of(lax.rem(order[count] + d, ZS) * rows, rows), rows)
        low_refs[d][...] = ctx_ref[spot, 0:3 * HEAD_DIM].astype(BF)


def attend(order, q, seg, kvs, after=()):
    total = q.shape[0]
    span = len(kvs) * total // ZS
    outs = [((total // ZS, 3 * HEAD_DIM), BF)] * ZS + [((2, total, 2 * LANES), F32)]
    scratch = [pltpu.VMEM((ZS * span, 3 * LANES), BF), pltpu.VMEM((span, total), F32), pltpu.VMEM((3, LANES, total), F32), pltpu.VMEM((LANES, LANES), F32)]
    return call(attend_kernel, (order, q, seg, *kvs), outs, "attend", 1, after, scratch, 20)


def attend_back_kernel(order, q_ref, gc0, gc1, gc2, gc3, both_ref, seg_ref, *rest):
    ctx_ref, tot_ref = both_ref.at[0], both_ref.at[1]
    count = len(rest) - 9
    kv_refs, (dq_ref, kept_ref, sent_ref), (keys, bias, ge, acc, gctx_ref, turned) = rest[:count], rest[count:count + 3], rest[count + 3:]
    total = q_ref.shape[0]
    rows = total // ZS
    for d, ref in enumerate((gc0, gc1, gc2, gc3)):
        spot = pl.ds(pl.multiple_of(lax.rem(order[count] + ZS - d, ZS) * rows, rows), rows)
        gctx_ref[spot, :] = ref[...].astype(F32)
    span = count * rows
    fill_keys(kv_refs, keys, rows)
    queries = turn_segments(order, seg_ref, turned, count)
    lane = lax.broadcasted_iota(jnp.int32, (total, LANES), 1)
    lower_q = lane < HEAD_DIM
    lower_k = lax.broadcasted_iota(jnp.int32, (span, LANES), 1) < HEAD_DIM
    q01, q2 = q_ref[:, 0:LANES], q_ref[:, LANES:2 * LANES]
    none = jnp.zeros_like(q01)
    qs = (jnp.where(lower_q, q01, none), jnp.where(lower_q, none, q01), q2)
    gs = []
    g01 = gctx_ref[:, 0:LANES]
    g2 = jnp.concatenate([jnp.zeros((total, HEAD_DIM), F32), gctx_ref[:, LANES:]], 1)
    c2 = pltpu.roll(ctx_ref[:, LANES:], HEAD_DIM, 1)
    t2 = tot_ref[:, LANES:]
    t2 = jnp.where(lower_q, 1.0, pltpu.roll(t2, HEAD_DIM, 1))
    for h in range(3):
        grad = g2 if h == 2 else g01
        tot = t2 if h == 2 else tot_ref[:, 0:LANES]
        ctx = c2 if h == 2 else ctx_ref[:, 0:LANES]
        mine = lower_q if h == 0 else jnp.logical_not(lower_q)
        gu = jnp.where(mine, grad / tot, 0.0).astype(BF)
        gtot = -jnp.sum(jnp.where(mine, grad * ctx / tot, 0.0), -1, keepdims=True)
        high = gtot.astype(BF)
        low = (gtot - high.astype(F32)).astype(BF)
        first = HEAD_DIM if h == 0 else 0
        ge[h] = jnp.where(lane == first, high, jnp.where(lane == first + 1, low, gu))
        gs.append(gu)
    for z in range(ZS):
        fill_bias(order, queries, turned, bias, z, count, rows)
        ks, vs = head_parts(q_ref, keys, z, span, lower_q, lower_k)
        dk, dv = [], []
        for h in range(3):
            qz = qs[h][z * rows:, :]
            expo = jnp.exp(dot_nt(ks[h], qz) + bias[:, z * rows:])
            gprob = dot_nt(vs[h], ge[h, z * rows:, :])
            gscore = (expo * gprob).astype(BF)
            dv.append(dot(expo.astype(BF), gs[h][z * rows:, :]))
            dk.append(dot(gscore, qz))
            part = dot_tn(ks[h], gscore)
            if z == 0:
                acc[h] = part
            else:
                acc[h, :, z * rows:] += part
        parts = (dk[0] + dk[1], dk[2] + dv[2], dv[0] + dv[1])
        for j in range(count):
            to = kept_ref if j < count // 2 else sent_ref
            for i in range(3):
                to[j % (count // 2), z * rows:(z + 1) * rows, i * LANES:(i + 1) * LANES] = parts[i][j * rows:(j + 1) * rows, :].astype(to.dtype)
    upper = lax.broadcasted_iota(jnp.int32, (LANES, total), 0) >= HEAD_DIM
    dq_ref[:, 0:LANES] = (0.125 * jnp.where(upper, acc[1], acc[0])).T.astype(BF)
    dq_ref[:, LANES:] = (0.125 * acc[2]).T[:, 0:HEAD_DIM].astype(BF)


def attend_back(order, q, gctx, both, seg, kvs, after=()):
    total = q.shape[0]
    count = len(kvs)
    span = count * total // ZS
    outs = [((total, 3 * HEAD_DIM), BF), ((count // 2, total, 6 * HEAD_DIM), F32), ((count // 2, total, 6 * HEAD_DIM), BF)]
    scratch = [
        pltpu.VMEM((ZS * span, 3 * LANES), BF),
        pltpu.VMEM((span, total), F32),
        pltpu.VMEM((3, total, LANES), BF),
        pltpu.VMEM((3, LANES, total), F32),
        pltpu.VMEM((total, 3 * HEAD_DIM), F32),
        pltpu.VMEM((LANES, LANES), F32),
    ]
    return call(attend_back_kernel, (order, q, *gctx, both, seg, *kvs), outs, "attend_back", 1, after, scratch, 24)


def norm_parts(values):
    mean = jnp.mean(values, -1, keepdims=True)
    centered = values - mean
    rstd = lax.rsqrt(jnp.mean(centered * centered, -1, keepdims=True) + 1e-05)
    return centered * rstd, rstd


def norm_back(normed, rstd, grad, gain):
    q = grad * gain
    return rstd * (q - jnp.mean(q, -1, keepdims=True) - normed * jnp.mean(q * normed, -1, keepdims=True))


GC = 0.7978845608028654


class Part:
    def __init__(self, value, first, last):
        self.value, self.first, self.last = value, first, last


def call(body, args, outs, name, smem=0, after=(), scratch=(), mib=12):
    values = [arg.value if isinstance(arg, Part) else arg for arg in args]
    count, waits = len(values), len(after)

    def whole(*refs):
        ins = [ref.at[:, arg.first:arg.last] if isinstance(arg, Part) else ref for arg, ref in zip(args, refs)]
        body(*ins, *refs[count + waits:])

    specs = [pl.BlockSpec(memory_space=pltpu.SMEM if i < smem else pltpu.VMEM) for i in range(count)]
    return pl.pallas_call(
        whole,
        in_specs=specs + [pl.BlockSpec(memory_space=pl.ANY)] * waits,
        out_shape=[jax.ShapeDtypeStruct(*out) for out in outs],
        scratch_shapes=list(scratch),
        compiler_params=params(mib),
        cost_estimate=SMALL,
        name=name,
    )(*values, *after)


def fold_both(kept, came, ix, iy, width):
    sy, sz, sx, wr, wide = kept.shape

    def body(at_ref, kept_ref, came_ref, *outs):
        for d in range(sx):
            x = lax.rem(at_ref[0] + d, sx)
            outs[d][...] = (kept_ref[:, :, pl.ds(x, 1), :, 0:width].astype(F32) + came_ref[:, :, pl.ds(x, 1), :, 0:width].astype(F32)).astype(BF)
        for d in range(sy):
            y = lax.rem(at_ref[1] + d, sy)
            outs[sx + d][...] = (kept_ref[pl.ds(y, 1), :, :, :, width:].astype(F32) + came_ref[pl.ds(y, 1), :, :, :, width:].astype(F32)).astype(BF)

    outs = [((sy, sz, 1, wr, width), BF)] * sx + [((1, sz, sx, wr, wide - width), BF)] * sy
    return call(body, (jnp.stack([ix, iy]).astype(jnp.int32), kept, came), outs, "fold_both", 1)


def fold_cross(first, first_came, second, second_came, ix, iy):
    sx, sy = len(first), len(second)
    sz, wr, width = first[0].shape[1], first[0].shape[3], first[0].shape[4]
    other = second[0].shape[4]

    def body(at_ref, *refs):
        one, two, outs = refs[:sx], refs[sx:sx + sy], refs[sx + sy:]
        for d in range(sy):
            y = lax.rem(at_ref[1] + d, sy)
            total = one[0][pl.ds(y, 1)].astype(F32)
            for ref in one[1:]:
                total = total + ref[pl.ds(y, 1)].astype(F32)
            outs[d][...] = total.astype(BF)
        for d in range(sx):
            x = lax.rem(at_ref[0] + d, sx)
            total = two[0][:, :, pl.ds(x, 1)].astype(F32)
            for ref in two[1:]:
                total = total + ref[:, :, pl.ds(x, 1)].astype(F32)
            outs[sy + d][...] = total.astype(BF)

    outs = [((1, sz, 1, wr, width), BF)] * sy + [((1, sz, 1, wr, other), BF)] * sx
    args = (jnp.stack([ix, iy]).astype(jnp.int32), first[0], *first_came, second[0], *second_came)
    return call(body, args, outs, "fold_cross", 1)


def fold_last(first, first_came, second, second_came, iz, after):
    sy, sx = len(first), len(second)
    wr, width = first[0].shape[3:]
    wide = width + second[0].shape[4]

    def body(at_ref, *refs):
        one, two, outs = refs[:sy], refs[sy:sy + sx], refs[sy + sx:]
        for d in range(ZS):
            z = lax.rem(at_ref[0] + d, ZS)
            for sums, cols in ((one, slice(0, width)), (two, slice(width, wide))):
                total = sums[0][:, pl.ds(z, 1)].astype(F32)
                for ref in sums[1:]:
                    total = total + ref[:, pl.ds(z, 1)].astype(F32)
                outs[d][:, :, :, :, cols] = total.astype(BF)

    outs = [((1, 1, 1, wr, wide), BF)] * ZS
    args = (iz.astype(jnp.int32).reshape(1), first[0], *first_came, second[0], *second_came)
    return call(body, args, outs, "fold_last", 1, after)


def passed(pieces, axis):
    return [shift(pieces[d], axis, d) for d in range(1, len(pieces))]


def beside(pieces):
    rows, group = pieces[0].shape

    def body(*refs):
        for d, ref in enumerate(refs[:-1]):
            refs[-1][:, d * group:(d + 1) * group] = ref[...]

    return call(body, tuple(pieces), [((rows, len(pieces) * group), BF)], "beside")[0]


def out_project(place, cat, halves, hidden, vectors):
    rows, width = hidden.shape
    group = width // ZS
    half = width // 2

    def body(place_ref, cat_ref, own_ref, other_ref, hidden_ref, vec_ref, res_ref, n2_ref):
        own = jnp.zeros((rows, half), F32)
        other = jnp.zeros((rows, half), F32)
        for d in range(ZS):
            piece = cat_ref[:, d * group:(d + 1) * group]
            spot = pl.ds(pl.multiple_of(lax.rem(place_ref[0] + ZS - d, ZS) * group, group), group)
            own = own + dot(piece, own_ref[spot, :])
            other = other + dot(piece, other_ref[spot, :])
        first = place_ref[1] == 0
        branch = jnp.concatenate([jnp.where(first, own, other), jnp.where(first, other, own)], 1)
        total = hidden_ref[...].astype(F32) + branch + vec_ref[2:3, :]
        res_ref[:, 0:width] = total
        res_ref[:, width:] = jnp.broadcast_to(vec_ref[15:16, 0:rows], (LANES, rows)).T
        n2, _ = norm_parts(total)
        n2_ref[...] = (n2 * vec_ref[6:7, :] + vec_ref[7:8, :]).astype(BF)

    outs = [((rows, width + LANES), F32), ((rows, width), BF)]
    return call(body, (place, cat, *halves, hidden, vectors), outs, "out_project", 1)


def mlp_parts(weights, ff):
    width = weights[0].shape[0]
    if len(weights) == 2:
        return Part(weights[0], 0, ff), weights[1]
    return Part(weights[0], 0, ff), Part(weights[0], ff + width // 2, ff + width // 2 + width)


def mlp_up(blocks, weights, bias, ff):
    rows, width = blocks[0].shape
    count = len(blocks)
    half = count // 2

    def body(*refs):
        n2_refs, (bias_ref, up_ref, down_ref), (kept_ref, sent_ref, slope_ref, saved_ref) = refs[:count], refs[count:count + 3], refs[-4:]
        for j in range(count):
            saved_ref[j * rows:(j + 1) * rows, ff:] = n2_refs[j][...]
            pre = dot(n2_refs[j][...], up_ref[...]) + bias_ref[0:1, 0:ff]
            square = pre * pre
            tanh = jnp.tanh(GC * pre * (1.0 + 0.044715 * square))
            half_one = 0.5 * (1.0 + tanh)
            act = (pre * half_one).astype(BF)
            slope_ref[j] = (half_one + 0.5 * pre * (1.0 - tanh * tanh) * (GC + GC * 0.134145 * square)).astype(BF)
            saved_ref[j * rows:(j + 1) * rows, 0:ff] = act
            part = dot(act, down_ref[...])
            if j < half:
                kept_ref[j] = part + bias_ref[1:2, 0:width] if j == 0 else part
            else:
                sent_ref[j - half] = part.astype(BF)

    outs = [((half, rows, width), F32), ((half, rows, width), BF), ((count, rows, ff), BF), ((count * rows, ff + width), BF)]
    return call(body, (*blocks, bias, *mlp_parts(weights, ff)), outs, "mlp_up")


def finish(terms, residual, targets, scale):
    rows, width = targets.shape[1:]
    size = len(terms)

    def body(scale_ref, *refs):
        res_ref, target_ref, out_ref, err_ref, both_ref, gmlp_ref = refs[size:]
        valid = res_ref[:, width:width + 1]
        final = res_ref[:, 0:width]
        for ref in refs[:size]:
            final = final + ref[...].astype(F32)
        out_ref[...] = final.astype(BF)
        deviation = final - target_ref[0].astype(F32)
        grad = valid * (target_ref[1].astype(F32) + deviation * scale_ref[0])
        both_ref[0] = res_ref[:, 0:width]
        both_ref[1] = grad
        low = grad.astype(BF)
        gmlp_ref[...] = low
        err_ref[0:1, :] = jnp.sum(valid * deviation * deviation, 0, keepdims=True)
        err_ref[1:2, :] = jnp.sum(low.astype(F32), 0, keepdims=True)

    outs = [((rows, width), BF), ((2, width), F32), ((2, rows, width), F32), ((rows, width), BF)]
    return call(body, (scale, *terms, residual, targets), outs, "finish", 1)


def mlp_back(grads, weights, slope):
    rows, width = grads[0].shape
    count = len(grads)
    half = count // 2
    ff = slope.shape[2]

    def body(*refs):
        g_refs, (slope_ref, up_ref, down_ref), (kept_ref, sent_ref, gpre_ref, g_all) = refs[:count], refs[count:count + 3], refs[-4:]
        for j in range(count):
            g_all[j * rows:(j + 1) * rows, :] = g_refs[j][...]
            gpre = (dot_nt(g_refs[j][...], down_ref[...]) * slope_ref[j].astype(F32)).astype(BF)
            gpre_ref[j * rows:(j + 1) * rows, :] = gpre
            part = dot_nt(gpre, up_ref[...])
            if j < half:
                kept_ref[j] = part
            else:
                sent_ref[j - half] = part.astype(BF)

    outs = [((half, rows, width), F32), ((half, rows, width), BF), ((count * rows, ff), BF), ((count * rows, width), BF)]
    return call(body, (*grads, slope, *mlp_parts(weights, ff)), outs, "mlp_back")


def mlp_weights(grads, saved, gpre, after):
    width = grads.shape[1]
    ff = gpre.shape[1]

    def body(g_ref, saved_ref, gpre_ref, *outs):
        down_ref, up_ref = (outs[0].at[:, 0:width], outs[0].at[:, width:]) if ff == width else outs[:2]
        down_ref[...] = dot_tn(saved_ref[:, 0:ff], g_ref[...]).astype(BF)
        up_ref[...] = dot_tn(saved_ref[:, ff:], gpre_ref[...]).astype(BF)
        outs[-1][...] = jnp.sum(gpre_ref[...].astype(F32), 0, keepdims=True)

    outs = [((width, 2 * width), BF)] if ff == width else [((ff, width), BF), ((width, ff), BF)]
    *grads, sums = call(body, (grads, saved, gpre), outs + [((1, ff), F32)], "mlp_weights", after=after)
    return grads, sums


def out_back(place, terms, res_and_grad, vectors, ctx_cat, halves, after):
    rows, width = res_and_grad.shape[1:]
    group = width // ZS
    size = len(terms)

    def body(place_ref, *refs):
        (both_ref, vec_ref, cat_ref, own_ref, other_ref, gres_ref), gctx_refs, (gw_ref, sums_ref) = refs[size:size + 6], refs[size + 6:size + 10], refs[size + 10:]
        gn2 = refs[0][...]
        for ref in refs[1:size]:
            gn2 = gn2 + ref[...].astype(F32)
        n2, rstd = norm_parts(both_ref[0])
        gres = both_ref[1] + norm_back(n2, rstd, gn2, vec_ref[6:7, :])
        gres_ref[...] = gres
        branch = gres.astype(BF)
        left, right = branch[:, 0:width // 2], branch[:, width // 2:]
        first = place_ref[1] == 0
        own, other = jnp.where(first, left, right), jnp.where(first, right, left)
        for d in range(ZS):
            spot = pl.ds(pl.multiple_of(lax.rem(place_ref[0] + d, ZS) * group, group), group)
            gctx_refs[d][...] = (dot_nt(own, own_ref[spot, :]) + dot_nt(other, other_ref[spot, :])).astype(BF)
        for d in range(ZS):
            spot = pl.ds(pl.multiple_of(lax.rem(place_ref[0] + ZS - d, ZS) * group, group), group)
            gw_ref[spot, :] = dot_tn(cat_ref[:, d * group:(d + 1) * group], branch).astype(BF)
        rowsum = lambda v: jnp.sum(v, 0, keepdims=True)
        sums_ref[0:1, :] = rowsum(branch.astype(F32))
        sums_ref[1:2, :] = rowsum(gn2 * n2)
        sums_ref[2:3, :] = rowsum(gn2)

    outs = [((rows, width), F32)] + [((rows, group), BF)] * ZS + [((width, width), BF), ((3, width), F32)]
    args = (place, *terms, res_and_grad, vectors, ctx_cat, *halves)
    return call(body, args, outs, "out_back", 1, after)


def join_back(place, terms, dq, one):
    total, group = dq.shape
    width = one.shape[0]
    rows = total // ZS
    size = len(terms)
    cols = 3 * group

    def body(place_ref, *refs):
        dq_ref, w_ref, gj_ref, gn1_ref = refs[size:size + 4]
        out_refs = refs[size + 4:]
        dkv = refs[0][...]
        for ref in refs[1:size]:
            dkv = dkv + ref[...].astype(F32)
        gj_ref[:, 0:2 * group] = dkv.astype(BF)
        gj_ref[:, 2 * group:] = dq_ref[...]
        gn1_ref[...] = dot_nt(gj_ref[...], w_ref[:, 0:cols])
        for d in range(ZS):
            spot = pl.ds(pl.multiple_of(lax.rem(place_ref[0] + d, ZS) * rows, rows), rows)
            out_refs[d][...] = gn1_ref[spot, :].astype(out_refs[d].dtype)

    outs = [((total, cols), BF), ((total, width), F32), ((rows, width), F32)] + [((rows, width), BF)] * (ZS - 1)
    return call(body, (place, *terms, dq, one), outs, "join_back", 1)


def weights_back(place, n1, grad_joined, gn1, hidden, out_sums, fin_sums, up_rows, gw_out, wr, devices):
    total, cols = grad_joined.shape
    width = n1.shape[1]
    rows = total // ZS
    group = cols // 3
    upc = up_rows.shape[0]
    chips = width // (2 * wr)
    wide = width + cols + HEAD_DIM + LANES
    slots = -(-devices // wr)

    def body(place_ref, n1_ref, gj_ref, gn1_ref, hidden_ref, sums_ref, fin_ref, up_ref, gw_ref, kept_ref, sent_ref, vec, full):
        gain_sum = jnp.zeros((1, width), F32)
        for z in range(ZS):
            spot = slice(z * rows, (z + 1) * rows)
            normed, _ = norm_parts(hidden_ref[spot, :].astype(F32))
            gain_sum = gain_sum + jnp.sum(gn1_ref[spot, :] * normed, 0, keepdims=True)
        joined_sums = jnp.sum(gj_ref[...].astype(F32), 0, keepdims=True)
        vec[...] = jnp.zeros_like(vec)
        hd = HEAD_DIM
        for g in range(ZS):
            here = place_ref[0] == g
            at = g * group
            vec[0:1, at:at + group] = jnp.where(here, joined_sums[:, 2 * group:], 0.0)
            vec[1:2, at:at + 2 * hd] = jnp.where(here, joined_sums[:, 4 * hd:6 * hd], 0.0)
            vec[1:2, at + 2 * hd:at + 3 * hd] = jnp.where(here, joined_sums[:, 3 * hd:4 * hd], 0.0)
        vec[2:3, :] = sums_ref[0:1, :]
        vec[3:4, :] = fin_ref[1:2, :]
        vec[4:5, :] = gain_sum
        vec[5:6, :] = jnp.sum(gn1_ref[...], 0, keepdims=True)
        vec[6:8, :] = sums_ref[1:3, :]
        vec[8:8 + upc, :] = up_ref[...]
        error = jnp.sum(fin_ref[0:1, :], -1, keepdims=True)
        high = error.astype(BF).astype(F32)
        turn = lax.rem(lax.broadcasted_iota(jnp.int32, (1, width), 1), wr)
        for s in range(slots):
            vec[16 + s:17 + s, :] = jnp.where(turn + s * wr == place_ref[2], high, 0.0)
        vec[16 + slots:17 + slots, :] = jnp.where(turn == 0, error - high, 0.0)
        full[:, 0:width] = gw_ref[...].astype(F32)
        full[:, width:width + cols] = dot_tn(n1_ref[...], gj_ref[...])
        full[:, width + cols:width + cols + hd] = jnp.zeros((width, hd), F32)
        full[:, width + cols + hd:] = vec[...].T
        for c in range(2):
            @pl.when(place_ref[1] == c)
            def _():
                for chip in range(chips):
                    at = chip * 2 * wr
                    kept_ref[chip] = full[at + c * wr:at + (c + 1) * wr, :].astype(BF)
                    sent_ref[chip] = full[at + (1 - c) * wr:at + (2 - c) * wr, :].astype(BF)

    outs = [((chips, wr, wide), BF)] * 2
    scratch = [pltpu.VMEM((LANES, width), F32), pltpu.VMEM((width, wide), F32)]
    return call(body, (place, n1, grad_joined, gn1, hidden, out_sums, fin_sums, up_rows, gw_out), outs, "weights_back", 1, scratch=scratch, mib=20)


def input_back(terms, hidden, vectors, grad_res):
    rows, width = hidden.shape

    def body(t0, t1, t2, t3, hidden_ref, gain_ref, gres_ref, out_ref):
        back = t0[...] + t1[...].astype(F32) + t2[...].astype(F32) + t3[...].astype(F32)
        normed, rstd = norm_parts(hidden_ref[...].astype(F32))
        out_ref[...] = gres_ref[...] + norm_back(normed, rstd, back, gain_ref[4:5, :])

    return call(body, (terms[0], *terms[1:], hidden, vectors, grad_res), [((rows, width), F32)], "input_back")[0]


def unpack_one(place, pieces, after):
    rows, wide = pieces[0].shape[-2:]
    hd = HEAD_DIM
    group = 3 * hd
    width = ZS * group

    def body(place_ref, p0, p1, p2, p3, qkv_ref, vec_ref, out_ref, held_ref):
        for d, piece in enumerate((p0, p1, p2, p3)):
            held_ref[pl.ds(lax.rem(place_ref[0] + ZS - d, ZS), 1)] = piece[...].reshape(1, rows, wide).astype(F32)
        vec_total = jnp.zeros((rows, LANES), F32)
        out_total = jnp.zeros((rows, width), F32)
        for g in range(ZS):
            k = width + g * group
            v = 2 * width + g * group
            at = width
            qkv_ref[:, k:k + 3 * hd] = held_ref[g, :, at:at + 3 * hd]
            qkv_ref[:, v + 2 * hd:v + 3 * hd] = held_ref[g, :, at + 3 * hd:at + 4 * hd]
            qkv_ref[:, v:v + 2 * hd] = held_ref[g, :, at + 4 * hd:at + 6 * hd]
            qkv_ref[:, g * group:g * group + 3 * hd] = held_ref[g, :, at + 6 * hd:at + 9 * hd]
            vec_total = vec_total + held_ref[g, :, at + 10 * hd:]
            out_total = out_total + held_ref[g, :, 0:width]
        vec_ref[...] = vec_total
        out_ref[...] = out_total

    outs = [((rows, 3 * width), F32), ((rows, LANES), F32), ((rows, width), F32)]
    return call(body, (place, *pieces), outs, "unpack_one", 1, after, scratch=[pltpu.VMEM((ZS, rows, wide), F32)])


def per_device(hidden_in, w_qkv, q_bias, v_bias, w_out, out_bias, w_up, up_bias, w_down, down_bias, ln1_gain, ln1_bias, ln2_gain, ln2_bias, segment_ids, padding_mask, teacher, cotangent):
    sy, sz, sx = (lax.axis_size(a) for a in ("y", "z", "x"))
    iy, iz, ix, core = (lax.axis_index(a) for a in ("y", "z", "x", "core"))
    device = ((iy * sz + iz) * sx + ix) * 2 + core
    devices = sy * sz * sx * 2
    rows, width = hidden_in.shape[1:]
    wr = w_qkv.shape[0]
    ffd = w_down.shape[0]
    ff = sy * sz * ffd
    upc = ffd // wr
    wcols = 9 * HEAD_DIM
    group = width // sz
    place = iz.astype(jnp.int32).reshape(1)
    at_zc = jnp.stack([iz, core]).astype(jnp.int32)

    def from_z(value):
        return [value] + [shift(value, "z", d) for d in range(1, sz)]

    def to_z(pieces):
        return [pieces[0]] + [shift(pieces[d], "z", d) for d in range(1, sz)]

    def cut_z(value):
        return [lax.dynamic_slice_in_dim(value, lax.rem(iz + d, sz), 1, 0) for d in range(sz)]

    flat = jnp.concatenate([jnp.stack([q_bias, v_bias, out_bias, down_bias, ln1_gain, ln1_bias, ln2_gain, ln2_bias]), up_bias.reshape(upc, wr)])
    hidden = hidden_in[0]
    pieces = from_z(hidden)
    targets = jnp.concatenate([teacher, cotangent], 0)
    one = arrange(to_z(cut_z(pack_one(w_qkv, flat, segment_ids, padding_mask))), iz, 0)
    one = gather(one[None, :, None], "x", 2, after=[pieces[1]])
    one = gather(one, "y", 0, after=pieces[2:])[:, :, :, None]
    one = gather(one, "core", 3).reshape(width, -1)

    at_xc = jnp.stack([ix, core]).astype(jnp.int32)
    ups = list(pack_up(at_xc, w_up, w_out, ffd, sx))
    for d in range(1, 2 * sx):
        dc, dx = d // sx, d % sx
        pairs = [(x * 2 + c, (x + dx) % sx * 2 + (c + dc) % 2) for x in range(sx) for c in range(2)]
        ups[d] = lax.ppermute(ups[d], ("x", "core"), pairs)
    weights = [join_up(at_xc, ups, w_down)]
    if ffd != 2 * sx * wr:
        weights = weights + [w_down]
    weights = [lax.all_gather(member, ("y", "z"), axis=0, tiled=True) for member in weights]

    vec = one[:, wcols:]
    vectors = jnp.concatenate([vec[:, :15].T.astype(F32), jnp.pad(padding_mask.astype(F32), ((0, 0), (0, width - rows)))])
    ub = vectors[8:8 + upc].reshape(upc, sy * sz, sx * 2, wr)
    ub = lax.dynamic_index_in_dim(ub, ix * 2 + core, 2, keepdims=False).transpose(1, 0, 2).reshape(1, ff)
    wide = max(ff, width)
    biases = jnp.concatenate([jnp.pad(ub, ((0, 0), (0, wide - ff))), jnp.pad(vectors[3:4], ((0, 0), (0, wide - width)))])
    count = jnp.sum(vectors[8 + upc]) / wr
    seg = lax.dynamic_index_in_dim(vec.reshape(sy, sz * sx * 2, wr, LANES), iy, 0, keepdims=False)[:, :2, HEAD_DIM:].astype(F32).reshape(sz * sx * 2, rows)
    spots = [(lax.rem(ix + sx - d, sx), core) for d in range(sx)]
    spots = spots + [(at, 1 - core) for at, _ in spots]
    order = jnp.stack([at * 2 + c for at, c in spots] + [iz]).astype(jnp.int32)

    n1_low, q, kv, hidden_all = project(place, pieces, one, vectors)
    kvs = spread_tokens(kv)
    *ctx_parts, ctx_tot = attend(order, q, seg, kvs, after=[biases])
    ctx_cat = beside(to_z(ctx_parts))
    wo = [held(Part(weights[0], ff, ff + width // 2), [ctx_cat])]
    wo = wo + [shift(wo[0], "core", 1)]
    residual, n2_low = out_project(at_zc, ctx_cat, wo, hidden, vectors)
    kept, sent, slope, saved = mlp_up(spread_tokens(n2_low), weights, biases, ff)
    layer_out, fin_sums, res_and_grad, grad_mlp = finish(fold_tokens(kept, sent), residual, targets, (2.0 / (count * width)).reshape(1))

    kept, sent, grad_pre, grads = mlp_back(spread_tokens(grad_mlp), weights, slope)
    gn2_terms = fold_tokens(kept, sent)
    gw_mlp, up_sums = mlp_weights(grads, saved, grad_pre, after=gn2_terms[:1])
    gw_sums = [lax.psum_scatter(member, ("y", "z"), scatter_dimension=0, tiled=True) for member in gw_mlp]
    grad_res, *gctx, gw_out, out_sums = out_back(at_zc, gn2_terms, res_and_grad, vectors, ctx_cat, wo, after=[up_sums])
    dq, dkv_kept, dkv_sent = attend_back(order, q, to_z(gctx), ctx_tot, seg, kvs)
    grad_joined, gn1, *gn1_parts = join_back(place, fold_tokens(dkv_kept, dkv_sent), dq, one)
    gn1_parts = to_z(gn1_parts)
    input_grad = input_back(gn1_parts, hidden, vectors, grad_res)

    up_rows = jnp.zeros((upc, sy * sz, sx * 2, wr), F32)
    up_rows = lax.dynamic_update_slice_in_dim(up_rows, up_sums.reshape(sy * sz, upc, wr).transpose(1, 0, 2)[:, :, None], ix * 2 + core, 2).reshape(upc, width)
    places = jnp.stack([iz, core, device]).astype(jnp.int32)
    kept, sent = weights_back(places, n1_low, grad_joined, gn1, hidden_all, out_sums, fin_sums, up_rows, gw_out, wr, devices)
    third = fold_both(kept.reshape(sy, sz, sx, wr, -1), shift(sent, "core", 1).reshape(sy, sz, sx, wr, -1), ix, iy, width)
    third = fold_cross(third[:sx], passed(third[:sx], "x"), third[sx:], passed(third[sx:], "y"), ix, iy)
    third = fold_last(third[:sy], passed(third[:sy], "y"), third[sy:], passed(third[sy:], "x"), iz, after=[gn1_parts[2], gn1_parts[3]])
    ready = third[0][0, 0, 0, :, :LANES]
    gw_sums = [held(member, [ready]) for member in gw_sums]
    third = [third[0]] + passed(third, "z")

    gw_down = gw_sums[0][:, :width].astype(F32)
    gw_up = gw_sums[-1][:, -ff:].reshape(1, 1, sx, 2, wr, ff)
    up_x = [lax.dynamic_slice_in_dim(gw_up, lax.rem(ix + d, sx), 1, 2) for d in range(sx)]
    gw_up = arrange([up_x[0]] + [shift(up_x[d], "x", d) for d in range(1, sx)], ix, 2)
    gw_up = arrange([lax.dynamic_slice_in_dim(gw_up, core, 1, 3), shift(lax.dynamic_slice_in_dim(gw_up, 1 - core, 1, 3), "core", 1)], core, 3)
    gw_up = gw_up.reshape(sx, 2, wr, sy * sz, ffd).transpose(2, 3, 0, 1, 4).reshape(wr, -1).astype(F32)

    grad_w_qkv, sums, gw_out = unpack_one(place, third, after=[gw_up])
    sums = sums.T
    loss = jnp.sum(sums[16:17 + -(-devices // wr)]) / (count * width)
    return (
        layer_out[None], loss, input_grad[None], grad_w_qkv, sums[0], sums[1], gw_out, sums[2],
        gw_up, sums[8:8 + upc].reshape(-1), gw_down, sums[3], sums[4], sums[5], sums[6], sums[7],
    )


def solution(mesh):
    seq, ctx = mesh.shape["seq"], mesh.shape["ctx"]
    grid = Mesh(mesh.devices.reshape(seq, ZS, ctx // (2 * ZS), 2), ("y", "z", "x", "core"))
    every = ("y", "z", "x", "core")
    matrix, vector = P(every, None), P(every)
    tokens = P("y", ("z", "x", "core"), None)
    marks = P("y", ("z", "x", "core"))
    return jax.shard_map(
        per_device,
        mesh=grid,
        in_specs=(tokens, matrix, vector, vector, matrix, vector, matrix, vector, matrix, vector, vector, vector, vector, vector, marks, marks, tokens, tokens),
        out_specs=(tokens, P(), tokens, matrix, vector, vector, matrix, vector, matrix, vector, matrix, vector, vector, vector, vector, vector),
        check_vma=False,
    )
```

```python
import functools

import jax
import jax.numpy as jnp
from jax import lax
from jax.experimental import pallas as pl
from jax.experimental.pallas import tpu as pltpu
from jax.sharding import Mesh
from jax.sharding import PartitionSpec as P

HEADS = 12
HEAD_DIM = 64
ZS = 4
BF = jnp.bfloat16
F32 = jnp.float32
NEG = -1e30
LANES = 128


def shift(value, axis, step):
    size = lax.axis_size(axis)
    return lax.ppermute(value, axis, [(a, (a + step) % size) for a in range(size)])


def gather(value, axis, dim, after=()):
    size = lax.axis_size(axis)
    return arrange([value] + [shift(value, axis, d) for d in range(1, size)], lax.axis_index(axis), dim, after)


def scatter_sum(value, axis, dim, last=BF, after=()):
    size = lax.axis_size(axis)
    place = lax.axis_index(axis)

    def cut(d):
        return lax.dynamic_slice_in_dim(value, lax.rem(place + d, size), 1, dim)

    came = [shift(cut(d), axis, d) for d in range(1, size)]

    def body(place_ref, value_ref, *refs):
        index = (slice(None),) * dim + (pl.ds(place_ref[0], 1),)
        total = value_ref[index].astype(F32)
        for ref in refs[:size - 1]:
            total = total + ref[...].astype(F32)
        refs[-1][...] = total.astype(last)

    vmem = pl.BlockSpec(memory_space=pltpu.VMEM)
    return pl.pallas_call(
        body,
        in_specs=[pl.BlockSpec(memory_space=pltpu.SMEM)] + [vmem] * size + [pl.BlockSpec(memory_space=pl.ANY)] * len(after),
        out_shape=jax.ShapeDtypeStruct(came[0].shape, last),
        compiler_params=params(),
        cost_estimate=SMALL,
        name="scatter_sum",
    )(place.astype(jnp.int32).reshape(1), value, *came, *after)


def spread_tokens(value):
    some = [value] + [shift(value, "x", d) for d in range(1, lax.axis_size("x"))]
    return some + [shift(member, "core", 1) for member in some]


def fold_tokens(kept, sent, own=F32):
    came = shift(sent, "core", 1)
    size = kept.shape[0]
    shape = kept.shape[1:]

    def body(kept_ref, came_ref, *outs):
        for d in range(size):
            outs[d][...] = (kept_ref[d] + came_ref[d].astype(F32)).astype(outs[d].dtype)

    terms = call(body, (kept, came), [(shape, BF if d else own) for d in range(size)], "fold_tokens")
    return [terms[0]] + [shift(terms[d], "x", -d) for d in range(1, size)]


def dot(a, b):
    return jnp.dot(a, b, preferred_element_type=F32)


def dot_nt(a, b):
    return lax.dot_general(a, b, (((1,), (1,)), ((), ())), preferred_element_type=F32)


def dot_tn(a, b):
    return lax.dot_general(a, b, (((0,), (0,)), ((), ())), preferred_element_type=F32)


SMALL = pl.CostEstimate(flops=1, bytes_accessed=1, transcendentals=0)


def params(mib=6):
    return pltpu.CompilerParams(vmem_limit_bytes=mib * 1024 * 1024)


def pack_one(w_qkv, flat, marks):
    rows, width = w_qkv.shape[0], w_qkv.shape[1] // 3
    group = width // ZS
    hd = HEAD_DIM
    upc = flat.shape[0] - 8

    def body(qkv_ref, flat_ref, marks_ref, one_ref, vec):
        vec[...] = jnp.zeros_like(vec)
        vec[0:8 + upc, 0:rows] = flat_ref[...].astype(F32)
        count = jnp.sum(marks_ref[1:2, :].astype(F32), -1, keepdims=True)
        lane = lax.broadcasted_iota(jnp.int32, (LANES, LANES), 1)
        vec[...] = jnp.where(lane == 8 + upc, count, vec[...].T)
        ids = marks_ref[0:1, :].astype(F32)
        vec[0:1, hd:] = ids[:, 0:hd]
        vec[1:2, hd:] = ids[:, hd:]
        cols = vec[0:rows, :].astype(BF)
        for g in range(ZS):
            k = width + g * group
            v = 2 * width + g * group
            one_ref[g, :, 0:3 * hd] = qkv_ref[:, k:k + 3 * hd]
            one_ref[g, :, 3 * hd:4 * hd] = qkv_ref[:, v + 2 * hd:v + 3 * hd]
            one_ref[g, :, 4 * hd:6 * hd] = qkv_ref[:, v:v + 2 * hd]
            one_ref[g, :, 6 * hd:9 * hd] = qkv_ref[:, g * group:g * group + 3 * hd]
            one_ref[g, :, 9 * hd:11 * hd] = cols

    outs = [((ZS, rows, 11 * hd), BF)]
    return call(body, (w_qkv, flat, marks), outs, "pack_one", scratch=[pltpu.VMEM((LANES, LANES), F32)])[0]


def pack_up(place, w_up, w_out, ffd, sx):
    rows, width = w_out.shape
    half = width // 2
    blocks = w_up.shape[1] // (2 * sx * ffd)
    ff = blocks * ffd

    def body(at_ref, up_ref, out_ref, *refs):
        outs, every = refs[:-1], refs[-1]
        for c in range(2):
            for x in range(sx):
                for b in range(blocks):
                    at = ((b * sx + x) * 2 + c) * ffd
                    every[c * sx + x, :, b * ffd:(b + 1) * ffd] = up_ref[:, at:at + ffd]
                every[c * sx + x, :, ff:] = out_ref[:, c * half:(c + 1) * half]
        for dc in range(2):
            core = at_ref[1] if dc == 0 else 1 - at_ref[1]
            for dx in range(sx):
                outs[dc * sx + dx][...] = every[core * sx + lax.rem(at_ref[0] + dx, sx)]

    outs = [((rows, ff + half), BF)] * (2 * sx)
    return call(body, (place, w_up, w_out), outs, "pack_up", 1, scratch=[pltpu.VMEM((2 * sx, rows, ff + half), BF)])


def join_up(place, pieces, w_down):
    sx = len(pieces) // 2
    rows, cols = pieces[0].shape
    joined = w_down.shape[0] == 2 * sx * rows
    wide = cols + w_down.shape[1] if joined else cols

    def body(at_ref, *refs):
        out = refs[-1]
        for dc in range(2):
            core = at_ref[1] if dc == 0 else 1 - at_ref[1]
            for dx in range(sx):
                spot = lax.rem(at_ref[0] + sx - dx, sx) * 2 + core
                out[pl.ds(spot, 1), :, 0:cols] = refs[dc * sx + dx][...].reshape(1, rows, cols)
        if joined:
            out[:, :, cols:] = refs[2 * sx][...]

    args = (place, *pieces, w_down.reshape(2 * sx, rows, -1)) if joined else (place, *pieces)
    return call(body, args, [((2 * sx, rows, wide), BF)], "join_up", 1)[0].reshape(2 * sx * rows, wide)


def held(value, after):
    def body(value_ref, out_ref):
        out_ref[...] = value_ref[...]

    array = value.value if isinstance(value, Part) else value
    shape = (array.shape[0], value.last - value.first) if isinstance(value, Part) else array.shape
    return call(body, (value,), [(shape, array.dtype)], "held", 0, after)[0]


def arrange(pieces, place, dim, after=()):
    size = len(pieces)
    shape = list(pieces[0].shape)
    shape[dim] = size

    def body(place_ref, *refs):
        out = refs[-1]
        for d in range(size):
            spot = lax.rem(place_ref[0] + size - d, size)
            index = (slice(None),) * dim + (pl.ds(spot, 1),)
            out[index] = refs[d][...]

    return pl.pallas_call(
        body,
        in_specs=[pl.BlockSpec(memory_space=pltpu.SMEM)] + [pl.BlockSpec(memory_space=pltpu.VMEM)] * size + [pl.BlockSpec(memory_space=pl.ANY)] * len(after),
        out_shape=jax.ShapeDtypeStruct(tuple(shape), pieces[0].dtype),
        compiler_params=params(),
        cost_estimate=SMALL,
        name="arrange",
    )(place.astype(jnp.int32).reshape(1), *pieces, *after)


def project(place, pieces, one, vectors):
    rows, width = pieces[0].shape
    total = ZS * rows
    hd = HEAD_DIM
    group = 3 * hd

    def body(place_ref, h0, h1, h2, h3, w_ref, vec_ref, kv_ref, q_ref, saved_ref):
        qb = jnp.zeros((1, group), F32)
        vb = jnp.zeros((1, group), F32)
        for g in range(ZS):
            here = place_ref[0] == g
            qb = jnp.where(here, vec_ref[0:1, g * group:(g + 1) * group], qb)
            vb = jnp.where(here, vec_ref[1:2, g * group:(g + 1) * group], vb)
        for d, piece in enumerate((h0, h1, h2, h3)):
            spot = pl.ds(pl.multiple_of(lax.rem(place_ref[0] + ZS - d, ZS) * rows, rows), rows)
            saved_ref[spot, width:] = piece[...]
            normed, _ = norm_parts(piece[...].astype(F32))
            n1 = (normed * vec_ref[4:5, :] + vec_ref[5:6, :]).astype(BF)
            saved_ref[spot, 0:width] = n1
            joined = dot(n1, w_ref[:, 0:9 * hd])
            kv_ref[spot, 0:3 * hd] = joined[:, 0:3 * hd].astype(BF)
            kv_ref[spot, 3 * hd:4 * hd] = (joined[:, 3 * hd:4 * hd] + vb[:, 2 * hd:]).astype(BF)
            kv_ref[spot, 4 * hd:6 * hd] = (joined[:, 4 * hd:6 * hd] + vb[:, 0:2 * hd]).astype(BF)
            q = (joined[:, 6 * hd:9 * hd] + qb).astype(BF).astype(F32) * 0.125
            q_ref[spot, 0:3 * hd] = q.astype(BF)
            q_ref[spot, 3 * hd:4 * hd] = jnp.zeros((rows, hd), BF)

    outs = [((total, 6 * hd), BF), ((total, 4 * hd), BF), ((total, 2 * width), BF)]
    return call(body, (place, pieces[0], *pieces[1:], one, vectors), outs, "project", 1)


def fill_keys(kv_refs, keys, rows):
    for j, ref in enumerate(kv_refs):
        for z in range(ZS):
            at = (z * len(kv_refs) + j) * rows
            keys[at:at + rows, :] = ref[z * rows:(z + 1) * rows, :]


def turn_segments(order, seg_ref, turned, count):
    turned[...] = jnp.zeros_like(turned)
    for z in range(ZS):
        for j in range(count):
            turned[z * count + j:z * count + j + 1, :] = seg_ref[pl.ds(z * count + order[j], 1), :]
    queries = jnp.concatenate([turned[z * count:z * count + 1, :] for z in range(ZS)], 1)
    turned[...] = turned[...].T
    return queries


def fill_bias(order, queries, turned, bias, z, count, rows):
    for j in range(count):
        same = turned[:, z * count + j:z * count + j + 1] == queries[:, z * rows:]
        bias[j * rows:(j + 1) * rows, z * rows:] = jnp.where(same, 0.0, NEG)
        key = lax.broadcasted_iota(jnp.int32, (rows, rows), 0) + order[j] * rows
        query = lax.broadcasted_iota(jnp.int32, (rows, rows), 1) + order[0] * rows
        ok = same[:, 0:rows] & (key <= query)
        bias[j * rows:(j + 1) * rows, z * rows:(z + 1) * rows] = jnp.where(ok, 0.0, NEG)


def head_parts(q_ref, keys, z, span, lower_q, lower_k):
    at = slice(z * span, (z + 1) * span)
    k01, kv2, v01 = (keys[at, i * LANES:(i + 1) * LANES] for i in range(3))
    one = jnp.ones_like(k01)
    return (k01, k01, kv2), (jnp.where(lower_k, v01, one), jnp.where(lower_k, one, v01), jnp.where(lower_k, one, kv2))


def attend_kernel(order, q_ref, seg_ref, *rest):
    count = len(rest) - 9
    kv_refs, low_refs, both_ref, (keys, bias, acc, turned) = rest[:count], rest[count:count + 4], rest[count + 4], rest[count + 5:]
    ctx_ref, tot_ref = both_ref.at[0], both_ref.at[1]
    total = q_ref.shape[0]
    rows = total // ZS
    span = count * rows
    fill_keys(kv_refs, keys, rows)
    queries = turn_segments(order, seg_ref, turned, count)
    lower_q = lax.broadcasted_iota(jnp.int32, (total, LANES), 1) < HEAD_DIM
    lower_k = lax.broadcasted_iota(jnp.int32, (span, LANES), 1) < HEAD_DIM
    q01, q2 = q_ref[:, 0:LANES], q_ref[:, LANES:2 * LANES]
    none = jnp.zeros_like(q01)
    qs = (jnp.where(lower_q, q01, none), jnp.where(lower_q, none, q01), q2)
    for z in range(ZS):
        fill_bias(order, queries, turned, bias, z, count, rows)
        ks, vs = head_parts(q_ref, keys, z, span, lower_q, lower_k)
        for h in range(3):
            scores = dot_nt(ks[h], qs[h][z * rows:, :]) + bias[:, z * rows:]
            expo = jnp.exp(scores).astype(BF)
            part = dot_tn(vs[h], expo)
            if z == 0:
                acc[h] = part
            else:
                acc[h, :, z * rows:] += part
    u0, u1, u2 = (acc[h].T for h in range(3))
    unnormed = jnp.where(lower_q, u0, u1)
    totals = jnp.where(lower_q, pltpu.roll(u0, HEAD_DIM, 1), pltpu.roll(u1, HEAD_DIM, 1))
    ctx = unnormed / totals
    tot_ref[:, 0:LANES] = totals
    ctx_ref[:, 0:LANES] = ctx
    ctx = pltpu.roll(u2, HEAD_DIM, 1) / u2
    tot_ref[:, LANES:] = u2
    ctx_ref[:, LANES:] = ctx
    for d in range(ZS):
        spot = pl.ds(pl.multiple_of(lax.rem(order[count] + d, ZS) * rows, rows), rows)
        low_refs[d][...] = ctx_ref[spot, 0:3 * HEAD_DIM].astype(BF)


def attend(order, q, seg, kvs, after=()):
    total = q.shape[0]
    span = len(kvs) * total // ZS
    outs = [((total // ZS, 3 * HEAD_DIM), BF)] * ZS + [((2, total, 2 * LANES), F32)]
    scratch = [pltpu.VMEM((ZS * span, 3 * LANES), BF), pltpu.VMEM((span, total), F32), pltpu.VMEM((3, LANES, total), F32), pltpu.VMEM((LANES, LANES), F32)]
    return call(attend_kernel, (order, q, seg, *kvs), outs, "attend", 1, after, scratch, 20)


def attend_back_kernel(order, q_ref, gc0, gc1, gc2, gc3, both_ref, seg_ref, *rest):
    ctx_ref, tot_ref = both_ref.at[0], both_ref.at[1]
    count = len(rest) - 10
    kv_refs, (dq_ref, kept_ref, sent_ref, done_ref), (keys, bias, ge, acc, gctx_ref, turned) = rest[:count], rest[count:count + 4], rest[count + 4:]
    done_ref[...] = jnp.zeros_like(done_ref)
    total = q_ref.shape[0]
    rows = total // ZS
    for d, ref in enumerate((gc0, gc1, gc2, gc3)):
        spot = pl.ds(pl.multiple_of(lax.rem(order[count] + ZS - d, ZS) * rows, rows), rows)
        gctx_ref[spot, :] = ref[...].astype(F32)
    span = count * rows
    fill_keys(kv_refs, keys, rows)
    queries = turn_segments(order, seg_ref, turned, count)
    lane = lax.broadcasted_iota(jnp.int32, (total, LANES), 1)
    lower_q = lane < HEAD_DIM
    lower_k = lax.broadcasted_iota(jnp.int32, (span, LANES), 1) < HEAD_DIM
    q01, q2 = q_ref[:, 0:LANES], q_ref[:, LANES:2 * LANES]
    none = jnp.zeros_like(q01)
    qs = (jnp.where(lower_q, q01, none), jnp.where(lower_q, none, q01), q2)
    gs = []
    g01 = gctx_ref[:, 0:LANES]
    g2 = jnp.concatenate([jnp.zeros((total, HEAD_DIM), F32), gctx_ref[:, LANES:]], 1)
    c2 = pltpu.roll(ctx_ref[:, LANES:], HEAD_DIM, 1)
    t2 = tot_ref[:, LANES:]
    t2 = jnp.where(lower_q, 1.0, pltpu.roll(t2, HEAD_DIM, 1))
    for h in range(3):
        grad = g2 if h == 2 else g01
        tot = t2 if h == 2 else tot_ref[:, 0:LANES]
        ctx = c2 if h == 2 else ctx_ref[:, 0:LANES]
        mine = lower_q if h == 0 else jnp.logical_not(lower_q)
        gu = jnp.where(mine, grad / tot, 0.0).astype(BF)
        gtot = -jnp.sum(jnp.where(mine, grad * ctx / tot, 0.0), -1, keepdims=True)
        high = gtot.astype(BF)
        low = (gtot - high.astype(F32)).astype(BF)
        first = HEAD_DIM if h == 0 else 0
        ge[h] = jnp.where(lane == first, high, jnp.where(lane == first + 1, low, gu))
        gs.append(gu)
    for z in range(ZS):
        fill_bias(order, queries, turned, bias, z, count, rows)
        ks, vs = head_parts(q_ref, keys, z, span, lower_q, lower_k)
        dk, dv = [], []
        for h in range(3):
            qz = qs[h][z * rows:, :]
            expo = jnp.exp(dot_nt(ks[h], qz) + bias[:, z * rows:])
            gprob = dot_nt(vs[h], ge[h, z * rows:, :])
            gscore = (expo * gprob).astype(BF)
            dv.append(dot(expo.astype(BF), gs[h][z * rows:, :]))
            dk.append(dot(gscore, qz))
            part = dot_tn(ks[h], gscore)
            if z == 0:
                acc[h] = part
            else:
                acc[h, :, z * rows:] += part
        parts = (dk[0] + dk[1], dk[2] + dv[2], dv[0] + dv[1])
        for j in range(count):
            to = kept_ref if j < count // 2 else sent_ref
            for i in range(3):
                to[j % (count // 2), z * rows:(z + 1) * rows, i * LANES:(i + 1) * LANES] = parts[i][j * rows:(j + 1) * rows, :].astype(to.dtype)
    upper = lax.broadcasted_iota(jnp.int32, (LANES, total), 0) >= HEAD_DIM
    dq_ref[:, 0:LANES] = (0.125 * jnp.where(upper, acc[1], acc[0])).T.astype(BF)
    dq_ref[:, LANES:] = (0.125 * acc[2]).T[:, 0:HEAD_DIM].astype(BF)


def attend_back(order, q, gctx, both, seg, kvs, after=()):
    total = q.shape[0]
    count = len(kvs)
    span = count * total // ZS
    outs = [((total, 3 * HEAD_DIM), BF), ((count // 2, total, 6 * HEAD_DIM), F32), ((count // 2, total, 6 * HEAD_DIM), BF), ((8, LANES), F32)]
    scratch = [
        pltpu.VMEM((ZS * span, 3 * LANES), BF),
        pltpu.VMEM((span, total), F32),
        pltpu.VMEM((3, total, LANES), BF),
        pltpu.VMEM((3, LANES, total), F32),
        pltpu.VMEM((total, 3 * HEAD_DIM), F32),
        pltpu.VMEM((LANES, LANES), F32),
    ]
    return call(attend_back_kernel, (order, q, *gctx, both, seg, *kvs), outs, "attend_back", 1, after, scratch, 24)


def norm_parts(values):
    mean = jnp.mean(values, -1, keepdims=True)
    centered = values - mean
    rstd = lax.rsqrt(jnp.mean(centered * centered, -1, keepdims=True) + 1e-05)
    return centered * rstd, rstd


def norm_back(normed, rstd, grad, gain):
    q = grad * gain
    return rstd * (q - jnp.mean(q, -1, keepdims=True) - normed * jnp.mean(q * normed, -1, keepdims=True))


GC = 0.7978845608028654


class Part:
    def __init__(self, value, first, last):
        self.value, self.first, self.last = value, first, last


def call(body, args, outs, name, smem=0, after=(), scratch=(), mib=12):
    values = [arg.value if isinstance(arg, Part) else arg for arg in args]
    count, waits = len(values), len(after)

    def whole(*refs):
        ins = [ref.at[:, arg.first:arg.last] if isinstance(arg, Part) else ref for arg, ref in zip(args, refs)]
        body(*ins, *refs[count + waits:])

    specs = [pl.BlockSpec(memory_space=pltpu.SMEM if i < smem else pltpu.VMEM) for i in range(count)]
    return pl.pallas_call(
        whole,
        in_specs=specs + [pl.BlockSpec(memory_space=pl.ANY)] * waits,
        out_shape=[jax.ShapeDtypeStruct(*out) for out in outs],
        scratch_shapes=list(scratch),
        compiler_params=params(mib),
        cost_estimate=SMALL,
        name=name,
    )(*values, *after)


def fold_both(kept, came, ix, iy, width):
    sy, sz, sx, wr, wide = kept.shape

    def body(at_ref, kept_ref, came_ref, *outs):
        for d in range(sx):
            x = lax.rem(at_ref[0] + d, sx)
            outs[d][...] = (kept_ref[:, :, pl.ds(x, 1), :, 0:width].astype(F32) + came_ref[:, :, pl.ds(x, 1), :, 0:width].astype(F32)).astype(BF)
        for d in range(sy):
            y = lax.rem(at_ref[1] + d, sy)
            outs[sx + d][...] = (kept_ref[pl.ds(y, 1), :, :, :, width:].astype(F32) + came_ref[pl.ds(y, 1), :, :, :, width:].astype(F32)).astype(BF)

    outs = [((sy, sz, 1, wr, width), BF)] * sx + [((1, sz, sx, wr, wide - width), BF)] * sy
    return call(body, (jnp.stack([ix, iy]).astype(jnp.int32), kept, came), outs, "fold_both", 1)


def fold_cross(first, first_came, second, second_came, ix, iy):
    sx, sy = len(first), len(second)
    sz, wr, width = first[0].shape[1], first[0].shape[3], first[0].shape[4]
    other = second[0].shape[4]

    def body(at_ref, *refs):
        one, two, outs = refs[:sx], refs[sx:sx + sy], refs[sx + sy:]
        for d in range(sy):
            y = lax.rem(at_ref[1] + d, sy)
            total = one[0][pl.ds(y, 1)].astype(F32)
            for ref in one[1:]:
                total = total + ref[pl.ds(y, 1)].astype(F32)
            outs[d][...] = total.astype(BF)
        for d in range(sx):
            x = lax.rem(at_ref[0] + d, sx)
            total = two[0][:, :, pl.ds(x, 1)].astype(F32)
            for ref in two[1:]:
                total = total + ref[:, :, pl.ds(x, 1)].astype(F32)
            outs[sy + d][...] = total.astype(BF)

    outs = [((1, sz, 1, wr, width), BF)] * sy + [((1, sz, 1, wr, other), BF)] * sx
    args = (jnp.stack([ix, iy]).astype(jnp.int32), first[0], *first_came, second[0], *second_came)
    return call(body, args, outs, "fold_cross", 1)


def fold_last(first, first_came, second, second_came, iz, after):
    sy, sx = len(first), len(second)
    wr, width = first[0].shape[3:]
    wide = width + second[0].shape[4]

    def body(at_ref, *refs):
        one, two, outs = refs[:sy], refs[sy:sy + sx], refs[sy + sx:]
        for d in range(ZS):
            z = lax.rem(at_ref[0] + d, ZS)
            for sums, cols in ((one, slice(0, width)), (two, slice(width, wide))):
                total = sums[0][:, pl.ds(z, 1)].astype(F32)
                for ref in sums[1:]:
                    total = total + ref[:, pl.ds(z, 1)].astype(F32)
                outs[d][:, :, :, :, cols] = total.astype(BF)

    outs = [((1, 1, 1, wr, wide), BF)] * ZS
    args = (iz.astype(jnp.int32).reshape(1), first[0], *first_came, second[0], *second_came)
    return call(body, args, outs, "fold_last", 1, after)


def passed(pieces, axis):
    return [shift(pieces[d], axis, d) for d in range(1, len(pieces))]


def beside(pieces):
    rows, group = pieces[0].shape

    def body(*refs):
        for d, ref in enumerate(refs[:-1]):
            refs[-1][:, d * group:(d + 1) * group] = ref[...]

    return call(body, tuple(pieces), [((rows, len(pieces) * group), BF)], "beside")[0]


def out_project(place, cat, halves, hidden, vectors):
    rows, width = hidden.shape
    group = width // ZS
    half = width // 2

    def body(place_ref, cat_ref, own_ref, other_ref, hidden_ref, vec_ref, res_ref, n2_ref):
        own = jnp.zeros((rows, half), F32)
        other = jnp.zeros((rows, half), F32)
        for d in range(ZS):
            piece = cat_ref[:, d * group:(d + 1) * group]
            spot = pl.ds(pl.multiple_of(lax.rem(place_ref[0] + ZS - d, ZS) * group, group), group)
            own = own + dot(piece, own_ref[spot, :])
            other = other + dot(piece, other_ref[spot, :])
        first = place_ref[1] == 0
        branch = jnp.concatenate([jnp.where(first, own, other), jnp.where(first, other, own)], 1)
        total = hidden_ref[...].astype(F32) + branch + vec_ref[2:3, :]
        res_ref[:, 0:width] = total
        res_ref[:, width:] = jnp.broadcast_to(vec_ref[15:16, 0:rows], (LANES, rows)).T
        n2, _ = norm_parts(total)
        n2_ref[...] = (n2 * vec_ref[6:7, :] + vec_ref[7:8, :]).astype(BF)

    outs = [((rows, width + LANES), F32), ((rows, width), BF)]
    return call(body, (place, cat, *halves, hidden, vectors), outs, "out_project", 1)


def mlp_parts(weights, ff):
    width = weights[0].shape[0]
    if len(weights) == 2:
        return Part(weights[0], 0, ff), weights[1]
    return Part(weights[0], 0, ff), Part(weights[0], ff + width // 2, ff + width // 2 + width)


def mlp_up(blocks, weights, bias, ff):
    rows, width = blocks[0].shape
    count = len(blocks)
    half = count // 2

    def body(*refs):
        n2_refs, (bias_ref, up_ref, down_ref), (kept_ref, sent_ref, slope_ref, saved_ref) = refs[:count], refs[count:count + 3], refs[-4:]
        for j in range(count):
            saved_ref[j * rows:(j + 1) * rows, ff:] = n2_refs[j][...]
            pre = dot(n2_refs[j][...], up_ref[...]) + bias_ref[0:1, 0:ff]
            square = pre * pre
            tanh = jnp.tanh(GC * pre * (1.0 + 0.044715 * square))
            half_one = 0.5 * (1.0 + tanh)
            act = (pre * half_one).astype(BF)
            slope_ref[j] = (half_one + 0.5 * pre * (1.0 - tanh * tanh) * (GC + GC * 0.134145 * square)).astype(BF)
            saved_ref[j * rows:(j + 1) * rows, 0:ff] = act
            part = dot(act, down_ref[...])
            if j < half:
                kept_ref[j] = part + bias_ref[1:2, 0:width] if j == 0 else part
            else:
                sent_ref[j - half] = part.astype(BF)

    outs = [((half, rows, width), F32), ((half, rows, width), BF), ((count, rows, ff), BF), ((count * rows, ff + width), BF)]
    return call(body, (*blocks, bias, *mlp_parts(weights, ff)), outs, "mlp_up")


def finish(terms, residual, targets, scale):
    rows, width = targets.shape[1:]
    size = len(terms)

    def body(scale_ref, *refs):
        res_ref, target_ref, out_ref, err_ref, both_ref, gmlp_ref = refs[size:]
        valid = res_ref[:, width:width + 1]
        final = res_ref[:, 0:width]
        for ref in refs[:size]:
            final = final + ref[...].astype(F32)
        out_ref[...] = final.astype(BF)
        deviation = final - target_ref[0].astype(F32)
        grad = valid * (target_ref[1].astype(F32) + deviation * scale_ref[0])
        both_ref[0] = res_ref[:, 0:width]
        both_ref[1] = grad
        low = grad.astype(BF)
        gmlp_ref[...] = low
        err_ref[0:1, :] = jnp.sum(valid * deviation * deviation, 0, keepdims=True)
        err_ref[1:2, :] = jnp.sum(low.astype(F32), 0, keepdims=True)

    outs = [((rows, width), BF), ((2, width), F32), ((2, rows, width), F32), ((rows, width), BF)]
    return call(body, (scale, *terms, residual, targets), outs, "finish", 1)


def mlp_back(grads, weights, slope):
    rows, width = grads[0].shape
    count = len(grads)
    half = count // 2
    ff = slope.shape[2]

    def body(*refs):
        g_refs, (slope_ref, up_ref, down_ref), (kept_ref, sent_ref, gpre_ref, g_all) = refs[:count], refs[count:count + 3], refs[-4:]
        for j in range(count):
            g_all[j * rows:(j + 1) * rows, :] = g_refs[j][...]
            gpre = (dot_nt(g_refs[j][...], down_ref[...]) * slope_ref[j].astype(F32)).astype(BF)
            gpre_ref[j * rows:(j + 1) * rows, :] = gpre
            part = dot_nt(gpre, up_ref[...])
            if j < half:
                kept_ref[j] = part
            else:
                sent_ref[j - half] = part.astype(BF)

    outs = [((half, rows, width), F32), ((half, rows, width), BF), ((count * rows, ff), BF), ((count * rows, width), BF)]
    return call(body, (*grads, slope, *mlp_parts(weights, ff)), outs, "mlp_back")


def mlp_weights(place, grads, saved, gpre, size, after):
    width = grads.shape[1]
    ff = gpre.shape[1]
    joined = ff == width
    down, up = ff // size, width // size
    direct = down % LANES == 0 and up % LANES == 0

    def body(place_ref, g_ref, saved_ref, gpre_ref, *refs):
        outs, sums_ref, rest = refs[:size if joined else 2 * size], refs[size if joined else 2 * size], refs[size + 1 if joined else 2 * size + 1:]
        if not direct:
            rest[0][...] = dot_tn(saved_ref[:, 0:ff], g_ref[...])
            rest[1][...] = dot_tn(saved_ref[:, ff:], gpre_ref[...])
        for d in range(size):
            y = lax.rem(place_ref[0] + d, size)
            if direct:
                first = dot_tn(saved_ref[:, pl.ds(pl.multiple_of(y * down, LANES), down)], g_ref[...])
                second = dot_tn(saved_ref[:, pl.ds(pl.multiple_of(ff + y * up, LANES), up)], gpre_ref[...])
            else:
                first = rest[0][pl.ds(pl.multiple_of(y * down, 16), down), :]
                second = rest[1][pl.ds(pl.multiple_of(y * up, 16), up), :]
            if joined:
                outs[d][:, 0:width] = first.astype(BF)
                outs[d][:, width:] = second.astype(BF)
            else:
                outs[d][...] = first.astype(BF)
                outs[size + d][...] = second.astype(BF)
        sums_ref[...] = jnp.sum(gpre_ref[...].astype(F32), 0, keepdims=True)

    outs = [((up, 2 * width), BF)] * size if joined else [((down, width), BF)] * size + [((up, ff), BF)] * size
    scratch = [] if direct else [pltpu.VMEM((ff, width), F32), pltpu.VMEM((width, ff), F32)]
    *pieces, sums = call(body, (place, grads, saved, gpre), outs + [((1, ff), F32)], "mlp_weights", 1, after, scratch, 20)
    return [pieces[i:i + size] for i in range(0, len(pieces), size)], sums


def fold_first(own, came, after):
    def body(own_ref, *refs):
        total = own_ref[...].astype(F32)
        for ref in refs[:-1]:
            total = total + ref[...].astype(F32)
        refs[-1][...] = total.astype(BF)

    return call(body, (own, *came), [(own.shape, BF)], "fold_first", 0, after)[0]


def out_back(place, terms, res_and_grad, vectors, ctx_cat, halves, after):
    rows, width = res_and_grad.shape[1:]
    group = width // ZS
    size = len(terms)

    def body(place_ref, *refs):
        (both_ref, vec_ref, cat_ref, own_ref, other_ref, gres_ref), gctx_refs, (gw_ref, sums_ref) = refs[size:size + 6], refs[size + 6:size + 10], refs[size + 10:]
        gn2 = refs[0][...]
        for ref in refs[1:size]:
            gn2 = gn2 + ref[...].astype(F32)
        n2, rstd = norm_parts(both_ref[0])
        gres = both_ref[1] + norm_back(n2, rstd, gn2, vec_ref[6:7, :])
        gres_ref[...] = gres
        branch = gres.astype(BF)
        left, right = branch[:, 0:width // 2], branch[:, width // 2:]
        first = place_ref[1] == 0
        own, other = jnp.where(first, left, right), jnp.where(first, right, left)
        for d in range(ZS):
            spot = pl.ds(pl.multiple_of(lax.rem(place_ref[0] + d, ZS) * group, group), group)
            gctx_refs[d][...] = (dot_nt(own, own_ref[spot, :]) + dot_nt(other, other_ref[spot, :])).astype(BF)
        for d in range(ZS):
            spot = pl.ds(pl.multiple_of(lax.rem(place_ref[0] + ZS - d, ZS) * group, group), group)
            gw_ref[spot, :] = dot_tn(cat_ref[:, d * group:(d + 1) * group], branch).astype(BF)
        rowsum = lambda v: jnp.sum(v, 0, keepdims=True)
        sums_ref[0:1, :] = rowsum(branch.astype(F32))
        sums_ref[1:2, :] = rowsum(gn2 * n2)
        sums_ref[2:3, :] = rowsum(gn2)

    outs = [((rows, width), F32)] + [((rows, group), BF)] * ZS + [((width, width), BF), ((3, width), F32)]
    args = (place, *terms, res_and_grad, vectors, ctx_cat, *halves)
    return call(body, args, outs, "out_back", 1, after)


def join_back(place, terms, dq, one):
    total, group = dq.shape
    width = one.shape[0]
    rows = total // ZS
    size = len(terms)
    cols = 3 * group

    def body(place_ref, *refs):
        dq_ref, w_ref, gj_ref, gn1_ref = refs[size:size + 4]
        out_refs = refs[size + 4:]
        dkv = refs[0][...].astype(F32)
        for ref in refs[1:size]:
            dkv = dkv + ref[...].astype(F32)
        gj_ref[:, 0:2 * group] = dkv.astype(BF)
        gj_ref[:, 2 * group:] = dq_ref[...]
        gn1_ref[...] = dot_nt(gj_ref[...], w_ref[:, 0:cols])
        for d in range(ZS):
            spot = pl.ds(pl.multiple_of(lax.rem(place_ref[0] + d, ZS) * rows, rows), rows)
            out_refs[d][...] = gn1_ref[spot, :].astype(out_refs[d].dtype)

    outs = [((total, cols), BF), ((total, width), F32), ((rows, width), F32)] + [((rows, width), BF)] * (ZS - 1)
    return call(body, (place, *terms, dq, one), outs, "join_back", 1)


def weights_back(place, saved, grad_joined, gn1, out_sums, fin_sums, up_rows, gw_out, wr, devices):
    total, cols = grad_joined.shape
    width = gn1.shape[1]
    rows = total // ZS
    group = cols // 3
    upc = up_rows.shape[0]
    chips = width // (2 * wr)
    wide = width + cols + HEAD_DIM + LANES
    slots = -(-devices // wr)

    def body(place_ref, saved_ref, gj_ref, gn1_ref, sums_ref, fin_ref, up_ref, gw_ref, kept_ref, sent_ref, vec, full):
        gain_sum = jnp.zeros((1, width), F32)
        for z in range(ZS):
            spot = slice(z * rows, (z + 1) * rows)
            normed, _ = norm_parts(saved_ref[spot, width:].astype(F32))
            gain_sum = gain_sum + jnp.sum(gn1_ref[spot, :] * normed, 0, keepdims=True)
        joined_sums = jnp.sum(gj_ref[...].astype(F32), 0, keepdims=True)
        vec[...] = jnp.zeros_like(vec)
        hd = HEAD_DIM
        for g in range(ZS):
            here = place_ref[0] == g
            at = g * group
            vec[0:1, at:at + group] = jnp.where(here, joined_sums[:, 2 * group:], 0.0)
            vec[1:2, at:at + 2 * hd] = jnp.where(here, joined_sums[:, 4 * hd:6 * hd], 0.0)
            vec[1:2, at + 2 * hd:at + 3 * hd] = jnp.where(here, joined_sums[:, 3 * hd:4 * hd], 0.0)
        vec[2:3, :] = sums_ref[0:1, :]
        vec[3:4, :] = fin_ref[1:2, :]
        vec[4:5, :] = gain_sum
        vec[5:6, :] = jnp.sum(gn1_ref[...], 0, keepdims=True)
        vec[6:8, :] = sums_ref[1:3, :]
        vec[8:8 + upc, :] = up_ref[...]
        error = jnp.sum(fin_ref[0:1, :], -1, keepdims=True)
        high = error.astype(BF).astype(F32)
        turn = lax.rem(lax.broadcasted_iota(jnp.int32, (1, width), 1), wr)
        for s in range(slots):
            vec[16 + s:17 + s, :] = jnp.where(turn + s * wr == place_ref[2], high, 0.0)
        vec[16 + slots:17 + slots, :] = jnp.where(turn == 0, error - high, 0.0)
        full[:, 0:width] = gw_ref[...].astype(F32)
        full[:, width:width + cols] = dot_tn(saved_ref[:, 0:width], gj_ref[...])
        full[:, width + cols:width + cols + hd] = jnp.zeros((width, hd), F32)
        full[:, width + cols + hd:] = vec[...].T
        for c in range(2):
            @pl.when(place_ref[1] == c)
            def _():
                for chip in range(chips):
                    at = chip * 2 * wr
                    kept_ref[chip] = full[at + c * wr:at + (c + 1) * wr, :].astype(BF)
                    sent_ref[chip] = full[at + (1 - c) * wr:at + (2 - c) * wr, :].astype(BF)

    outs = [((chips, wr, wide), BF)] * 2
    scratch = [pltpu.VMEM((LANES, width), F32), pltpu.VMEM((width, wide), F32)]
    return call(body, (place, saved, grad_joined, gn1, out_sums, fin_sums, up_rows, gw_out), outs, "weights_back", 1, scratch=scratch, mib=20)


def input_back(terms, hidden, vectors, grad_res):
    rows, width = hidden.shape

    def body(t0, t1, t2, t3, hidden_ref, gain_ref, gres_ref, out_ref):
        back = t0[...] + t1[...].astype(F32) + t2[...].astype(F32) + t3[...].astype(F32)
        normed, rstd = norm_parts(hidden_ref[...].astype(F32))
        out_ref[...] = gres_ref[...] + norm_back(normed, rstd, back, gain_ref[4:5, :])

    return call(body, (terms[0], *terms[1:], hidden, vectors, grad_res), [((rows, width), F32)], "input_back")[0]


def unpack_one(place, pieces, after):
    rows, wide = pieces[0].shape[-2:]
    hd = HEAD_DIM
    group = 3 * hd
    width = ZS * group

    def body(place_ref, p0, p1, p2, p3, qkv_ref, vec_ref, out_ref, held_ref):
        for d, piece in enumerate((p0, p1, p2, p3)):
            held_ref[pl.ds(lax.rem(place_ref[0] + ZS - d, ZS), 1)] = piece[...].reshape(1, rows, wide).astype(F32)
        vec_total = jnp.zeros((rows, LANES), F32)
        out_total = jnp.zeros((rows, width), F32)
        for g in range(ZS):
            k = width + g * group
            v = 2 * width + g * group
            at = width
            qkv_ref[:, k:k + 3 * hd] = held_ref[g, :, at:at + 3 * hd]
            qkv_ref[:, v + 2 * hd:v + 3 * hd] = held_ref[g, :, at + 3 * hd:at + 4 * hd]
            qkv_ref[:, v:v + 2 * hd] = held_ref[g, :, at + 4 * hd:at + 6 * hd]
            qkv_ref[:, g * group:g * group + 3 * hd] = held_ref[g, :, at + 6 * hd:at + 9 * hd]
            vec_total = vec_total + held_ref[g, :, at + 10 * hd:]
            out_total = out_total + held_ref[g, :, 0:width]
        vec_ref[...] = vec_total
        out_ref[...] = out_total

    outs = [((rows, 3 * width), F32), ((rows, LANES), F32), ((rows, width), F32)]
    return call(body, (place, *pieces), outs, "unpack_one", 1, after, scratch=[pltpu.VMEM((ZS, rows, wide), F32)])


def per_device(hidden_in, w_qkv, q_bias, v_bias, w_out, out_bias, w_up, up_bias, w_down, down_bias, ln1_gain, ln1_bias, ln2_gain, ln2_bias, segment_ids, padding_mask, teacher, cotangent):
    sy, sz, sx = (lax.axis_size(a) for a in ("y", "z", "x"))
    iy, iz, ix, core = (lax.axis_index(a) for a in ("y", "z", "x", "core"))
    device = ((iy * sz + iz) * sx + ix) * 2 + core
    devices = sy * sz * sx * 2
    rows, width = hidden_in.shape[1:]
    wr = w_qkv.shape[0]
    ffd = w_down.shape[0]
    ff = sy * sz * ffd
    upc = ffd // wr
    wcols = 9 * HEAD_DIM
    group = width // sz
    place = iz.astype(jnp.int32).reshape(1)
    at_zc = jnp.stack([iz, core]).astype(jnp.int32)
    yplace = iy.astype(jnp.int32).reshape(1)

    def from_z(value):
        return [value] + [shift(value, "z", d) for d in range(1, sz)]

    def to_z(pieces):
        return [pieces[0]] + [shift(pieces[d], "z", d) for d in range(1, sz)]

    def cut_z(value):
        return [lax.dynamic_slice_in_dim(value, lax.rem(iz + d, sz), 1, 0) for d in range(sz)]

    flat = jnp.concatenate([jnp.stack([q_bias, v_bias, out_bias, down_bias, ln1_gain, ln1_bias, ln2_gain, ln2_bias]), up_bias.reshape(upc, wr)])
    hidden = hidden_in[0]
    pieces = from_z(hidden)
    targets = jnp.concatenate([teacher, cotangent], 0)
    one = arrange(to_z(cut_z(pack_one(w_qkv, flat, jnp.concatenate([segment_ids, padding_mask])))), iz, 0)
    one = gather(one[None, :, None], "x", 2, after=[pieces[1]])
    one = gather(one, "y", 0, after=pieces[2:])[:, :, :, None]
    one = gather(one, "core", 3).reshape(width, -1)

    at_xc = jnp.stack([ix, core]).astype(jnp.int32)
    ups = list(pack_up(at_xc, w_up, w_out, ffd, sx))
    for d in range(1, 2 * sx):
        dc, dx = d // sx, d % sx
        pairs = [(x * 2 + c, (x + dx) % sx * 2 + (c + dc) % 2) for x in range(sx) for c in range(2)]
        ups[d] = lax.ppermute(ups[d], ("x", "core"), pairs)
    weights = [join_up(at_xc, ups, w_down)]
    if ffd != 2 * sx * wr:
        weights = weights + [w_down]
    weights = [lax.all_gather(member, ("y", "z"), axis=0, tiled=True) for member in weights]

    vec = one[:, wcols:]
    vectors = jnp.concatenate([vec[:, :15].T.astype(F32), jnp.pad(padding_mask.astype(F32), ((0, 0), (0, width - rows)))])
    ub = vectors[8:8 + upc].reshape(upc, sy * sz, sx * 2, wr)
    ub = lax.dynamic_index_in_dim(ub, ix * 2 + core, 2, keepdims=False).transpose(1, 0, 2).reshape(1, ff)
    wide = max(ff, width)
    biases = jnp.concatenate([jnp.pad(ub, ((0, 0), (0, wide - ff))), jnp.pad(vectors[3:4], ((0, 0), (0, wide - width)))])
    count = jnp.sum(vectors[8 + upc]) / wr
    seg = lax.dynamic_index_in_dim(vec.reshape(sy, sz * sx * 2, wr, LANES), iy, 0, keepdims=False)[:, :2, HEAD_DIM:].astype(F32).reshape(sz * sx * 2, rows)
    spots = [(lax.rem(ix + sx - d, sx), core) for d in range(sx)]
    spots = spots + [(at, 1 - core) for at, _ in spots]
    order = jnp.stack([at * 2 + c for at, c in spots] + [iz]).astype(jnp.int32)

    kv, q, saved_one = project(place, pieces, one, vectors)
    kvs = spread_tokens(kv)
    *ctx_parts, ctx_tot = attend(order, q, seg, kvs, after=[biases])
    ctx_cat = beside(to_z(ctx_parts))
    wo = [held(Part(weights[0], ff, ff + width // 2), [ctx_cat])]
    wo = wo + [shift(wo[0], "core", 1)]
    residual, n2_low = out_project(at_zc, ctx_cat, wo, hidden, vectors)
    kept, sent, slope, saved = mlp_up(spread_tokens(n2_low), weights, biases, ff)
    layer_out, fin_sums, res_and_grad, grad_mlp = finish(fold_tokens(kept, sent), residual, targets, (2.0 / (count * width)).reshape(1))

    kept, sent, grad_pre, grads = mlp_back(spread_tokens(grad_mlp), weights, slope)
    gn2_terms = fold_tokens(kept, sent)
    gw_mlp, up_sums = mlp_weights(yplace, grads, saved, grad_pre, sy, after=gn2_terms[:1])
    gw_came = [passed(members, "y") for members in gw_mlp]
    grad_res, *gctx, gw_out, out_sums = out_back(at_zc, gn2_terms, res_and_grad, vectors, ctx_cat, wo, after=[up_sums])
    dq, dkv_kept, dkv_sent, done = attend_back(order, q, to_z(gctx), ctx_tot, seg, kvs)
    gw_sums = [lax.psum_scatter(fold_first(members[0], came, [done]), "z", scatter_dimension=0, tiled=True) for members, came in zip(gw_mlp, gw_came)]
    grad_joined, gn1, *gn1_parts = join_back(place, fold_tokens(dkv_kept, dkv_sent, BF), dq, one)
    gn1_parts = to_z(gn1_parts)
    input_grad = input_back(gn1_parts, hidden, vectors, grad_res)

    up_rows = jnp.zeros((upc, sy * sz, sx * 2, wr), F32)
    up_rows = lax.dynamic_update_slice_in_dim(up_rows, up_sums.reshape(sy * sz, upc, wr).transpose(1, 0, 2)[:, :, None], ix * 2 + core, 2).reshape(upc, width)
    places = jnp.stack([iz, core, device]).astype(jnp.int32)
    kept, sent = weights_back(places, saved_one, grad_joined, gn1, out_sums, fin_sums, up_rows, gw_out, wr, devices)
    third = fold_both(kept.reshape(sy, sz, sx, wr, -1), shift(sent, "core", 1).reshape(sy, sz, sx, wr, -1), ix, iy, width)
    third = fold_cross(third[:sx], passed(third[:sx], "x"), third[sx:], passed(third[sx:], "y"), ix, iy)
    third = fold_last(third[:sy], passed(third[:sy], "y"), third[sy:], passed(third[sy:], "x"), iz, after=[gn1_parts[2], gn1_parts[3]])
    ready = third[0][0, 0, 0, :, :LANES]
    gw_sums = [held(member, [ready]) for member in gw_sums]
    third = [third[0]] + passed(third, "z")

    gw_down = gw_sums[0][:, :width].astype(F32)
    gw_up = gw_sums[-1][:, -ff:].reshape(1, 1, sx, 2, wr, ff)
    up_x = [lax.dynamic_slice_in_dim(gw_up, lax.rem(ix + d, sx), 1, 2) for d in range(sx)]
    gw_up = arrange([up_x[0]] + [shift(up_x[d], "x", d) for d in range(1, sx)], ix, 2)
    gw_up = arrange([lax.dynamic_slice_in_dim(gw_up, core, 1, 3), shift(lax.dynamic_slice_in_dim(gw_up, 1 - core, 1, 3), "core", 1)], core, 3)
    gw_up = gw_up.reshape(sx, 2, wr, sy * sz, ffd).transpose(2, 3, 0, 1, 4).reshape(wr, -1).astype(F32)

    grad_w_qkv, sums, gw_out = unpack_one(place, third, after=[gw_up])
    sums = sums.T
    loss = jnp.sum(sums[16:17 + -(-devices // wr)]) / (count * width)
    return (
        layer_out[None], loss, input_grad[None], grad_w_qkv, sums[0], sums[1], gw_out, sums[2],
        gw_up, sums[8:8 + upc].reshape(-1), gw_down, sums[3], sums[4], sums[5], sums[6], sums[7],
    )


def solution(mesh):
    seq, ctx = mesh.shape["seq"], mesh.shape["ctx"]
    grid = Mesh(mesh.devices.reshape(seq, ZS, ctx // (2 * ZS), 2), ("y", "z", "x", "core"))
    every = ("y", "z", "x", "core")
    matrix, vector = P(every, None), P(every)
    tokens = P("y", ("z", "x", "core"), None)
    marks = P("y", ("z", "x", "core"))
    return jax.shard_map(
        per_device,
        mesh=grid,
        in_specs=(tokens, matrix, vector, vector, matrix, vector, matrix, vector, matrix, vector, vector, vector, vector, vector, marks, marks, tokens, tokens),
        out_specs=(tokens, P(), tokens, matrix, vector, vector, matrix, vector, matrix, vector, matrix, vector, vector, vector, vector, vector),
        check_vma=False,
    )
```

```python
import functools

import jax
import jax.numpy as jnp
from jax import lax
from jax.experimental import pallas as pl
from jax.experimental.pallas import tpu as pltpu
from jax.sharding import Mesh
from jax.sharding import PartitionSpec as P

HEADS = 12
HEAD_DIM = 64
ZS = 4
BF = jnp.bfloat16
F32 = jnp.float32
NEG = -1e30
LANES = 128


def shift(value, axis, step):
    size = lax.axis_size(axis)
    return lax.ppermute(value, axis, [(a, (a + step) % size) for a in range(size)])


def gather(value, axis, dim, after=()):
    size = lax.axis_size(axis)
    return arrange([value] + [shift(value, axis, d) for d in range(1, size)], lax.axis_index(axis), dim, after)


def scatter_sum(value, axis, dim, last=BF, after=()):
    size = lax.axis_size(axis)
    place = lax.axis_index(axis)

    def cut(d):
        return lax.dynamic_slice_in_dim(value, lax.rem(place + d, size), 1, dim)

    came = [shift(cut(d), axis, d) for d in range(1, size)]

    def body(place_ref, value_ref, *refs):
        index = (slice(None),) * dim + (pl.ds(place_ref[0], 1),)
        total = value_ref[index].astype(F32)
        for ref in refs[:size - 1]:
            total = total + ref[...].astype(F32)
        refs[-1][...] = total.astype(last)

    vmem = pl.BlockSpec(memory_space=pltpu.VMEM)
    return pl.pallas_call(
        body,
        in_specs=[pl.BlockSpec(memory_space=pltpu.SMEM)] + [vmem] * size + [pl.BlockSpec(memory_space=pl.ANY)] * len(after),
        out_shape=jax.ShapeDtypeStruct(came[0].shape, last),
        compiler_params=params(),
        cost_estimate=SMALL,
        name="scatter_sum",
    )(place.astype(jnp.int32).reshape(1), value, *came, *after)


def spread_tokens(value):
    some = [value] + [shift(value, "x", d) for d in range(1, lax.axis_size("x"))]
    return some + [shift(member, "core", 1) for member in some]


def fold_tokens(kept, sent, own=F32):
    came = shift(sent, "core", 1)
    size = kept.shape[0]
    shape = kept.shape[1:]

    def body(kept_ref, came_ref, *outs):
        for d in range(size):
            outs[d][...] = (kept_ref[d] + came_ref[d].astype(F32)).astype(outs[d].dtype)

    terms = call(body, (kept, came), [(shape, BF if d else own) for d in range(size)], "fold_tokens")
    return [terms[0]] + [shift(terms[d], "x", -d) for d in range(1, size)]


def dot(a, b):
    return jnp.dot(a, b, preferred_element_type=F32)


def dot_nt(a, b):
    return lax.dot_general(a, b, (((1,), (1,)), ((), ())), preferred_element_type=F32)


def dot_tn(a, b):
    return lax.dot_general(a, b, (((0,), (0,)), ((), ())), preferred_element_type=F32)


SMALL = pl.CostEstimate(flops=1, bytes_accessed=1, transcendentals=0)


def params(mib=6):
    return pltpu.CompilerParams(vmem_limit_bytes=mib * 1024 * 1024)


def pack_one(w_qkv, flat, marks):
    rows, width = w_qkv.shape[0], w_qkv.shape[1] // 3
    group = width // ZS
    hd = HEAD_DIM
    upc = flat.shape[0] - 8

    def body(qkv_ref, flat_ref, marks_ref, one_ref, vec):
        vec[...] = jnp.zeros_like(vec)
        vec[0:8 + upc, 0:rows] = flat_ref[...].astype(F32)
        count = jnp.sum(marks_ref[1:2, :].astype(F32), -1, keepdims=True)
        lane = lax.broadcasted_iota(jnp.int32, (LANES, LANES), 1)
        vec[...] = jnp.where(lane == 8 + upc, count, vec[...].T)
        ids = marks_ref[0:1, :].astype(F32)
        vec[0:1, hd:] = ids[:, 0:hd]
        vec[1:2, hd:] = ids[:, hd:]
        cols = vec[0:rows, :].astype(BF)
        for g in range(ZS):
            k = width + g * group
            v = 2 * width + g * group
            one_ref[g, :, 0:3 * hd] = qkv_ref[:, k:k + 3 * hd]
            one_ref[g, :, 3 * hd:4 * hd] = qkv_ref[:, v + 2 * hd:v + 3 * hd]
            one_ref[g, :, 4 * hd:6 * hd] = qkv_ref[:, v:v + 2 * hd]
            one_ref[g, :, 6 * hd:9 * hd] = qkv_ref[:, g * group:g * group + 3 * hd]
            one_ref[g, :, 9 * hd:11 * hd] = cols

    outs = [((ZS, rows, 11 * hd), BF)]
    return call(body, (w_qkv, flat, marks), outs, "pack_one", scratch=[pltpu.VMEM((LANES, LANES), F32)])[0]


def pack_up(place, w_up, w_out, ffd, sx):
    rows, width = w_out.shape
    half = width // 2
    blocks = w_up.shape[1] // (2 * sx * ffd)
    ff = blocks * ffd

    def body(at_ref, up_ref, out_ref, *refs):
        outs, every = refs[:-1], refs[-1]
        for c in range(2):
            for x in range(sx):
                for b in range(blocks):
                    at = ((b * sx + x) * 2 + c) * ffd
                    every[c * sx + x, :, b * ffd:(b + 1) * ffd] = up_ref[:, at:at + ffd]
                every[c * sx + x, :, ff:] = out_ref[:, c * half:(c + 1) * half]
        for dc in range(2):
            core = at_ref[1] if dc == 0 else 1 - at_ref[1]
            for dx in range(sx):
                outs[dc * sx + dx][...] = every[core * sx + lax.rem(at_ref[0] + dx, sx)]

    outs = [((rows, ff + half), BF)] * (2 * sx)
    return call(body, (place, w_up, w_out), outs, "pack_up", 1, scratch=[pltpu.VMEM((2 * sx, rows, ff + half), BF)])


def join_up(place, pieces, w_down):
    sx = len(pieces) // 2
    rows, cols = pieces[0].shape
    joined = w_down.shape[0] == 2 * sx * rows
    wide = cols + w_down.shape[1] if joined else cols

    def body(at_ref, *refs):
        out = refs[-1]
        for dc in range(2):
            core = at_ref[1] if dc == 0 else 1 - at_ref[1]
            for dx in range(sx):
                spot = lax.rem(at_ref[0] + sx - dx, sx) * 2 + core
                out[pl.ds(spot, 1), :, 0:cols] = refs[dc * sx + dx][...].reshape(1, rows, cols)
        if joined:
            out[:, :, cols:] = refs[2 * sx][...]

    args = (place, *pieces, w_down.reshape(2 * sx, rows, -1)) if joined else (place, *pieces)
    return call(body, args, [((2 * sx, rows, wide), BF)], "join_up", 1)[0].reshape(2 * sx * rows, wide)


def open_sums(place, sums, width, sx, wr, after):
    joined = len(sums) == 1
    rows = sums[0].shape[0]
    ff = sums[-1].shape[1] - width if joined else sums[-1].shape[1]
    first = width if joined else 0

    def body(at_ref, *refs):
        ups, down_ref, outs = refs[len(sums) - 1], refs[len(sums)], refs[len(sums) + 1:]
        if joined:
            for i in range(2 * sx):
                down_ref[i * wr:(i + 1) * wr, :] = ups[i, :, 0:width].astype(F32)
        else:
            down_ref[...] = refs[0][...].astype(F32)
        for dc in range(2):
            core = at_ref[1] if dc == 0 else 1 - at_ref[1]
            for dx in range(sx):
                outs[dc * sx + dx][...] = ups[lax.rem(at_ref[0] + dx, sx) * 2 + core][:, first:]

    outs = [((rows, width), F32)] + [((wr, ff), BF)] * (2 * sx)
    args = (place, *sums[:-1], sums[-1].reshape(2 * sx, wr, -1))
    down, *pieces = call(body, args, outs, "open_sums", 1, after)
    return down, pieces


def close_up(place, pieces, ffd):
    sx = len(pieces) // 2
    wr, ff = pieces[0].shape

    def body(at_ref, *refs):
        out, every = refs[-2:]
        for dc in range(2):
            core = at_ref[1] if dc == 0 else 1 - at_ref[1]
            for dx in range(sx):
                every[lax.rem(at_ref[0] + sx - dx, sx) * 2 + core] = refs[dc * sx + dx][...].astype(F32)
        for i in range(2 * sx):
            for b in range(ff // ffd):
                at = (b * 2 * sx + i) * ffd
                out[:, at:at + ffd] = every[i, :, b * ffd:(b + 1) * ffd]

    return call(body, (place, *pieces), [((wr, 2 * sx * ff), F32)], "close_up", 1, scratch=[pltpu.VMEM((2 * sx, wr, ff), F32)])[0]


def held(value, after):
    def body(value_ref, out_ref):
        out_ref[...] = value_ref[...]

    array = value.value if isinstance(value, Part) else value
    shape = (array.shape[0], value.last - value.first) if isinstance(value, Part) else array.shape
    return call(body, (value,), [(shape, array.dtype)], "held", 0, after)[0]


def arrange(pieces, place, dim, after=()):
    size = len(pieces)
    shape = list(pieces[0].shape)
    shape[dim] = size

    def body(place_ref, *refs):
        out = refs[-1]
        for d in range(size):
            spot = lax.rem(place_ref[0] + size - d, size)
            index = (slice(None),) * dim + (pl.ds(spot, 1),)
            out[index] = refs[d][...]

    return pl.pallas_call(
        body,
        in_specs=[pl.BlockSpec(memory_space=pltpu.SMEM)] + [pl.BlockSpec(memory_space=pltpu.VMEM)] * size + [pl.BlockSpec(memory_space=pl.ANY)] * len(after),
        out_shape=jax.ShapeDtypeStruct(tuple(shape), pieces[0].dtype),
        compiler_params=params(),
        cost_estimate=SMALL,
        name="arrange",
    )(place.astype(jnp.int32).reshape(1), *pieces, *after)


def project(place, pieces, one, vectors):
    rows, width = pieces[0].shape
    total = ZS * rows
    hd = HEAD_DIM
    group = 3 * hd

    def body(place_ref, h0, h1, h2, h3, w_ref, vec_ref, kv_ref, q_ref, saved_ref):
        qb = jnp.zeros((1, group), F32)
        vb = jnp.zeros((1, group), F32)
        for g in range(ZS):
            here = place_ref[0] == g
            qb = jnp.where(here, vec_ref[0:1, g * group:(g + 1) * group], qb)
            vb = jnp.where(here, vec_ref[1:2, g * group:(g + 1) * group], vb)
        for d, piece in enumerate((h0, h1, h2, h3)):
            spot = pl.ds(pl.multiple_of(lax.rem(place_ref[0] + ZS - d, ZS) * rows, rows), rows)
            saved_ref[spot, width:] = piece[...]
            normed, _ = norm_parts(piece[...].astype(F32))
            n1 = (normed * vec_ref[4:5, :] + vec_ref[5:6, :]).astype(BF)
            saved_ref[spot, 0:width] = n1
            joined = dot(n1, w_ref[:, 0:9 * hd])
            kv_ref[spot, 0:3 * hd] = joined[:, 0:3 * hd].astype(BF)
            kv_ref[spot, 3 * hd:4 * hd] = (joined[:, 3 * hd:4 * hd] + vb[:, 2 * hd:]).astype(BF)
            kv_ref[spot, 4 * hd:6 * hd] = (joined[:, 4 * hd:6 * hd] + vb[:, 0:2 * hd]).astype(BF)
            q = (joined[:, 6 * hd:9 * hd] + qb).astype(BF).astype(F32) * 0.125
            q_ref[spot, 0:3 * hd] = q.astype(BF)
            q_ref[spot, 3 * hd:4 * hd] = jnp.zeros((rows, hd), BF)

    outs = [((total, 6 * hd), BF), ((total, 4 * hd), BF), ((total, 2 * width), BF)]
    return call(body, (place, pieces[0], *pieces[1:], one, vectors), outs, "project", 1)


def fill_keys(kv_refs, keys, rows):
    for j, ref in enumerate(kv_refs):
        for z in range(ZS):
            at = (z * len(kv_refs) + j) * rows
            keys[at:at + rows, :] = ref[z * rows:(z + 1) * rows, :]


def turn_segments(order, seg_ref, turned, count):
    turned[...] = jnp.zeros_like(turned)
    for z in range(ZS):
        for j in range(count):
            turned[z * count + j:z * count + j + 1, :] = seg_ref[pl.ds(z * count + order[j], 1), :]
    queries = jnp.concatenate([turned[z * count:z * count + 1, :] for z in range(ZS)], 1)
    turned[...] = turned[...].T
    return queries


def fill_bias(order, queries, turned, bias, z, count, rows):
    for j in range(count):
        same = turned[:, z * count + j:z * count + j + 1] == queries[:, z * rows:]
        bias[j * rows:(j + 1) * rows, z * rows:] = jnp.where(same, 0.0, NEG)
        key = lax.broadcasted_iota(jnp.int32, (rows, rows), 0) + order[j] * rows
        query = lax.broadcasted_iota(jnp.int32, (rows, rows), 1) + order[0] * rows
        ok = same[:, 0:rows] & (key <= query)
        bias[j * rows:(j + 1) * rows, z * rows:(z + 1) * rows] = jnp.where(ok, 0.0, NEG)


def head_parts(q_ref, keys, z, span, lower_q, lower_k):
    at = slice(z * span, (z + 1) * span)
    k01, kv2, v01 = (keys[at, i * LANES:(i + 1) * LANES] for i in range(3))
    one = jnp.ones_like(k01)
    return (k01, k01, kv2), (jnp.where(lower_k, v01, one), jnp.where(lower_k, one, v01), jnp.where(lower_k, one, kv2))


def attend_kernel(order, q_ref, seg_ref, *rest):
    count = len(rest) - 9
    kv_refs, low_refs, both_ref, (keys, bias, acc, turned) = rest[:count], rest[count:count + 4], rest[count + 4], rest[count + 5:]
    ctx_ref, tot_ref = both_ref.at[0], both_ref.at[1]
    total = q_ref.shape[0]
    rows = total // ZS
    span = count * rows
    fill_keys(kv_refs, keys, rows)
    queries = turn_segments(order, seg_ref, turned, count)
    lower_q = lax.broadcasted_iota(jnp.int32, (total, LANES), 1) < HEAD_DIM
    lower_k = lax.broadcasted_iota(jnp.int32, (span, LANES), 1) < HEAD_DIM
    q01, q2 = q_ref[:, 0:LANES], q_ref[:, LANES:2 * LANES]
    none = jnp.zeros_like(q01)
    qs = (jnp.where(lower_q, q01, none), jnp.where(lower_q, none, q01), q2)
    for z in range(ZS):
        fill_bias(order, queries, turned, bias, z, count, rows)
        ks, vs = head_parts(q_ref, keys, z, span, lower_q, lower_k)
        for h in range(3):
            scores = dot_nt(ks[h], qs[h][z * rows:, :]) + bias[:, z * rows:]
            expo = jnp.exp(scores).astype(BF)
            part = dot_tn(vs[h], expo)
            if z == 0:
                acc[h] = part
            else:
                acc[h, :, z * rows:] += part
    u0, u1, u2 = (acc[h].T for h in range(3))
    unnormed = jnp.where(lower_q, u0, u1)
    totals = jnp.where(lower_q, pltpu.roll(u0, HEAD_DIM, 1), pltpu.roll(u1, HEAD_DIM, 1))
    ctx = unnormed / totals
    tot_ref[:, 0:LANES] = totals
    ctx_ref[:, 0:LANES] = ctx
    ctx = pltpu.roll(u2, HEAD_DIM, 1) / u2
    tot_ref[:, LANES:] = u2
    ctx_ref[:, LANES:] = ctx
    for d in range(ZS):
        spot = pl.ds(pl.multiple_of(lax.rem(order[count] + d, ZS) * rows, rows), rows)
        low_refs[d][...] = ctx_ref[spot, 0:3 * HEAD_DIM].astype(BF)


def attend(order, q, seg, kvs, after=()):
    total = q.shape[0]
    span = len(kvs) * total // ZS
    outs = [((total // ZS, 3 * HEAD_DIM), BF)] * ZS + [((2, total, 2 * LANES), F32)]
    scratch = [pltpu.VMEM((ZS * span, 3 * LANES), BF), pltpu.VMEM((span, total), F32), pltpu.VMEM((3, LANES, total), F32), pltpu.VMEM((LANES, LANES), F32)]
    return call(attend_kernel, (order, q, seg, *kvs), outs, "attend", 1, after, scratch, 20)


def attend_back_kernel(order, q_ref, gc0, gc1, gc2, gc3, both_ref, seg_ref, *rest):
    ctx_ref, tot_ref = both_ref.at[0], both_ref.at[1]
    count = len(rest) - 10
    kv_refs, (dq_ref, kept_ref, sent_ref, done_ref), (keys, bias, ge, acc, gctx_ref, turned) = rest[:count], rest[count:count + 4], rest[count + 4:]
    done_ref[...] = jnp.zeros_like(done_ref)
    total = q_ref.shape[0]
    rows = total // ZS
    for d, ref in enumerate((gc0, gc1, gc2, gc3)):
        spot = pl.ds(pl.multiple_of(lax.rem(order[count] + ZS - d, ZS) * rows, rows), rows)
        gctx_ref[spot, :] = ref[...].astype(F32)
    span = count * rows
    fill_keys(kv_refs, keys, rows)
    queries = turn_segments(order, seg_ref, turned, count)
    lane = lax.broadcasted_iota(jnp.int32, (total, LANES), 1)
    lower_q = lane < HEAD_DIM
    lower_k = lax.broadcasted_iota(jnp.int32, (span, LANES), 1) < HEAD_DIM
    q01, q2 = q_ref[:, 0:LANES], q_ref[:, LANES:2 * LANES]
    none = jnp.zeros_like(q01)
    qs = (jnp.where(lower_q, q01, none), jnp.where(lower_q, none, q01), q2)
    gs = []
    g01 = gctx_ref[:, 0:LANES]
    g2 = jnp.concatenate([jnp.zeros((total, HEAD_DIM), F32), gctx_ref[:, LANES:]], 1)
    c2 = pltpu.roll(ctx_ref[:, LANES:], HEAD_DIM, 1)
    t2 = tot_ref[:, LANES:]
    t2 = jnp.where(lower_q, 1.0, pltpu.roll(t2, HEAD_DIM, 1))
    for h in range(3):
        grad = g2 if h == 2 else g01
        tot = t2 if h == 2 else tot_ref[:, 0:LANES]
        ctx = c2 if h == 2 else ctx_ref[:, 0:LANES]
        mine = lower_q if h == 0 else jnp.logical_not(lower_q)
        gu = jnp.where(mine, grad / tot, 0.0).astype(BF)
        gtot = -jnp.sum(jnp.where(mine, grad * ctx / tot, 0.0), -1, keepdims=True)
        high = gtot.astype(BF)
        low = (gtot - high.astype(F32)).astype(BF)
        first = HEAD_DIM if h == 0 else 0
        ge[h] = jnp.where(lane == first, high, jnp.where(lane == first + 1, low, gu))
        gs.append(gu)
    for z in range(ZS):
        fill_bias(order, queries, turned, bias, z, count, rows)
        ks, vs = head_parts(q_ref, keys, z, span, lower_q, lower_k)
        dk, dv = [], []
        for h in range(3):
            qz = qs[h][z * rows:, :]
            expo = jnp.exp(dot_nt(ks[h], qz) + bias[:, z * rows:])
            gprob = dot_nt(vs[h], ge[h, z * rows:, :])
            gscore = (expo * gprob).astype(BF)
            dv.append(dot(expo.astype(BF), gs[h][z * rows:, :]))
            dk.append(dot(gscore, qz))
            part = dot_tn(ks[h], gscore)
            if z == 0:
                acc[h] = part
            else:
                acc[h, :, z * rows:] += part
        parts = (dk[0] + dk[1], dk[2] + dv[2], dv[0] + dv[1])
        for j in range(count):
            to = kept_ref if j < count // 2 else sent_ref
            for i in range(3):
                to[j % (count // 2), z * rows:(z + 1) * rows, i * LANES:(i + 1) * LANES] = parts[i][j * rows:(j + 1) * rows, :].astype(to.dtype)
    upper = lax.broadcasted_iota(jnp.int32, (LANES, total), 0) >= HEAD_DIM
    dq_ref[:, 0:LANES] = (0.125 * jnp.where(upper, acc[1], acc[0])).T.astype(BF)
    dq_ref[:, LANES:] = (0.125 * acc[2]).T[:, 0:HEAD_DIM].astype(BF)


def attend_back(order, q, gctx, both, seg, kvs, after=()):
    total = q.shape[0]
    count = len(kvs)
    span = count * total // ZS
    outs = [((total, 3 * HEAD_DIM), BF), ((count // 2, total, 6 * HEAD_DIM), F32), ((count // 2, total, 6 * HEAD_DIM), BF), ((8, LANES), F32)]
    scratch = [
        pltpu.VMEM((ZS * span, 3 * LANES), BF),
        pltpu.VMEM((span, total), F32),
        pltpu.VMEM((3, total, LANES), BF),
        pltpu.VMEM((3, LANES, total), F32),
        pltpu.VMEM((total, 3 * HEAD_DIM), F32),
        pltpu.VMEM((LANES, LANES), F32),
    ]
    return call(attend_back_kernel, (order, q, *gctx, both, seg, *kvs), outs, "attend_back", 1, after, scratch, 24)


def norm_parts(values):
    mean = jnp.mean(values, -1, keepdims=True)
    centered = values - mean
    rstd = lax.rsqrt(jnp.mean(centered * centered, -1, keepdims=True) + 1e-05)
    return centered * rstd, rstd


def norm_back(normed, rstd, grad, gain):
    q = grad * gain
    return rstd * (q - jnp.mean(q, -1, keepdims=True) - normed * jnp.mean(q * normed, -1, keepdims=True))


GC = 0.7978845608028654


class Part:
    def __init__(self, value, first, last):
        self.value, self.first, self.last = value, first, last


def call(body, args, outs, name, smem=0, after=(), scratch=(), mib=12):
    values = [arg.value if isinstance(arg, Part) else arg for arg in args]
    count, waits = len(values), len(after)

    def whole(*refs):
        ins = [ref.at[:, arg.first:arg.last] if isinstance(arg, Part) else ref for arg, ref in zip(args, refs)]
        body(*ins, *refs[count + waits:])

    specs = [pl.BlockSpec(memory_space=pltpu.SMEM if i < smem else pltpu.VMEM) for i in range(count)]
    return pl.pallas_call(
        whole,
        in_specs=specs + [pl.BlockSpec(memory_space=pl.ANY)] * waits,
        out_shape=[jax.ShapeDtypeStruct(*out) for out in outs],
        scratch_shapes=list(scratch),
        compiler_params=params(mib),
        cost_estimate=SMALL,
        name=name,
    )(*values, *after)


def fold_both(kept, came, ix, iy, width):
    sy, sz, sx, wr, wide = kept.shape

    def body(at_ref, kept_ref, came_ref, *outs):
        for d in range(sx):
            x = lax.rem(at_ref[0] + d, sx)
            outs[d][...] = (kept_ref[:, :, pl.ds(x, 1), :, 0:width].astype(F32) + came_ref[:, :, pl.ds(x, 1), :, 0:width].astype(F32)).astype(BF)
        for d in range(sy):
            y = lax.rem(at_ref[1] + d, sy)
            outs[sx + d][...] = (kept_ref[pl.ds(y, 1), :, :, :, width:].astype(F32) + came_ref[pl.ds(y, 1), :, :, :, width:].astype(F32)).astype(BF)

    outs = [((sy, sz, 1, wr, width), BF)] * sx + [((1, sz, sx, wr, wide - width), BF)] * sy
    return call(body, (jnp.stack([ix, iy]).astype(jnp.int32), kept, came), outs, "fold_both", 1)


def fold_cross(first, first_came, second, second_came, ix, iy):
    sx, sy = len(first), len(second)
    sz, wr, width = first[0].shape[1], first[0].shape[3], first[0].shape[4]
    other = second[0].shape[4]

    def body(at_ref, *refs):
        one, two, outs = refs[:sx], refs[sx:sx + sy], refs[sx + sy:]
        for d in range(sy):
            y = lax.rem(at_ref[1] + d, sy)
            total = one[0][pl.ds(y, 1)].astype(F32)
            for ref in one[1:]:
                total = total + ref[pl.ds(y, 1)].astype(F32)
            outs[d][...] = total.astype(BF)
        for d in range(sx):
            x = lax.rem(at_ref[0] + d, sx)
            total = two[0][:, :, pl.ds(x, 1)].astype(F32)
            for ref in two[1:]:
                total = total + ref[:, :, pl.ds(x, 1)].astype(F32)
            outs[sy + d][...] = total.astype(BF)

    outs = [((1, sz, 1, wr, width), BF)] * sy + [((1, sz, 1, wr, other), BF)] * sx
    args = (jnp.stack([ix, iy]).astype(jnp.int32), first[0], *first_came, second[0], *second_came)
    return call(body, args, outs, "fold_cross", 1)


def fold_last(first, first_came, second, second_came, iz, after):
    sy, sx = len(first), len(second)
    wr, width = first[0].shape[3:]
    wide = width + second[0].shape[4]

    def body(at_ref, *refs):
        one, two, outs = refs[:sy], refs[sy:sy + sx], refs[sy + sx:]
        for d in range(ZS):
            z = lax.rem(at_ref[0] + d, ZS)
            for sums, cols in ((one, slice(0, width)), (two, slice(width, wide))):
                total = sums[0][:, pl.ds(z, 1)].astype(F32)
                for ref in sums[1:]:
                    total = total + ref[:, pl.ds(z, 1)].astype(F32)
                outs[d][:, :, :, :, cols] = total.astype(BF)

    outs = [((1, 1, 1, wr, wide), BF)] * ZS
    args = (iz.astype(jnp.int32).reshape(1), first[0], *first_came, second[0], *second_came)
    return call(body, args, outs, "fold_last", 1, after)


def passed(pieces, axis):
    return [shift(pieces[d], axis, d) for d in range(1, len(pieces))]


def beside(pieces):
    rows, group = pieces[0].shape

    def body(*refs):
        for d, ref in enumerate(refs[:-1]):
            refs[-1][:, d * group:(d + 1) * group] = ref[...]

    return call(body, tuple(pieces), [((rows, len(pieces) * group), BF)], "beside")[0]


def out_project(place, cat, halves, hidden, vectors):
    rows, width = hidden.shape
    group = width // ZS
    half = width // 2

    def body(place_ref, cat_ref, own_ref, other_ref, hidden_ref, vec_ref, res_ref, n2_ref):
        own = jnp.zeros((rows, half), F32)
        other = jnp.zeros((rows, half), F32)
        for d in range(ZS):
            piece = cat_ref[:, d * group:(d + 1) * group]
            spot = pl.ds(pl.multiple_of(lax.rem(place_ref[0] + ZS - d, ZS) * group, group), group)
            own = own + dot(piece, own_ref[spot, :])
            other = other + dot(piece, other_ref[spot, :])
        first = place_ref[1] == 0
        branch = jnp.concatenate([jnp.where(first, own, other), jnp.where(first, other, own)], 1)
        total = hidden_ref[...].astype(F32) + branch + vec_ref[2:3, :]
        res_ref[:, 0:width] = total
        res_ref[:, width:] = jnp.broadcast_to(vec_ref[15:16, 0:rows], (LANES, rows)).T
        n2, _ = norm_parts(total)
        n2_ref[...] = (n2 * vec_ref[6:7, :] + vec_ref[7:8, :]).astype(BF)

    outs = [((rows, width + LANES), F32), ((rows, width), BF)]
    return call(body, (place, cat, *halves, hidden, vectors), outs, "out_project", 1)


def mlp_parts(weights, ff):
    width = weights[0].shape[0]
    if len(weights) == 2:
        return Part(weights[0], 0, ff), weights[1]
    return Part(weights[0], 0, ff), Part(weights[0], ff + width // 2, ff + width // 2 + width)


def mlp_up(blocks, weights, bias, ff):
    rows, width = blocks[0].shape
    count = len(blocks)
    half = count // 2

    def body(*refs):
        n2_refs, (bias_ref, up_ref, down_ref), (kept_ref, sent_ref, slope_ref, saved_ref) = refs[:count], refs[count:count + 3], refs[-4:]
        for j in range(count):
            saved_ref[j * rows:(j + 1) * rows, ff:] = n2_refs[j][...]
            pre = dot(n2_refs[j][...], up_ref[...]) + bias_ref[0:1, 0:ff]
            square = pre * pre
            tanh = jnp.tanh(GC * pre * (1.0 + 0.044715 * square))
            half_one = 0.5 * (1.0 + tanh)
            act = (pre * half_one).astype(BF)
            slope_ref[j] = (half_one + 0.5 * pre * (1.0 - tanh * tanh) * (GC + GC * 0.134145 * square)).astype(BF)
            saved_ref[j * rows:(j + 1) * rows, 0:ff] = act
            part = dot(act, down_ref[...])
            if j < half:
                kept_ref[j] = part + bias_ref[1:2, 0:width] if j == 0 else part
            else:
                sent_ref[j - half] = part.astype(BF)

    outs = [((half, rows, width), F32), ((half, rows, width), BF), ((count, rows, ff), BF), ((count * rows, ff + width), BF)]
    return call(body, (*blocks, bias, *mlp_parts(weights, ff)), outs, "mlp_up")


def finish(terms, residual, targets, scale):
    rows, width = targets.shape[1:]
    size = len(terms)

    def body(scale_ref, *refs):
        res_ref, target_ref, out_ref, err_ref, both_ref, gmlp_ref = refs[size:]
        valid = res_ref[:, width:width + 1]
        final = res_ref[:, 0:width]
        for ref in refs[:size]:
            final = final + ref[...].astype(F32)
        out_ref[...] = final.astype(BF)
        deviation = final - target_ref[0].astype(F32)
        grad = valid * (target_ref[1].astype(F32) + deviation * scale_ref[0])
        both_ref[0] = res_ref[:, 0:width]
        both_ref[1] = grad
        low = grad.astype(BF)
        gmlp_ref[...] = low
        err_ref[0:1, :] = jnp.sum(valid * deviation * deviation, 0, keepdims=True)
        err_ref[1:2, :] = jnp.sum(low.astype(F32), 0, keepdims=True)

    outs = [((rows, width), BF), ((2, width), F32), ((2, rows, width), F32), ((rows, width), BF)]
    return call(body, (scale, *terms, residual, targets), outs, "finish", 1)


def mlp_back(grads, weights, slope):
    rows, width = grads[0].shape
    count = len(grads)
    half = count // 2
    ff = slope.shape[2]

    def body(*refs):
        g_refs, (slope_ref, up_ref, down_ref), (kept_ref, sent_ref, gpre_ref, g_all) = refs[:count], refs[count:count + 3], refs[-4:]
        for j in range(count):
            g_all[j * rows:(j + 1) * rows, :] = g_refs[j][...]
            gpre = (dot_nt(g_refs[j][...], down_ref[...]) * slope_ref[j].astype(F32)).astype(BF)
            gpre_ref[j * rows:(j + 1) * rows, :] = gpre
            part = dot_nt(gpre, up_ref[...])
            if j < half:
                kept_ref[j] = part
            else:
                sent_ref[j - half] = part.astype(BF)

    outs = [((half, rows, width), F32), ((half, rows, width), BF), ((count * rows, ff), BF), ((count * rows, width), BF)]
    return call(body, (*grads, slope, *mlp_parts(weights, ff)), outs, "mlp_back")


def mlp_weights(place, grads, saved, gpre, size, after):
    width = grads.shape[1]
    ff = gpre.shape[1]
    joined = ff == width
    down, up = ff // size, width // size
    direct = down % LANES == 0 and up % LANES == 0

    def body(place_ref, g_ref, saved_ref, gpre_ref, *refs):
        outs, sums_ref, rest = refs[:size if joined else 2 * size], refs[size if joined else 2 * size], refs[size + 1 if joined else 2 * size + 1:]
        if not direct:
            rest[0][...] = dot_tn(saved_ref[:, 0:ff], g_ref[...])
            rest[1][...] = dot_tn(saved_ref[:, ff:], gpre_ref[...])
        for d in range(size):
            y = lax.rem(place_ref[0] + d, size)
            if direct:
                first = dot_tn(saved_ref[:, pl.ds(pl.multiple_of(y * down, LANES), down)], g_ref[...])
                second = dot_tn(saved_ref[:, pl.ds(pl.multiple_of(ff + y * up, LANES), up)], gpre_ref[...])
            else:
                first = rest[0][pl.ds(pl.multiple_of(y * down, 16), down), :]
                second = rest[1][pl.ds(pl.multiple_of(y * up, 16), up), :]
            if joined:
                outs[d][:, 0:width] = first.astype(BF)
                outs[d][:, width:] = second.astype(BF)
            else:
                outs[d][...] = first.astype(BF)
                outs[size + d][...] = second.astype(BF)
        sums_ref[...] = jnp.sum(gpre_ref[...].astype(F32), 0, keepdims=True)

    outs = [((up, 2 * width), BF)] * size if joined else [((down, width), BF)] * size + [((up, ff), BF)] * size
    scratch = [] if direct else [pltpu.VMEM((ff, width), F32), pltpu.VMEM((width, ff), F32)]
    *pieces, sums = call(body, (place, grads, saved, gpre), outs + [((1, ff), F32)], "mlp_weights", 1, after, scratch, 20)
    return [pieces[i:i + size] for i in range(0, len(pieces), size)], sums


def fold_first(own, came, after):
    def body(own_ref, *refs):
        total = own_ref[...].astype(F32)
        for ref in refs[:-1]:
            total = total + ref[...].astype(F32)
        refs[-1][...] = total.astype(BF)

    return call(body, (own, *came), [(own.shape, BF)], "fold_first", 0, after)[0]


def out_back(place, terms, res_and_grad, vectors, ctx_cat, halves, after):
    rows, width = res_and_grad.shape[1:]
    group = width // ZS
    size = len(terms)

    def body(place_ref, *refs):
        (both_ref, vec_ref, cat_ref, own_ref, other_ref, gres_ref), gctx_refs, (gw_ref, sums_ref) = refs[size:size + 6], refs[size + 6:size + 10], refs[size + 10:]
        gn2 = refs[0][...]
        for ref in refs[1:size]:
            gn2 = gn2 + ref[...].astype(F32)
        n2, rstd = norm_parts(both_ref[0])
        gres = both_ref[1] + norm_back(n2, rstd, gn2, vec_ref[6:7, :])
        gres_ref[...] = gres
        branch = gres.astype(BF)
        left, right = branch[:, 0:width // 2], branch[:, width // 2:]
        first = place_ref[1] == 0
        own, other = jnp.where(first, left, right), jnp.where(first, right, left)
        for d in range(ZS):
            spot = pl.ds(pl.multiple_of(lax.rem(place_ref[0] + d, ZS) * group, group), group)
            gctx_refs[d][...] = (dot_nt(own, own_ref[spot, :]) + dot_nt(other, other_ref[spot, :])).astype(BF)
        for d in range(ZS):
            spot = pl.ds(pl.multiple_of(lax.rem(place_ref[0] + ZS - d, ZS) * group, group), group)
            gw_ref[spot, :] = dot_tn(cat_ref[:, d * group:(d + 1) * group], branch).astype(BF)
        rowsum = lambda v: jnp.sum(v, 0, keepdims=True)
        sums_ref[0:1, :] = rowsum(branch.astype(F32))
        sums_ref[1:2, :] = rowsum(gn2 * n2)
        sums_ref[2:3, :] = rowsum(gn2)

    outs = [((rows, width), F32)] + [((rows, group), BF)] * ZS + [((width, width), BF), ((3, width), F32)]
    args = (place, *terms, res_and_grad, vectors, ctx_cat, *halves)
    return call(body, args, outs, "out_back", 1, after)


def join_back(place, terms, dq, one):
    total, group = dq.shape
    width = one.shape[0]
    rows = total // ZS
    size = len(terms)
    cols = 3 * group

    def body(place_ref, *refs):
        dq_ref, w_ref, gj_ref, gn1_ref = refs[size:size + 4]
        out_refs = refs[size + 4:]
        dkv = refs[0][...].astype(F32)
        for ref in refs[1:size]:
            dkv = dkv + ref[...].astype(F32)
        gj_ref[:, 0:2 * group] = dkv.astype(BF)
        gj_ref[:, 2 * group:] = dq_ref[...]
        gn1_ref[...] = dot_nt(gj_ref[...], w_ref[:, 0:cols])
        for d in range(ZS):
            spot = pl.ds(pl.multiple_of(lax.rem(place_ref[0] + d, ZS) * rows, rows), rows)
            out_refs[d][...] = gn1_ref[spot, :].astype(out_refs[d].dtype)

    outs = [((total, cols), BF), ((total, width), F32), ((rows, width), F32)] + [((rows, width), BF)] * (ZS - 1)
    return call(body, (place, *terms, dq, one), outs, "join_back", 1)


def weights_back(place, saved, grad_joined, gn1, out_sums, fin_sums, up_rows, gw_out, wr, devices):
    total, cols = grad_joined.shape
    width = gn1.shape[1]
    rows = total // ZS
    group = cols // 3
    upc = up_rows.shape[0]
    chips = width // (2 * wr)
    wide = width + cols + HEAD_DIM + LANES
    slots = -(-devices // wr)

    def body(place_ref, saved_ref, gj_ref, gn1_ref, sums_ref, fin_ref, up_ref, gw_ref, kept_ref, sent_ref, vec, full):
        gain_sum = jnp.zeros((1, width), F32)
        for z in range(ZS):
            spot = slice(z * rows, (z + 1) * rows)
            normed, _ = norm_parts(saved_ref[spot, width:].astype(F32))
            gain_sum = gain_sum + jnp.sum(gn1_ref[spot, :] * normed, 0, keepdims=True)
        joined_sums = jnp.sum(gj_ref[...].astype(F32), 0, keepdims=True)
        vec[...] = jnp.zeros_like(vec)
        hd = HEAD_DIM
        for g in range(ZS):
            here = place_ref[0] == g
            at = g * group
            vec[0:1, at:at + group] = jnp.where(here, joined_sums[:, 2 * group:], 0.0)
            vec[1:2, at:at + 2 * hd] = jnp.where(here, joined_sums[:, 4 * hd:6 * hd], 0.0)
            vec[1:2, at + 2 * hd:at + 3 * hd] = jnp.where(here, joined_sums[:, 3 * hd:4 * hd], 0.0)
        vec[2:3, :] = sums_ref[0:1, :]
        vec[3:4, :] = fin_ref[1:2, :]
        vec[4:5, :] = gain_sum
        vec[5:6, :] = jnp.sum(gn1_ref[...], 0, keepdims=True)
        vec[6:8, :] = sums_ref[1:3, :]
        vec[8:8 + upc, :] = up_ref[...]
        error = jnp.sum(fin_ref[0:1, :], -1, keepdims=True)
        high = error.astype(BF).astype(F32)
        turn = lax.rem(lax.broadcasted_iota(jnp.int32, (1, width), 1), wr)
        for s in range(slots):
            vec[16 + s:17 + s, :] = jnp.where(turn + s * wr == place_ref[2], high, 0.0)
        vec[16 + slots:17 + slots, :] = jnp.where(turn == 0, error - high, 0.0)
        full[:, 0:width] = gw_ref[...].astype(F32)
        full[:, width:width + cols] = dot_tn(saved_ref[:, 0:width], gj_ref[...])
        full[:, width + cols:width + cols + hd] = jnp.zeros((width, hd), F32)
        full[:, width + cols + hd:] = vec[...].T
        for c in range(2):
            @pl.when(place_ref[1] == c)
            def _():
                for chip in range(chips):
                    at = chip * 2 * wr
                    kept_ref[chip] = full[at + c * wr:at + (c + 1) * wr, :].astype(BF)
                    sent_ref[chip] = full[at + (1 - c) * wr:at + (2 - c) * wr, :].astype(BF)

    outs = [((chips, wr, wide), BF)] * 2
    scratch = [pltpu.VMEM((LANES, width), F32), pltpu.VMEM((width, wide), F32)]
    return call(body, (place, saved, grad_joined, gn1, out_sums, fin_sums, up_rows, gw_out), outs, "weights_back", 1, scratch=scratch, mib=20)


def input_back(terms, hidden, vectors, grad_res):
    rows, width = hidden.shape

    def body(t0, t1, t2, t3, hidden_ref, gain_ref, gres_ref, out_ref):
        back = t0[...] + t1[...].astype(F32) + t2[...].astype(F32) + t3[...].astype(F32)
        normed, rstd = norm_parts(hidden_ref[...].astype(F32))
        out_ref[...] = gres_ref[...] + norm_back(normed, rstd, back, gain_ref[4:5, :])

    return call(body, (terms[0], *terms[1:], hidden, vectors, grad_res), [((rows, width), F32)], "input_back")[0]


def unpack_one(place, pieces, after):
    rows, wide = pieces[0].shape[-2:]
    hd = HEAD_DIM
    group = 3 * hd
    width = ZS * group

    def body(place_ref, p0, p1, p2, p3, qkv_ref, vec_ref, out_ref, held_ref):
        for d, piece in enumerate((p0, p1, p2, p3)):
            held_ref[pl.ds(lax.rem(place_ref[0] + ZS - d, ZS), 1)] = piece[...].reshape(1, rows, wide).astype(F32)
        vec_total = jnp.zeros((rows, LANES), F32)
        out_total = jnp.zeros((rows, width), F32)
        for g in range(ZS):
            k = width + g * group
            v = 2 * width + g * group
            at = width
            qkv_ref[:, k:k + 3 * hd] = held_ref[g, :, at:at + 3 * hd]
            qkv_ref[:, v + 2 * hd:v + 3 * hd] = held_ref[g, :, at + 3 * hd:at + 4 * hd]
            qkv_ref[:, v:v + 2 * hd] = held_ref[g, :, at + 4 * hd:at + 6 * hd]
            qkv_ref[:, g * group:g * group + 3 * hd] = held_ref[g, :, at + 6 * hd:at + 9 * hd]
            vec_total = vec_total + held_ref[g, :, at + 10 * hd:]
            out_total = out_total + held_ref[g, :, 0:width]
        vec_ref[...] = vec_total
        out_ref[...] = out_total

    outs = [((rows, 3 * width), F32), ((rows, LANES), F32), ((rows, width), F32)]
    return call(body, (place, *pieces), outs, "unpack_one", 1, after, scratch=[pltpu.VMEM((ZS, rows, wide), F32)])


def per_device(hidden_in, w_qkv, q_bias, v_bias, w_out, out_bias, w_up, up_bias, w_down, down_bias, ln1_gain, ln1_bias, ln2_gain, ln2_bias, segment_ids, padding_mask, teacher, cotangent):
    sy, sz, sx = (lax.axis_size(a) for a in ("y", "z", "x"))
    iy, iz, ix, core = (lax.axis_index(a) for a in ("y", "z", "x", "core"))
    device = ((iy * sz + iz) * sx + ix) * 2 + core
    devices = sy * sz * sx * 2
    rows, width = hidden_in.shape[1:]
    wr = w_qkv.shape[0]
    ffd = w_down.shape[0]
    ff = sy * sz * ffd
    upc = ffd // wr
    wcols = 9 * HEAD_DIM
    group = width // sz
    place = iz.astype(jnp.int32).reshape(1)
    at_zc = jnp.stack([iz, core]).astype(jnp.int32)
    yplace = iy.astype(jnp.int32).reshape(1)

    def from_z(value):
        return [value] + [shift(value, "z", d) for d in range(1, sz)]

    def to_z(pieces):
        return [pieces[0]] + [shift(pieces[d], "z", d) for d in range(1, sz)]

    def cut_z(value):
        return [lax.dynamic_slice_in_dim(value, lax.rem(iz + d, sz), 1, 0) for d in range(sz)]

    def to_group(pieces):
        sent = [pieces[0]]
        for d in range(1, 2 * sx):
            dc, dx = d // sx, d % sx
            pairs = [(x * 2 + c, (x + dx) % sx * 2 + (c + dc) % 2) for x in range(sx) for c in range(2)]
            sent.append(lax.ppermute(pieces[d], ("x", "core"), pairs))
        return sent

    flat = jnp.concatenate([jnp.stack([q_bias, v_bias, out_bias, down_bias, ln1_gain, ln1_bias, ln2_gain, ln2_bias]), up_bias.reshape(upc, wr)])
    hidden = hidden_in[0]
    pieces = from_z(hidden)
    targets = jnp.concatenate([teacher, cotangent], 0)
    one = arrange(to_z(cut_z(pack_one(w_qkv, flat, jnp.concatenate([segment_ids, padding_mask])))), iz, 0)
    one = gather(one[None, :, None], "x", 2, after=[pieces[1]])
    one = gather(one, "y", 0, after=pieces[2:])[:, :, :, None]
    one = gather(one, "core", 3).reshape(width, -1)

    at_xc = jnp.stack([ix, core]).astype(jnp.int32)
    ups = list(pack_up(at_xc, w_up, w_out, ffd, sx))
    ups = to_group(ups)
    weights = [join_up(at_xc, ups, w_down)]
    if ffd != 2 * sx * wr:
        weights = weights + [w_down]
    weights = [lax.all_gather(member, ("y", "z"), axis=0, tiled=True) for member in weights]

    vec = one[:, wcols:]
    vectors = jnp.concatenate([vec[:, :15].T.astype(F32), jnp.pad(padding_mask.astype(F32), ((0, 0), (0, width - rows)))])
    ub = vectors[8:8 + upc].reshape(upc, sy * sz, sx * 2, wr)
    ub = lax.dynamic_index_in_dim(ub, ix * 2 + core, 2, keepdims=False).transpose(1, 0, 2).reshape(1, ff)
    wide = max(ff, width)
    biases = jnp.concatenate([jnp.pad(ub, ((0, 0), (0, wide - ff))), jnp.pad(vectors[3:4], ((0, 0), (0, wide - width)))])
    count = jnp.sum(vectors[8 + upc]) / wr
    seg = lax.dynamic_index_in_dim(vec.reshape(sy, sz * sx * 2, wr, LANES), iy, 0, keepdims=False)[:, :2, HEAD_DIM:].astype(F32).reshape(sz * sx * 2, rows)
    spots = [(lax.rem(ix + sx - d, sx), core) for d in range(sx)]
    spots = spots + [(at, 1 - core) for at, _ in spots]
    order = jnp.stack([at * 2 + c for at, c in spots] + [iz]).astype(jnp.int32)

    kv, q, saved_one = project(place, pieces, one, vectors)
    kvs = spread_tokens(kv)
    *ctx_parts, ctx_tot = attend(order, q, seg, kvs, after=[biases])
    ctx_cat = beside(to_z(ctx_parts))
    wo = [held(Part(weights[0], ff, ff + width // 2), [ctx_cat])]
    wo = wo + [shift(wo[0], "core", 1)]
    residual, n2_low = out_project(at_zc, ctx_cat, wo, hidden, vectors)
    kept, sent, slope, saved = mlp_up(spread_tokens(n2_low), weights, biases, ff)
    layer_out, fin_sums, res_and_grad, grad_mlp = finish(fold_tokens(kept, sent), residual, targets, (2.0 / (count * width)).reshape(1))

    kept, sent, grad_pre, grads = mlp_back(spread_tokens(grad_mlp), weights, slope)
    gn2_terms = fold_tokens(kept, sent)
    gw_mlp, up_sums = mlp_weights(yplace, grads, saved, grad_pre, sy, after=gn2_terms[:1])
    gw_came = [passed(members, "y") for members in gw_mlp]
    grad_res, *gctx, gw_out, out_sums = out_back(at_zc, gn2_terms, res_and_grad, vectors, ctx_cat, wo, after=[up_sums])
    dq, dkv_kept, dkv_sent, done = attend_back(order, q, to_z(gctx), ctx_tot, seg, kvs)
    gw_sums = [lax.psum_scatter(fold_first(members[0], came, [done]), "z", scatter_dimension=0, tiled=True) for members, came in zip(gw_mlp, gw_came)]
    grad_joined, gn1, *gn1_parts = join_back(place, fold_tokens(dkv_kept, dkv_sent, BF), dq, one)
    gn1_parts = to_z(gn1_parts)
    input_grad = input_back(gn1_parts, hidden, vectors, grad_res)

    up_rows = jnp.zeros((upc, sy * sz, sx * 2, wr), F32)
    up_rows = lax.dynamic_update_slice_in_dim(up_rows, up_sums.reshape(sy * sz, upc, wr).transpose(1, 0, 2)[:, :, None], ix * 2 + core, 2).reshape(upc, width)
    places = jnp.stack([iz, core, device]).astype(jnp.int32)
    kept, sent = weights_back(places, saved_one, grad_joined, gn1, out_sums, fin_sums, up_rows, gw_out, wr, devices)
    third = fold_both(kept.reshape(sy, sz, sx, wr, -1), shift(sent, "core", 1).reshape(sy, sz, sx, wr, -1), ix, iy, width)
    third = fold_cross(third[:sx], passed(third[:sx], "x"), third[sx:], passed(third[sx:], "y"), ix, iy)
    third = fold_last(third[:sy], passed(third[:sy], "y"), third[sy:], passed(third[sy:], "x"), iz, after=[gn1_parts[2], gn1_parts[3]])
    third = [third[0]] + passed(third, "z")
    ready = third[1:2]

    gw_down, ups = open_sums(at_xc, gw_sums, width, sx, wr, ready)
    ups = to_group(ups)
    gw_up = close_up(at_xc, ups, ffd)

    grad_w_qkv, sums, gw_out = unpack_one(place, third, after=ups[-1:])
    sums = sums.T
    loss = jnp.sum(sums[16:17 + -(-devices // wr)]) / (count * width)
    return (
        layer_out[None], loss, input_grad[None], grad_w_qkv, sums[0], sums[1], gw_out, sums[2],
        gw_up, sums[8:8 + upc].reshape(-1), gw_down, sums[3], sums[4], sums[5], sums[6], sums[7],
    )


def solution(mesh):
    seq, ctx = mesh.shape["seq"], mesh.shape["ctx"]
    grid = Mesh(mesh.devices.reshape(seq, ZS, ctx // (2 * ZS), 2), ("y", "z", "x", "core"))
    every = ("y", "z", "x", "core")
    matrix, vector = P(every, None), P(every)
    tokens = P("y", ("z", "x", "core"), None)
    marks = P("y", ("z", "x", "core"))
    return jax.shard_map(
        per_device,
        mesh=grid,
        in_specs=(tokens, matrix, vector, vector, matrix, vector, matrix, vector, matrix, vector, vector, vector, vector, vector, marks, marks, tokens, tokens),
        out_specs=(tokens, P(), tokens, matrix, vector, vector, matrix, vector, matrix, vector, matrix, vector, vector, vector, vector, vector),
        check_vma=False,
    )
```
